128 devices in a mesh: section: 2 (over x_lo), dp: 64 (over y, z, x_hi, core).
Axes of the slice: x: 4 (x_hi: 2, x_lo: 2; x = x_hi * 2 + x_lo), y: 4, z: 4, core: 2. Of those that a mesh axis runs over, the one named last changes fastest.
Arguments:
- tokens: bfloat16 [2, 16384, 768], P(None, 'dp'), may hold values from -16 to 16
- cotangent: bfloat16 [2, 16384, 768], P(None, 'dp'), may hold values from -6 to 6
- short_lens: int32 [128], P('dp'), may hold values from 64 to 128, as said below
- long_lens: int32 [64], P('dp'), may hold values from 128 to 256, as said below
- w_qkv: bfloat16 [2, 768, 2304], P('section'), may hold values from -0.21875 to 0.21875
- w_out: bfloat16 [2, 768, 768], P('section'), may hold values from -0.625 to 0.625
- w_gate_up: bfloat16 [2, 768, 6144], P('section'), may hold values from -0.21875 to 0.21875
- w_down: bfloat16 [2, 3072, 768], P('section'), may hold values from -0.15625 to 0.15625
- gains: float32 [2, 2, 768], P('section'), may hold values from 0.5 to 1.5
- biases: float32 [2, 6, 768], P('section'), may hold values from -3 to 3
Outputs:
- boundary: float32 [2, 2, 16384, 768], P('section', None, 'dp')
- grad_qkv: float32 [2, 768, 2304], P('section', 'dp')
- grad_out: float32 [2, 768, 768], P('section', 'dp')
- grad_gate_up: float32 [2, 768, 6144], P('section', 'dp')
- grad_down: float32 [2, 3072, 768], P('section', 'dp')
- grad_gains: float32 [2, 2, 768], P('section', None, 'dp')
- grad_biases: float32 [2, 6, 768], P('section', None, 'dp')
The draws below stay inside these ranges and needn't reach their ends.
Inputs may be any that keep to these rules, and one draw needn't show every extreme that they name: `short_lens`: on every second dp index the first short sequence is full. `long_lens`: on every second dp index the first long sequence is full.
All inputs are finite; a program needn't handle non-finite values.
Results may differ from the reference program's by a relative error of at most 0.018.
Values may be sent and summed in bfloat16 or wider, within the bound.
A program may use at most 512 MiB of HBM per device.

```python
import jax
import jax.numpy as jnp
from jax import lax

D = 768
HEADS = 12
HEAD = 64
FF = 3072
SHORT_LEN = 128
LONG_LEN = 256
SHORT_DEV = 2
LONG_DEV = 1
SHORTS = 128
LONGS = 64
ROWS = 16384


def draw_short_lens(key, part):
    key = jax.random.fold_in(key, 11)
    lengths = jax.random.randint(key, (SHORTS,), SHORT_LEN // 2, SHORT_LEN + 1)
    leading = jnp.arange(SHORTS) % (2 * SHORT_DEV) == 0
    return jnp.where(leading, SHORT_LEN, lengths).astype(jnp.int32)


def draw_long_lens(key, part):
    key = jax.random.fold_in(key, 23)
    lengths = jax.random.randint(key, (LONGS,), LONG_LEN // 2, LONG_LEN + 1)
    leading = jnp.arange(LONGS) % (2 * LONG_DEV) == 0
    return jnp.where(leading, LONG_LEN, lengths).astype(jnp.int32)


def spiked(drawn, own_key, source, target, shards_of, factor):
    owner, partner = [(jnp.arange(drawn.shape[dim]) // (drawn.shape[dim] // shards_of)).reshape([-1 if axis == dim else 1 for axis in range(drawn.ndim)]) for dim in (source, target)]
    chosen = jax.random.permutation(own_key, shards_of)[partner]
    strong = (owner == chosen) | (owner == (partner + shards_of // 2) % shards_of)
    return jnp.where(strong, factor * drawn, drawn)


def steps_of(own_key, shape, shards, smallest, top_value):
    loudness = 1.0
    for axis_at, parts in shards:
        steps = jax.random.uniform(jax.random.fold_in(jax.random.fold_in(own_key, 6), axis_at), (parts,), jnp.float32, smallest / len(shards), top_value / len(shards))
        loudness = loudness * jnp.repeat(jnp.exp(steps), shape[axis_at] // parts).reshape((-1,) + (1,) * (len(shape) - 1 - axis_at))
    return loudness


def bell_draw(rng, extent, scale, bound, split=(), held_as=jnp.bfloat16):
    array = jax.random.normal(rng, extent, jnp.float32) * scale
    if len(split) > 0:
        array = steps_of(rng, extent, split, -0.22, 0.18) * array
    return jnp.clip(array, min=-bound, max=bound).astype(held_as)


def heavy_noise(own_key, shape, scale, bound, shards, heavy, held_as=jnp.bfloat16):
    entries = scale * jax.random.normal(own_key, shape, jnp.float32)
    if shards:
        entries = entries * steps_of(own_key, shape, shards, -0.22, 0.18)
    return jnp.clip(spiked(entries, jax.random.fold_in(own_key, 3), *heavy), -bound, bound).astype(held_as)


def setup_inputs(seed: int = 0) -> dict:
    key_of = jax.random.split(jax.random.key(seed), 11)
    tokens = heavy_noise(key_of[0], (2, ROWS, D), 1.0, 16.0, ((1, 64),), (1, 2, 64, 4.0))
    cotangent = bell_draw(key_of[1], (2, ROWS, D), 1.0, 6.0, ((1, 64),))
    short_lens = draw_short_lens(jax.random.fold_in(key_of[10], 71), 0)
    long_lens = draw_long_lens(jax.random.fold_in(key_of[10], 71), 0)
    w_qkv = bell_draw(key_of[4], (2, D, 3 * D), D ** -0.5, 0.21875, ((0, 2),))
    w_out = bell_draw(key_of[5], (2, D, D), (D // 8) ** -0.5, 0.625, ((0, 2),))
    w_gate_up = bell_draw(key_of[6], (2, D, 2 * FF), D ** -0.5, 0.21875, ((0, 2),))
    w_down = bell_draw(key_of[7], (2, FF, D), (FF // 2) ** -0.5, 0.15625, ((0, 2),))
    gains = jnp.clip(1.0 + 0.1 * jax.random.normal(key_of[8], (2, 2, D), jnp.float32), 0.5, 1.5)
    biases = bell_draw(key_of[9], (2, 6, D), 0.5, 3.0, ((0, 2),), jnp.float32)
    return dict(tokens=tokens, cotangent=cotangent, short_lens=short_lens, long_lens=long_lens, w_qkv=w_qkv, w_out=w_out, w_gate_up=w_gate_up, w_down=w_down, gains=gains, biases=biases)


@jax.custom_vjp
def low(v):
    return lax.optimization_barrier(v.astype(jnp.bfloat16)).astype(jnp.float32)

@jax.custom_vjp
def low_back(v):
    return v

def low_keep(v):
    return (low(v), None)

def low_pass(kept, grad):
    return (grad,)

def back_keep(v):
    return (v, None)

def back_low(kept, grad):
    return (low(grad),)
low.defvjp(low_keep, low_pass)
low_back.defvjp(back_keep, back_low)
epsilon = 1e-05
masked_value = -1000000000.0
highest = lax.Precision.HIGHEST

def round_both(values_in):
    return low_back(low(values_in))

def layer_norm(values_in, gain_row, shift_row):
    average = lax.optimization_barrier(jnp.mean(values_in, -1, keepdims=True))
    centred = values_in - average
    spread = lax.optimization_barrier(jnp.mean(centred * centred, -1, keepdims=True))
    return centred * lax.rsqrt(spread + epsilon) * gain_row + shift_row

def tables(segment, lengths):
    positions = jnp.arange(LONG_LEN)
    distance = jnp.abs(positions[:, None] - positions[None, :]).astype(jnp.float32)
    same_seq = positions[:, None] // segment == positions[None, :] // segment
    key_len = jnp.repeat(lengths, segment).reshape(-1, LONG_LEN)
    key_live = (positions % segment)[None, :] < key_len
    allowed = same_seq[None] & key_live[:, None, :]
    slopes = jnp.exp2(-8.0 * (jnp.arange(HEADS).astype(jnp.float32) + 1.0) / HEADS)
    alibi_bias = -slopes[:, None, None] * distance[None]
    return (allowed, alibi_bias, key_live.reshape(-1))

def attend(query, keys, values, allowed, alibi_bias):
    groups = allowed.shape[0]
    block_shape = (groups, LONG_LEN, HEADS, HEAD)

    def attend_block(operands):
        query_block, keys_block, values_block, allowed_block = operands
        scores = jnp.einsum('qhd,khd->hqk', query_block, keys_block, precision=highest) * HEAD ** (-0.5) + alibi_bias
        scores = low_back(jnp.where(allowed_block[None], scores, masked_value))
        probs = jax.nn.softmax(scores, axis=-1)
        return jnp.einsum('hqk,khd->qhd', low(probs), values_block, precision=highest)
    mixed = lax.map(jax.checkpoint(attend_block), (query.reshape(block_shape), keys.reshape(block_shape), values.reshape(block_shape), allowed))
    return mixed.reshape(-1, HEADS * HEAD)

def encoder_layer(section_in, weight_qkv, weight_out, weight_gate_up, weight_down, gain_rows, bias_rows, allowed, alibi_bias):
    projected = jnp.dot(section_in, weight_qkv, precision=highest)
    query = round_both(projected[:, :D] + bias_rows[0])
    keys = round_both(projected[:, D:2 * D])
    values = round_both(projected[:, 2 * D:] + bias_rows[1])
    mixed = round_both(attend(query, keys, values, allowed, alibi_bias))
    attn_out = low_back(jnp.dot(mixed, weight_out, precision=highest) + bias_rows[2])
    normed = layer_norm(section_in + attn_out, gain_rows[0], bias_rows[3])
    gate_up = low_back(jnp.dot(low(normed), weight_gate_up, precision=highest))
    hidden = low(jax.nn.gelu(gate_up[:, :FF], approximate=False) * gate_up[:, FF:])
    ffn_out = low_back(jnp.dot(hidden, weight_down, precision=highest) + bias_rows[4])
    return layer_norm(normed + ffn_out, gain_rows[1], bias_rows[5])

def reference(tokens, cotangent, short_lens, long_lens, w_qkv, w_out, w_gate_up, w_down, gains, biases):
    layouts = (tables(SHORT_LEN, short_lens), tables(LONG_LEN, long_lens))

    def whole_model(token_rows, qkv_all, out_all, gate_up_all, down_all, gain_all, bias_all):
        results = []
        for micro in range(2):
            allowed, alibi_bias, unused = layouts[micro]
            hidden_rows = token_rows[micro]
            for section_id in range(2):
                if section_id == 1:
                    hidden_rows = low_back(low(hidden_rows))
                hidden_rows = encoder_layer(hidden_rows, qkv_all[section_id], out_all[section_id], gate_up_all[section_id], down_all[section_id], gain_all[section_id], bias_all[section_id], allowed, alibi_bias)
            results.append(hidden_rows)
        return jnp.stack(results)
    primals = (tokens.astype(jnp.float32), w_qkv.astype(jnp.float32), w_out.astype(jnp.float32), w_gate_up.astype(jnp.float32), w_down.astype(jnp.float32), gains.astype(jnp.float32), biases.astype(jnp.float32))
    output, pullback = jax.vjp(whole_model, *primals)
    row_live = jnp.stack([layouts[0][2], layouts[1][2]]).astype(jnp.float32)
    gradients = pullback(cotangent.astype(jnp.float32) * row_live[..., None])
    boundary = jnp.stack([gradients[0], output])
    return (boundary, gradients[1], gradients[2], gradients[3], gradients[4], gradients[5], gradients[6])
```

```python
from functools import partial

import jax
import jax.numpy as jnp
from jax import lax
from jax.experimental import pallas as pl
from jax.experimental.pallas import tpu as pltpu
from jax.sharding import PartitionSpec as P

D = 768
HEADS = 12
HEAD = 64
FF = 3072
SHORT_LEN = 128
LONG_LEN = 256


epsilon = 1e-05
masked_value = -1000000000.0


def passed_along(value, axis, steps):
    count = lax.axis_size(axis)
    initial, last = (max(0, -steps), min(count, count - steps))
    return lax.ppermute(value, axis, [(source, source + steps) for source in range(initial, last)])


def layer_norm(values_in, gain_row, shift_row):
    average = jnp.mean(values_in, -1, keepdims=True)
    centred = values_in - average
    spread = jnp.mean(centred * centred, -1, keepdims=True)
    return centred * lax.rsqrt(spread + epsilon) * gain_row + shift_row


def gated_units(gate_up):
    return jax.nn.gelu(gate_up[:, :FF], approximate=False) * gate_up[:, FF:]


def tables(segment, lengths):
    positions = jnp.arange(LONG_LEN)
    distance = jnp.abs(positions[:, None] - positions[None, :]).astype(jnp.float32)
    same_seq = positions[:, None] // segment == positions[None, :] // segment
    key_len = jnp.repeat(lengths, segment).reshape(-1, LONG_LEN)
    key_live = (positions % segment)[None, :] < key_len
    allowed = same_seq[None] & key_live[:, None, :]
    slopes = jnp.exp2(-8.0 * (jnp.arange(HEADS).astype(jnp.float32) + 1.0) / HEADS)
    alibi_bias = -slopes[:, None, None] * distance[None]
    return (allowed, alibi_bias, key_live.reshape(-1))


def grouped(rows_in, groups):
    return rows_in.reshape(groups, LONG_LEN, HEADS, HEAD)


def masked_scores(query, keys, allowed, alibi_bias):
    groups = allowed.shape[0]
    scores = jnp.einsum(
        "gqhd,gkhd->ghqk",
        grouped(query, groups),
        grouped(keys, groups),
        preferred_element_type=jnp.float32,
    )
    scores = scores * HEAD ** (-0.5) + alibi_bias[None]
    return jnp.where(allowed[:, None], scores, masked_value)


def forward(section_in, params, layout):
    weight_qkv, weight_out, weight_gate_up, weight_down, gain_rows, bias_rows = params
    allowed, alibi_bias, unused = layout
    rows_dev = section_in.shape[0]
    groups = allowed.shape[0]
    projected = jnp.dot(section_in, weight_qkv, preferred_element_type=jnp.float32)
    query = (projected[:, :D] + bias_rows[0]).astype(jnp.bfloat16)
    keys = projected[:, D : 2 * D].astype(jnp.bfloat16)
    values = (projected[:, 2 * D :] + bias_rows[1]).astype(jnp.bfloat16)
    scores = masked_scores(query, keys, allowed, alibi_bias)
    peak = jnp.max(scores, -1, keepdims=True)
    expo = jnp.exp(scores - peak)
    totals = jnp.sum(expo, -1, keepdims=True)
    probs_low = (expo / totals).astype(jnp.bfloat16)
    log_sums = (peak + jnp.log(totals))[..., 0]
    mixed = jnp.einsum(
        "ghqk,gkhd->gqhd", probs_low, grouped(values, groups), preferred_element_type=jnp.float32
    )
    mixed = mixed.reshape(rows_dev, D).astype(jnp.bfloat16)
    resid_one = section_in.astype(jnp.float32) + (
        jnp.dot(mixed, weight_out, preferred_element_type=jnp.float32) + bias_rows[2]
    )
    normed = layer_norm(resid_one, gain_rows[0], bias_rows[3])
    normed_low = normed.astype(jnp.bfloat16)
    gate_up = jnp.dot(normed_low, weight_gate_up, preferred_element_type=jnp.float32)
    hidden = gated_units(gate_up).astype(jnp.bfloat16)
    resid_two = normed + (
        jnp.dot(hidden, weight_down, preferred_element_type=jnp.float32) + bias_rows[4]
    )
    result = layer_norm(resid_two, gain_rows[1], bias_rows[5])
    return (
        result,
        (query, keys, values, log_sums, mixed, resid_one, normed_low, gate_up, hidden, resid_two),
    )


def forward_only(section_in, params, layout):
    return forward(section_in, params, layout)[0]


def back_ffn(incoming, saved, params):
    weight_qkv, weight_out, weight_gate_up, weight_down, gain_rows, bias_rows = params
    query, keys, values, log_sums, mixed, resid_one, normed_low, gate_up, hidden, resid_two = saved
    unused, pullback = jax.vjp(layer_norm, resid_two, gain_rows[1], bias_rows[5])
    grad_resid_two, grad_gain_two, grad_shift_two = pullback(incoming)
    grad_ffn = grad_resid_two.astype(jnp.bfloat16)
    grad_hidden = jnp.dot(grad_ffn, weight_down.T, preferred_element_type=jnp.float32)
    unused, pullback = jax.vjp(gated_units, gate_up)
    grad_gate_up = pullback(grad_hidden)[0].astype(jnp.bfloat16)
    grad_normed = (
        jnp.dot(grad_gate_up, weight_gate_up.T, preferred_element_type=jnp.float32) + grad_resid_two
    )
    unused, pullback = jax.vjp(layer_norm, resid_one, gain_rows[0], bias_rows[3])
    grad_resid_one, grad_gain_one, grad_shift_one = pullback(grad_normed)
    zero_row = jnp.zeros_like(grad_shift_one)
    grad_vectors = jnp.stack(
        [
            zero_row,
            zero_row,
            zero_row,
            grad_shift_one,
            jnp.sum(grad_ffn.astype(jnp.float32), 0),
            grad_shift_two,
        ]
    )
    grad_gain_rows = jnp.stack([grad_gain_one, grad_gain_two])
    return (grad_resid_one, (grad_gate_up, grad_ffn, grad_vectors, grad_gain_rows, normed_low, hidden))


def back_attn(grad_resid_one, saved, section_in, params, layout):
    weight_qkv, weight_out, weight_gate_up, weight_down, gain_rows, bias_rows = params
    allowed, alibi_bias, unused = layout
    query, keys, values, log_sums, mixed, resid_one, normed_low, gate_up, hidden, resid_two = saved
    rows_dev = section_in.shape[0]
    groups = allowed.shape[0]
    grad_attn = grad_resid_one.astype(jnp.bfloat16)
    grad_mixed = jnp.dot(grad_attn, weight_out.T, preferred_element_type=jnp.float32).astype(
        jnp.bfloat16
    )
    grad_mixed_g = grouped(grad_mixed, groups)
    probs = jnp.exp(masked_scores(query, keys, allowed, alibi_bias) - log_sums[..., None])
    grad_probs = jnp.einsum(
        "gqhd,gkhd->ghqk", grad_mixed_g, grouped(values, groups), preferred_element_type=jnp.float32
    )
    grad_scores = (probs * (grad_probs - jnp.sum(probs * grad_probs, -1, keepdims=True))).astype(
        jnp.bfloat16
    )
    grad_values = jnp.einsum(
        "ghqk,gqhd->gkhd",
        probs.astype(jnp.bfloat16),
        grad_mixed_g,
        preferred_element_type=jnp.float32,
    )
    grad_values = grad_values.reshape(rows_dev, D).astype(jnp.bfloat16)
    grad_query = jnp.einsum(
        "ghqk,gkhd->gqhd", grad_scores, grouped(keys, groups), preferred_element_type=jnp.float32
    ) * HEAD ** (-0.5)
    grad_query = grad_query.reshape(rows_dev, D).astype(jnp.bfloat16)
    grad_keys = jnp.einsum(
        "ghqk,gqhd->gkhd", grad_scores, grouped(query, groups), preferred_element_type=jnp.float32
    ) * HEAD ** (-0.5)
    grad_keys = grad_keys.reshape(rows_dev, D).astype(jnp.bfloat16)
    grad_projected = jnp.concatenate([grad_query, grad_keys, grad_values], 1)
    grad_section_in = (
        jnp.dot(grad_projected, weight_qkv.T, preferred_element_type=jnp.float32) + grad_resid_one
    )
    zero_row = jnp.zeros((D,), jnp.float32)
    grad_vectors = jnp.stack(
        [
            jnp.sum(grad_query.astype(jnp.float32), 0),
            jnp.sum(grad_values.astype(jnp.float32), 0),
            jnp.sum(grad_attn.astype(jnp.float32), 0),
            zero_row,
            zero_row,
            zero_row,
        ]
    )
    return (grad_section_in, (grad_projected, grad_attn, grad_vectors, mixed))


def silent(function):

    def quiet(*operands):
        return jax.tree.map(jnp.zeros_like, function(*operands))

    return quiet


def by_section(period, builder):
    branches = []
    for section_id in (0, 1):
        micro = period - section_id
        if 0 <= micro < 2:
            branches.append(builder(micro))
        else:
            branches.append(silent(builder(0)))
    return branches


S_SLOTS = 5
OWN_SLOTS = 3
N_CHUNKS = 12
MESH_IDS = pl.DeviceIdType.MESH


def reduce_kernel(
    xa, xm, xn, xh, gq, go, gg, gf, vec,
    o_qkv, o_out, o_gu, o_dn, o_vec,
    t_a, t_m, t_n, t_h, w_q, w_o, w_g, w_f,
    own, ra_relay, ra_fin, sa, own_b, rb_relay, rb_fin, sb, x_send, x_keep, x_recv, c_tmp, c_send, c_keep, c_recv,
    v_acc, v_recv,
    in_sem, peer_send, peer_recv,
    a_send, a_relay_recv, a_fin_recv, a2_send,
    b_send, b_relay_recv, b_fin_recv, b2_send,
    xs_sem, xr_sem, cs_sem, cr_sem, vs_sem, vr_sem,
):
    me = lax.axis_index("dp")
    core = me % 2
    xhi = (me // 2) % 2
    zz = (me // 4) % 4
    yy = me // 16

    def dev(y, z, x, c):
        return ((y * 4 + z) * 2 + x) * 2 + c

    peer_core = dev(yy, zz, xhi, 1 - core)
    peer_x = dev(yy, zz, 1 - xhi, core)
    y_ids = [dev((yy + k) % 4, zz, xhi, core) for k in (1, 2, 3)]
    z_ids = [dev(yy, (zz + k) % 4, xhi, core) for k in (1, 2, 3)]
    peers = [peer_core, peer_x] + y_ids + z_ids

    def remote(src, dst, send, recv, target):
        return pltpu.make_async_remote_copy(
            src_ref=src, dst_ref=dst, send_sem=send, recv_sem=recv,
            device_id={"dp": target}, device_id_type=MESH_IDS,
        )

    half = 512
    local = [
        pltpu.make_async_copy(xn, t_n.at[:, pl.ds(0, half)], in_sem.at[0]),
        pltpu.make_async_copy(gg.at[:, pl.ds(core * 3072, 3072)], w_g.at[pl.ds(0, half)], in_sem.at[1]),
        pltpu.make_async_copy(xa, t_a.at[:, pl.ds(0, half)], in_sem.at[2]),
        pltpu.make_async_copy(gq.at[:, pl.ds(core * 1152, 1152)], w_q.at[pl.ds(0, half)], in_sem.at[3]),
        pltpu.make_async_copy(xm, t_m.at[:, pl.ds(0, half)], in_sem.at[4]),
        pltpu.make_async_copy(go.at[:, pl.ds(core * 384, 384)], w_o.at[pl.ds(0, half)], in_sem.at[5]),
        pltpu.make_async_copy(xh.at[:, core], t_h.at[:, :, pl.ds(0, half)], in_sem.at[6]),
        pltpu.make_async_copy(gf, w_f.at[pl.ds(0, half)], in_sem.at[7]),
    ]
    other = 1 - core
    across = [
        remote(xn, t_n.at[:, pl.ds(half, half)], peer_send.at[0], peer_recv.at[0], peer_core),
        remote(gg.at[:, pl.ds(other * 3072, 3072)], w_g.at[pl.ds(half, half)], peer_send.at[1], peer_recv.at[1], peer_core),
        remote(xa, t_a.at[:, pl.ds(half, half)], peer_send.at[2], peer_recv.at[2], peer_core),
        remote(gq.at[:, pl.ds(other * 1152, 1152)], w_q.at[pl.ds(half, half)], peer_send.at[3], peer_recv.at[3], peer_core),
        remote(xm, t_m.at[:, pl.ds(half, half)], peer_send.at[4], peer_recv.at[4], peer_core),
        remote(go.at[:, pl.ds(other * 384, 384)], w_o.at[pl.ds(half, half)], peer_send.at[5], peer_recv.at[5], peer_core),
        remote(xh.at[:, other], t_h.at[:, :, pl.ds(half, half)], peer_send.at[6], peer_recv.at[6], peer_core),
        remote(gf, w_f.at[pl.ds(half, half)], peer_send.at[7], peer_recv.at[7], peer_core),
    ]
    for copy in local:
        copy.start()
    barrier = pltpu.get_barrier_semaphore()
    for peer in peers:
        pl.semaphore_signal(barrier, inc=1, device_id={"dp": peer}, device_id_type=MESH_IDS)
    pl.semaphore_wait(barrier, len(peers))
    for copy in across:
        copy.start()

    def v_sends(stage):
        targets = ([peer_core], [peer_x], y_ids, z_ids)[stage]
        base = (0, 1, 2, 5)[stage]
        count = len(targets)
        return [
            remote(
                v_acc.at[stage], v_recv.at[base + (count - 1 - k)],
                vs_sem.at[base + k], vr_sem.at[base + (count - 1 - k)], targets[k],
            )
            for k in range(count)
        ]

    def v_start(stage):
        for copy in v_sends(stage):
            copy.start()

    def v_finish(stage):
        base = (0, 1, 2, 5)[stage]
        count = (1, 1, 3, 3)[stage]
        copies = v_sends(stage)
        for copy in copies:
            copy.wait_send()
        total = v_acc[stage]
        for k in range(count):
            copies[count - 1 - k].wait_recv()
        for k in range(count):
            total = total + v_recv[base + k]
        v_acc[stage + 1] = total

    v_acc[0] = vec[...]
    v_start(0)

    def ring(par):
        right = y_ids[0] * (1 - par) + z_ids[0] * par
        left = y_ids[2] * (1 - par) + z_ids[2] * par
        place = yy * (1 - par) + zz * par
        return right, left, place

    def a1_copies(j):
        slot, mine = j % S_SLOTS, j % OWN_SLOTS
        right, left, p = ring(j % 2)
        far, nxt, prv = (p + 2) % 4, (p + 1) % 4, (p + 3) % 4
        return (
            remote(own.at[mine, 0, far], ra_relay.at[slot, 0], a_send.at[slot, 0], a_relay_recv.at[slot, 0], right),
            remote(own.at[mine, 1, far], ra_relay.at[slot, 1], a_send.at[slot, 1], a_relay_recv.at[slot, 1], left),
            remote(own.at[mine, 1, nxt], ra_fin.at[slot, 0, 1], a_send.at[slot, 2], a_fin_recv.at[slot, 0, 1], right),
            remote(own.at[mine, 0, prv], ra_fin.at[slot, 1, 0], a_send.at[slot, 3], a_fin_recv.at[slot, 1, 0], left),
        )

    def a2_copies(j):
        slot = j % S_SLOTS
        right, left, _ = ring(j % 2)
        return (
            remote(sa.at[slot, 0], ra_fin.at[slot, 0, 0], a2_send.at[slot, 0], a_fin_recv.at[slot, 0, 0], right),
            remote(sa.at[slot, 1], ra_fin.at[slot, 1, 1], a2_send.at[slot, 1], a_fin_recv.at[slot, 1, 1], left),
        )

    def b1_copies(j):
        slot = j % S_SLOTS
        right, left, p = ring(1 - j % 2)
        far, nxt, prv = (p + 2) % 4, (p + 1) % 4, (p + 3) % 4
        return (
            remote(own_b.at[slot, 0, far], rb_relay.at[slot, 0], b_send.at[slot, 0], b_relay_recv.at[slot, 0], right),
            remote(own_b.at[slot, 1, far], rb_relay.at[slot, 1], b_send.at[slot, 1], b_relay_recv.at[slot, 1], left),
            remote(own_b.at[slot, 1, nxt], rb_fin.at[slot, 0, 1], b_send.at[slot, 2], b_fin_recv.at[slot, 0, 1], right),
            remote(own_b.at[slot, 0, prv], rb_fin.at[slot, 1, 0], b_send.at[slot, 3], b_fin_recv.at[slot, 1, 0], left),
        )

    def b2_copies(j):
        slot = j % S_SLOTS
        right, left, _ = ring(1 - j % 2)
        return (
            remote(sb.at[slot, 0], rb_fin.at[slot, 0, 0], b2_send.at[slot, 0], b_fin_recv.at[slot, 0, 0], right),
            remote(sb.at[slot, 1], rb_fin.at[slot, 1, 1], b2_send.at[slot, 1], b_fin_recv.at[slot, 1, 1], left),
        )

    def x_copy(j):
        slot = j % S_SLOTS
        return remote(x_send.at[slot], x_recv.at[slot], xs_sem.at[slot], xr_sem.at[slot], peer_x)

    def c_copy(j):
        slot = j % S_SLOTS
        return remote(c_send.at[slot], c_recv.at[slot], cs_sem.at[slot], cr_sem.at[slot], peer_core)

    def wait_operands(*which):
        for k in which:
            local[k].wait()
            across[k].wait()

    def store_rows(j, halves):
        mine = j % OWN_SLOTS
        par = j % 2
        for y in range(4):
            for z in range(4):
                first = y * (1 - par) + z * par
                second = z * (1 - par) + y * par
                for h in range(2):
                    own[mine, h, first, second] = halves[h][y * 4 + z]

    def product(lhs, rhs):
        return jnp.dot(lhs, rhs, preferred_element_type=jnp.float32).astype(jnp.bfloat16)

    def split_halves(result):
        return [result[:, h * 256:(h + 1) * 256].reshape(16, 48, 256) for h in range(2)]

    def compute(j):
        @pl.when(j < 6)
        def _():
            @pl.when(j == 0)
            def _():
                wait_operands(0, 1)
            rhs = w_g[:, pl.ds(pl.multiple_of(j * 512, 512), 512)]
            store_rows(j, split_halves(product(t_n[...], rhs)))

        @pl.when((j >= 6) & (j < 8))
        def _():
            @pl.when(j == 6)
            def _():
                wait_operands(2, 3)
            rhs = w_q[:, pl.ds(pl.multiple_of((j - 6) * 512, 512), 512)]
            store_rows(j, split_halves(product(t_a[...], rhs)))

        @pl.when(j == 8)
        def _():
            wait_operands(4, 5)
            one = product(t_a[...], w_q[:, pl.ds(1024, 128)])
            two = product(t_m[...], w_o[...])
            store_rows(j, split_halves(jnp.concatenate([one, two], axis=1)))

        @pl.when(j >= 9)
        def _():
            @pl.when(j == 9)
            def _():
                wait_operands(6, 7)
            rhs = w_f[:, pl.ds(pl.multiple_of((j - 9) * 256, 256), 256)]
            result = product(t_h[...].reshape(1536, 1024), rhs).reshape(16, 2, 48, 256)
            store_rows(j, [result[:, 0], result[:, 1]])

    def f32(value):
        return value.astype(jnp.float32)

    def step(i, carry):
        @pl.when(i < N_CHUNKS)
        def _():
            compute(i)
            for copy in a1_copies(i):
                copy.start()

        j1 = i - 1

        @pl.when((j1 >= 0) & (j1 < N_CHUNKS))
        def _():
            slot, mine = j1 % S_SLOTS, j1 % OWN_SLOTS
            _, _, p = ring(j1 % 2)
            first = a1_copies(j1)
            second = a2_copies(j1)
            first[0].wait_recv()
            sa[slot, 0] = (f32(own[mine, 0, (p + 1) % 4]) + f32(ra_relay[slot, 0])).astype(jnp.bfloat16)
            second[0].start()
            first[1].wait_recv()
            sa[slot, 1] = (f32(own[mine, 1, (p + 3) % 4]) + f32(ra_relay[slot, 1])).astype(jnp.bfloat16)
            second[1].start()

        j2 = i - 2

        @pl.when((j2 >= 0) & (j2 < N_CHUNKS))
        def _():
            slot, mine = j2 % S_SLOTS, j2 % OWN_SLOTS
            _, _, p = ring(j2 % 2)
            first = a1_copies(j2)
            second = a2_copies(j2)
            for copy in first + second:
                copy.wait_send()
            first[2].wait_recv()
            first[3].wait_recv()
            second[0].wait_recv()
            second[1].wait_recv()
            for h in range(2):
                own_b[slot, h] = (
                    f32(own[mine, h, p]) + f32(ra_fin[slot, 0, h]) + f32(ra_fin[slot, 1, h])
                ).astype(jnp.bfloat16)
            for copy in b1_copies(j2):
                copy.start()

        j3 = i - 3

        @pl.when((j3 >= 0) & (j3 < N_CHUNKS))
        def _():
            slot = j3 % S_SLOTS
            _, _, p = ring(1 - j3 % 2)
            first = b1_copies(j3)
            second = b2_copies(j3)
            first[0].wait_recv()
            sb[slot, 0] = (f32(own_b[slot, 0, (p + 1) % 4]) + f32(rb_relay[slot, 0])).astype(jnp.bfloat16)
            second[0].start()
            first[1].wait_recv()
            sb[slot, 1] = (f32(own_b[slot, 1, (p + 3) % 4]) + f32(rb_relay[slot, 1])).astype(jnp.bfloat16)
            second[1].start()

        j4 = i - 4

        @pl.when((j4 >= 0) & (j4 < N_CHUNKS))
        def _():
            slot = j4 % S_SLOTS
            _, _, p = ring(1 - j4 % 2)
            first = b1_copies(j4)
            second = b2_copies(j4)
            for copy in first + second:
                copy.wait_send()
            first[2].wait_recv()
            first[3].wait_recv()
            second[0].wait_recv()
            second[1].wait_recv()
            total = [
                f32(own_b[slot, h, p]) + f32(rb_fin[slot, 0, h]) + f32(rb_fin[slot, 1, h])
                for h in range(2)
            ]
            low = xhi == 0

            @pl.when(j4 < 9)
            def _():
                for h in range(2):
                    x_send[slot, h] = jnp.where(low, total[h][24:], total[h][:24])
                    x_keep[slot, h] = jnp.where(low, total[h][:24], total[h][24:])

            @pl.when(j4 >= 9)
            def _():
                sent = jnp.where(low, total[1], total[0])
                kept = jnp.where(low, total[0], total[1])
                for h in range(2):
                    x_send[slot, h] = sent[h * 24:(h + 1) * 24]
                    x_keep[slot, h] = kept[h * 24:(h + 1) * 24]

            x_copy(j4).start()

        j5 = i - 5

        @pl.when((j5 >= 0) & (j5 < N_CHUNKS))
        def _():
            slot = j5 % S_SLOTS
            x_copy(j5).wait()

            @pl.when(j5 < 9)
            def _():
                for h in range(2):
                    c_tmp[h] = x_keep[slot, h] + x_recv[slot, h]
                low = core == 0
                for h in range(2):
                    upper, lower = c_tmp[h, 0:12], c_tmp[h, 12:24]
                    c_send[slot, h, 0:12] = jnp.where(low, lower, upper)
                    c_keep[slot, h, 0:12] = jnp.where(low, upper, lower)
                c_copy(j5).start()

            @pl.when(j5 >= 9)
            def _():
                column = pl.ds(pl.multiple_of((j5 - 9) * 256, 256), 256)
                for h in range(2):
                    o_dn[h * 24:(h + 1) * 24, column] = x_keep[slot, h] + x_recv[slot, h]

        j6 = i - 6

        @pl.when((j6 >= 0) & (j6 < 9))
        def _():
            slot = j6 % S_SLOTS
            c_copy(j6).wait()
            for source, who in ((c_keep, core), (c_recv, 1 - core)):
                @pl.when(j6 < 6)
                def _():
                    for h in range(2):
                        column = pl.multiple_of(who * 3072 + j6 * 512 + h * 256, 256)
                        o_gu[:, pl.ds(column, 256)] = source[slot, h, 0:12]

                @pl.when((j6 >= 6) & (j6 < 8))
                def _():
                    for h in range(2):
                        column = pl.multiple_of(who * 1152 + (j6 - 6) * 512 + h * 256, 128)
                        o_qkv[:, pl.ds(column, 256)] = source[slot, h, 0:12]

                @pl.when(j6 == 8)
                def _():
                    o_qkv[:, pl.ds(pl.multiple_of(who * 1152 + 1024, 128), 128)] = source[slot, 0, 0:12, 0:128]
                    o_out[:, pl.ds(pl.multiple_of(who * 384, 128), 128)] = source[slot, 0, 0:12, 128:256]
                    o_out[:, pl.ds(pl.multiple_of(who * 384 + 128, 128), 256)] = source[slot, 1, 0:12]

        for stage in range(4):
            @pl.when(i == 2 * stage + 2)
            def _():
                v_finish(stage)
                if stage < 3:
                    v_start(stage + 1)

        return carry

    lax.fori_loop(0, N_CHUNKS + 6, step, 0)
    o_vec[...] = v_acc[4]


def reduce_weights(xa, xm, xn, xh, gq, go, gg, gf, vec):
    low, wide = jnp.bfloat16, jnp.float32
    hbm = pl.BlockSpec(memory_space=pl.ANY)
    vmem = pl.BlockSpec(memory_space=pltpu.VMEM)
    dma = pltpu.SemaphoreType.DMA
    s = S_SLOTS
    return pl.pallas_call(
        reduce_kernel,
        out_shape=[
            jax.ShapeDtypeStruct((12, 2304), wide),
            jax.ShapeDtypeStruct((12, 768), wide),
            jax.ShapeDtypeStruct((12, 6144), wide),
            jax.ShapeDtypeStruct((48, 768), wide),
            jax.ShapeDtypeStruct((8, 768), wide),
        ],
        in_specs=[hbm] * 8 + [vmem],
        out_specs=[vmem] * 5,
        scratch_shapes=[
            pltpu.VMEM((768, 1024), low),
            pltpu.VMEM((768, 1024), low),
            pltpu.VMEM((768, 1024), low),
            pltpu.VMEM((32, 48, 1024), low),
            pltpu.VMEM((1024, 1152), low),
            pltpu.VMEM((1024, 384), low),
            pltpu.VMEM((1024, 3072), low),
            pltpu.VMEM((1024, 768), low),
            pltpu.VMEM((OWN_SLOTS, 2, 4, 4, 48, 256), low),
            pltpu.VMEM((s, 2, 4, 48, 256), low),
            pltpu.VMEM((s, 2, 2, 4, 48, 256), low),
            pltpu.VMEM((s, 2, 4, 48, 256), low),
            pltpu.VMEM((s, 2, 4, 48, 256), low),
            pltpu.VMEM((s, 2, 48, 256), low),
            pltpu.VMEM((s, 2, 2, 48, 256), low),
            pltpu.VMEM((s, 2, 48, 256), low),
            pltpu.VMEM((s, 2, 24, 256), wide),
            pltpu.VMEM((s, 2, 24, 256), wide),
            pltpu.VMEM((s, 2, 24, 256), wide),
            pltpu.VMEM((2, 24, 256), wide),
            pltpu.VMEM((s, 2, 16, 256), wide),
            pltpu.VMEM((s, 2, 16, 256), wide),
            pltpu.VMEM((s, 2, 16, 256), wide),
            pltpu.VMEM((5, 8, 768), wide),
            pltpu.VMEM((8, 8, 768), wide),
            dma((8,)), dma((8,)), dma((8,)),
            dma((s, 4)), dma((s, 2)), dma((s, 2, 2)), dma((s, 2)),
            dma((s, 4)), dma((s, 2)), dma((s, 2, 2)), dma((s, 2)),
            dma((s,)), dma((s,)), dma((s,)), dma((s,)),
            dma((8,)), dma((8,)),
        ],
        compiler_params=pltpu.CompilerParams(
            collective_id=0, has_side_effects=True, vmem_limit_bytes=56 * 1024 * 1024
        ),
        cost_estimate=pl.CostEstimate(flops=10 ** 10, bytes_accessed=2 * 10 ** 7, transcendentals=0),
        name="reduce_weights",
    )(xa, xm, xn, xh.reshape(32, 2, 48, 512), gq, go, gg, gf, vec)


def on_device(
    tokens, cotangent, short_lens, long_lens, w_qkv, w_out, w_gate_up, w_down, gains, biases
):
    first_section = lax.axis_index("section") == 0
    params = (w_qkv[0], w_out[0], w_gate_up[0], w_down[0], gains[0], biases[0])
    rows_dev = tokens.shape[1]
    layouts = (tables(SHORT_LEN, short_lens), tables(LONG_LEN, long_lens))
    received = jnp.zeros((rows_dev, D), jnp.bfloat16)
    section_inputs = []
    finals = []
    for period in range(3):
        section_in = jnp.where(first_section, tokens[min(period, 1)], received)
        branches = by_section(
            period, lambda micro: partial(forward_only, params=params, layout=layouts[micro])
        )
        result = lax.cond(first_section, branches[0], branches[1], section_in)
        section_inputs.append(section_in)
        finals.append(result)
        if period < 2:
            received = passed_along(result.astype(jnp.bfloat16), "section", 1)
    cot_rows = [
        cotangent[micro].astype(jnp.float32) * layouts[micro][2][:, None].astype(jnp.float32)
        for micro in range(2)
    ]
    grad_gain_rows = jnp.zeros(params[4].shape, jnp.float32)
    grad_vectors = jnp.zeros(params[5].shape, jnp.float32)
    operands = [None, None, None]
    returned = jnp.zeros((rows_dev, D), jnp.bfloat16)
    grad_rows = [None, None]
    for rewind in range(3):
        period = 2 - rewind
        incoming = jnp.where(
            first_section, returned.astype(jnp.float32), cot_rows[max(1 - rewind, 0)]
        )
        branches = by_section(
            period, lambda micro: partial(forward, params=params, layout=layouts[micro])
        )
        saved = lax.cond(first_section, branches[0], branches[1], section_inputs[period])[1]
        branches = by_section(period, lambda micro: partial(back_ffn, params=params))
        grad_resid_one, ffn_terms = lax.cond(
            first_section, branches[0], branches[1], incoming, saved
        )
        grad_vectors = grad_vectors + ffn_terms[2]
        grad_gain_rows = grad_gain_rows + ffn_terms[3]
        branches = by_section(
            period, lambda micro: partial(back_attn, params=params, layout=layouts[micro])
        )
        grad_section_in, attn_terms = lax.cond(
            first_section, branches[0], branches[1], grad_resid_one, saved, section_inputs[period]
        )
        operands[period] = (
            section_inputs[period], attn_terms[3], ffn_terms[4], ffn_terms[5],
            attn_terms[0], attn_terms[1], ffn_terms[0], ffn_terms[1],
        )
        grad_vectors = grad_vectors + attn_terms[2]
        if rewind < 2:
            returned = passed_along(grad_section_in.astype(jnp.bfloat16), "section", -1)
        if rewind > 0:
            grad_rows[period] = grad_section_in
    boundary = jnp.where(
        first_section, jnp.stack([grad_rows[0], grad_rows[1]]), jnp.stack([finals[1], finals[2]])
    )[None]
    early = jax.tree.map(lambda u, v: jnp.where(first_section, u, v), operands[0], operands[1])
    late = jax.tree.map(lambda u, v: jnp.where(first_section, u, v), operands[1], operands[2])
    both = [jnp.concatenate(pair, 0) for pair in zip(early, late)]
    vec = jnp.concatenate([grad_gain_rows, grad_vectors], 0)
    g_qkv, g_out, g_gu, g_dn, g_vec = reduce_weights(
        both[0].T, both[1].T, both[2].T, both[3].T, both[4], both[5], both[6], both[7], vec
    )
    mine = lax.dynamic_slice_in_dim(g_vec, lax.axis_index("dp") * 12, 12, axis=1)
    return (boundary, g_qkv[None], g_out[None], g_gu[None], g_dn[None], mine[None, :2], mine[None, 2:])


def solution(mesh):
    placed = (
        P(None, "dp", None),
        P(None, "dp", None),
        P("dp"),
        P("dp"),
        P("section", None, None),
        P("section", None, None),
        P("section", None, None),
        P("section", None, None),
        P("section", None, None),
        P("section", None, None),
    )
    return jax.shard_map(
        on_device,
        mesh=mesh,
        in_specs=placed,
        out_specs=(
            P("section", None, "dp", None),
            P("section", "dp", None),
            P("section", "dp", None),
            P("section", "dp", None),
            P("section", "dp", None),
            P("section", None, "dp"),
            P("section", None, "dp"),
        ),
        check_vma=False,
    )
```

```python
import jax
import jax.numpy as jnp
from jax import lax
from jax.experimental import pallas as pl
from jax.experimental.pallas import tpu as pltpu
from jax.sharding import PartitionSpec as P

D = 768
HEADS = 12
HEAD = 64
FF = 3072


epsilon = 1e-05
masked_value = -1000000000.0


ROWS_DEV = 256
BLOCK = 512
BAND = 32


def dot_nn(lhs, rhs):
    return jnp.dot(lhs, rhs, preferred_element_type=jnp.float32)


def dot_nt(lhs, rhs):
    return lax.dot_general(lhs, rhs, (((1,), (1,)), ((), ())), preferred_element_type=jnp.float32)


def dot_tn(lhs, rhs):
    return lax.dot_general(lhs, rhs, (((0,), (0,)), ((), ())), preferred_element_type=jnp.float32)


def f32(value):
    return value.astype(jnp.float32)


def bf16(value):
    return value.astype(jnp.bfloat16)


def fold_rows(value):
    return jnp.sum(value.reshape(value.shape[0] // 8, 8, value.shape[1]), 0)


def gelu_terms(gate):
    cdf = 0.5 * (1.0 + lax.erf(gate * 0.7071067811865476))
    density = jnp.exp(-0.5 * gate * gate) * 0.3989422804014327
    return gate * cdf, cdf + gate * density


def layers_kernel(
    short_lens, long_lens, slopes, tokens, cotangent, w_qkv, w_out, w_gate_up, w_down, gains, biases,
    boundary, o_at, o_mt, o_nt, o_ht, o_gq, o_go, o_gg, o_gf, o_vec,
    wq, wo, wg, wd, x_s, g_s, qkv_s, p_s, mixed_s, low_s, n1_s, n2_s, r1_s, r2_s, gu_s, at_s, mt_s, nt_s, ht_s,
    gf_s, ga_s, send_s, out_s, acc_s, f_s, gate_s, up_s, dist_s, mask_s, vec_s,
    w_sem, x_sem, g_sem, out_sem, spill_sem, f_send, f_recv, b_send, b_recv,
):
    sec = lax.axis_index("section")
    first = sec == 0
    second = sec == 1
    w_copies = [
        pltpu.make_async_copy(w_qkv, wq, w_sem.at[0]),
        pltpu.make_async_copy(w_out, wo, w_sem.at[1]),
        pltpu.make_async_copy(w_gate_up, wg, w_sem.at[2]),
        pltpu.make_async_copy(w_down, wd, w_sem.at[3]),
    ]

    def token_copy(m):
        return pltpu.make_async_copy(tokens.at[m], x_s.at[m], x_sem.at[m])

    def cot_copy(m):
        return pltpu.make_async_copy(cotangent.at[m], g_s.at[m], g_sem.at[m])

    def across(src, dst, send, recv):
        return pltpu.make_async_remote_copy(
            src_ref=src, dst_ref=dst, send_sem=send, recv_sem=recv,
            device_id={"section": 1 - sec}, device_id_type=pl.DeviceIdType.MESH,
        )

    def hand_on(m):
        return across(send_s.at[m], x_s.at[m], f_send.at[m], f_recv.at[m])

    def hand_back(m):
        return across(send_s.at[m], g_s.at[m], b_send.at[m], b_recv.at[m])

    @pl.when(first)
    def _():
        token_copy(0).start()

    w_copies[0].start()
    w_copies[1].start()

    @pl.when(first)
    def _():
        token_copy(1).start()

    w_copies[2].start()
    w_copies[3].start()

    @pl.when(second)
    def _():
        cot_copy(0).start()
        cot_copy(1).start()

    barrier = pltpu.get_barrier_semaphore()
    pl.semaphore_signal(
        barrier, inc=1, device_id={"section": 1 - sec}, device_id_type=pl.DeviceIdType.MESH
    )
    pl.semaphore_wait(barrier, 1)

    vec_s[...] = jnp.zeros_like(vec_s)
    rows_j = lax.broadcasted_iota(jnp.int32, (256, 256), 0)
    cols_i = lax.broadcasted_iota(jnp.int32, (256, 256), 1)
    dist_s[...] = jnp.abs(rows_j - cols_i).astype(jnp.float32)
    length_a, length_b, length_long = short_lens[0], short_lens[1], long_lens[0]
    for m in range(2):
        if m == 0:
            limit = jnp.where(rows_j < 128, length_a, length_b + 128)
            apart = jnp.where((rows_j >> 7) == (cols_i >> 7), 0, 1024)
            ok = rows_j + apart < limit
        else:
            ok = rows_j < length_long
        mask_s[m] = jnp.where(ok, 1.0, 0.0)

    def band(k):
        return pl.ds(pl.multiple_of(k * BAND, BAND), BAND)

    def normalise(value):
        average = jnp.mean(value, -1, keepdims=True)
        centred = value - average
        inverse = lax.rsqrt(jnp.mean(centred * centred, -1, keepdims=True) + epsilon)
        return centred * inverse, inverse

    def spill(m):
        cols = pl.ds(m * 256, 256)
        return [
            pltpu.make_async_copy(at_s.at[m], o_at.at[m], spill_sem.at[m, 0]),
            pltpu.make_async_copy(mt_s.at[m], o_mt.at[m], spill_sem.at[m, 1]),
            pltpu.make_async_copy(nt_s.at[m], o_nt.at[m], spill_sem.at[m, 2]),
            pltpu.make_async_copy(ht_s.at[m], o_ht.at[m], spill_sem.at[m, 3]),
        ]

    def spill_back(m):
        return [
            pltpu.make_async_copy(qkv_s.at[m], o_gq.at[m], spill_sem.at[m, 4]),
            pltpu.make_async_copy(ga_s.at[m], o_go.at[m], spill_sem.at[m, 5]),
            pltpu.make_async_copy(gu_s.at[m], o_gg.at[m], spill_sem.at[m, 6]),
            pltpu.make_async_copy(gf_s.at[m], o_gf.at[m], spill_sem.at[m, 7]),
        ]

    def out_copy(m):
        return pltpu.make_async_copy(out_s.at[m], boundary.at[m], out_sem.at[m])

    lanes = lax.broadcasted_iota(jnp.int32, (256, 128), 1)

    def forward(m, carry):
        @pl.when(first)
        def _():
            token_copy(m).wait()

        @pl.when(second)
        def _():
            hand_on(m).wait_recv()

        @pl.when(m == 0)
        def _():
            w_copies[0].wait()

        x = x_s[m]
        at_s[m] = x.T
        query = dot_nn(x, wq[:, 0:768]) + biases[0:1]
        qkv_s[m, :, 0:768] = bf16(f32(bf16(query)) * 0.125)
        qkv_s[m, :, 768:1536] = bf16(dot_nn(x, wq[:, 768:1536]))
        qkv_s[m, :, 1536:2304] = bf16(dot_nn(x, wq[:, 1536:2304]) + biases[1:2])

        def heads(hp, carry):
            lane0 = pl.multiple_of(hp * 128, 128)
            q2 = qkv_s[m, :, pl.ds(lane0, 128)]
            k2 = qkv_s[m, :, pl.ds(lane0 + 768, 128)]
            v2 = qkv_s[m, :, pl.ds(lane0 + 1536, 128)]
            outs = []
            for e in range(2):
                keep = (lanes < 64) if e == 0 else (lanes >= 64)
                qm = jnp.where(keep, q2, jnp.zeros_like(q2))
                scores = dot_nt(k2, qm) - slopes[2 * hp + e] * dist_s[...]
                scores = jnp.where(mask_s[m] > 0.5, scores, masked_value)
                expo = jnp.exp(scores - jnp.max(scores, 0, keepdims=True))
                total = jnp.sum(expo, 0, keepdims=True)
                probs = bf16(expo * (1.0 / total))
                p_s[m, 2 * hp + e] = probs
                outs.append(dot_tn(probs, v2))
            mixed_s[m, :, pl.ds(lane0, 128)] = bf16(jnp.where(lanes < 64, outs[0], outs[1]))
            return carry

        lax.fori_loop(0, 6, heads, 0)

        @pl.when(m == 0)
        def _():
            w_copies[1].wait()

        mixed = mixed_s[m]
        mt_s[m] = mixed.T
        acc_s[...] = dot_nn(mixed, wo[...])

        def norm_one(k, carry):
            r = band(k)
            value = f32(x_s[m, r]) + (acc_s[r] + biases[2:3])
            unit, inverse = normalise(value)
            normed = unit * gains[0:1] + biases[3:4]
            n1_s[m, r] = bf16(unit)
            r1_s[m, r] = inverse
            f_s[r] = normed
            low_s[r] = bf16(normed)
            return carry

        lax.fori_loop(0, 8, norm_one, 0)

        @pl.when(m == 0)
        def _():
            w_copies[2].wait()
            w_copies[3].wait()

        nt_s[m] = low_s[...].T
        acc_s[...] = jnp.zeros_like(acc_s)

        def ffn(jb, carry):
            c0 = pl.multiple_of(jb * BLOCK, BLOCK)
            low = low_s[...]
            gate_s[...] = dot_nn(low, wg[:, pl.ds(c0, BLOCK)])
            up_s[...] = dot_nn(low, wg[:, pl.ds(c0 + FF, BLOCK)])
            for k in range(8):
                r = pl.ds(k * BAND, BAND)
                gate, up = gate_s[r], up_s[r]
                act, slope = gelu_terms(gate)
                gu_s[m, r, pl.ds(c0, BLOCK)] = bf16(up * slope)
                gu_s[m, r, pl.ds(c0 + FF, BLOCK)] = bf16(act)
                gate_s[r] = act * up
            hid = bf16(gate_s[...])
            ht_s[m, pl.ds(c0, BLOCK)] = hid.T
            acc_s[...] += dot_nn(hid, wd[pl.ds(c0, BLOCK)])
            return carry

        lax.fori_loop(0, 6, ffn, 0)

        def norm_two(k, carry):
            r = band(k)
            value = f_s[r] + (acc_s[r] + biases[4:5])
            unit, inverse = normalise(value)
            n2_s[m, r] = bf16(unit)
            r2_s[m, r] = inverse
            result = unit * gains[1:2] + biases[5:6]
            out_s[m, r] = result
            send_s[m, r] = bf16(result)
            return carry

        lax.fori_loop(0, 8, norm_two, 0)

        @pl.when(first)
        def _():
            hand_on(m).start()

        @pl.when(second)
        def _():
            out_copy(m).start()

        for copy in spill(m):
            copy.start()
        return carry

    lax.fori_loop(0, 2, forward, 0)

    def norm_back(grad, unit, inverse, gain):
        scaled = grad * gain
        mean_one = jnp.mean(scaled, -1, keepdims=True)
        mean_two = jnp.mean(scaled * unit, -1, keepdims=True)
        return inverse * (scaled - mean_one - unit * mean_two)

    def backward(m, carry):
        @pl.when(first)
        def _():
            hand_on(m).wait_send()
            hand_back(m).wait_recv()

        @pl.when(second)
        def _():
            cot_copy(m).wait()
            out_copy(m).wait()

        def back_two(k, carry):
            r = band(k)
            row = lax.broadcasted_iota(jnp.int32, (BAND, 1), 0) + k * BAND
            limit = jnp.where(m == 0, jnp.where(row < 128, length_a, length_b + 128), length_long)
            live = jnp.where((row < limit) | first, 1.0, 0.0)
            grad = f32(g_s[m, r]) * live
            unit = f32(n2_s[m, r])
            vec_s[1] += fold_rows(grad * unit)
            vec_s[7] += fold_rows(grad)
            grad_in = norm_back(grad, unit, r2_s[m, r], gains[1:2])
            f_s[r] = grad_in
            low = bf16(grad_in)
            gf_s[m, r] = low
            vec_s[6] += fold_rows(f32(low))
            return carry

        lax.fori_loop(0, 8, back_two, 0)
        acc_s[...] = jnp.zeros_like(acc_s)

        def ffn_back(jb, carry):
            c0 = pl.multiple_of(jb * BLOCK, BLOCK)
            gate_s[...] = dot_nt(gf_s[m], wd[pl.ds(c0, BLOCK)])
            for k in range(8):
                r = pl.ds(k * BAND, BAND)
                hid = gate_s[r]
                gu_s[m, r, pl.ds(c0, BLOCK)] = bf16(hid * f32(gu_s[m, r, pl.ds(c0, BLOCK)]))
                gu_s[m, r, pl.ds(c0 + FF, BLOCK)] = bf16(hid * f32(gu_s[m, r, pl.ds(c0 + FF, BLOCK)]))
            acc_s[...] += dot_nt(gu_s[m, :, pl.ds(c0, BLOCK)], wg[:, pl.ds(c0, BLOCK)])
            acc_s[...] += dot_nt(gu_s[m, :, pl.ds(c0 + FF, BLOCK)], wg[:, pl.ds(c0 + FF, BLOCK)])
            return carry

        lax.fori_loop(0, 6, ffn_back, 0)

        def back_one(k, carry):
            r = band(k)
            grad = acc_s[r] + f_s[r]
            unit = f32(n1_s[m, r])
            vec_s[0] += fold_rows(grad * unit)
            vec_s[5] += fold_rows(grad)
            grad_in = norm_back(grad, unit, r1_s[m, r], gains[0:1])
            f_s[r] = grad_in
            low = bf16(grad_in)
            ga_s[m, r] = low
            vec_s[4] += fold_rows(f32(low))
            return carry

        lax.fori_loop(0, 8, back_one, 0)
        low_s[...] = bf16(dot_nt(ga_s[m], wo[...]))

        def heads_back(hp, carry):
            lane0 = pl.multiple_of(hp * 128, 128)
            q2 = qkv_s[m, :, pl.ds(lane0, 128)]
            k2 = qkv_s[m, :, pl.ds(lane0 + 768, 128)]
            v2 = qkv_s[m, :, pl.ds(lane0 + 1536, 128)]
            do2 = low_s[:, pl.ds(lane0, 128)]
            dq, dk, dv = [], [], []
            for e in range(2):
                keep = (lanes < 64) if e == 0 else (lanes >= 64)
                vm = jnp.where(keep, v2, jnp.zeros_like(v2))
                probs = p_s[m, 2 * hp + e]
                grad_probs = dot_nt(vm, do2)
                weighted = f32(probs) * grad_probs
                total = jnp.sum(weighted, 0, keepdims=True)
                grad_scores = bf16(weighted - f32(probs) * total)
                dv.append(dot_nn(probs, do2))
                dk.append(dot_nn(grad_scores, q2))
                dq.append(dot_tn(grad_scores, k2))
            grad_q = bf16(jnp.where(lanes < 64, dq[0], dq[1]) * 0.125)
            grad_k = bf16(jnp.where(lanes < 64, dk[0], dk[1]))
            grad_v = bf16(jnp.where(lanes < 64, dv[0], dv[1]))
            vec_s[2, :, pl.ds(lane0, 128)] += fold_rows(f32(grad_q))
            vec_s[3, :, pl.ds(lane0, 128)] += fold_rows(f32(grad_v))
            qkv_s[m, :, pl.ds(lane0, 128)] = grad_q
            qkv_s[m, :, pl.ds(lane0 + 768, 128)] = grad_k
            qkv_s[m, :, pl.ds(lane0 + 1536, 128)] = grad_v
            return carry

        lax.fori_loop(0, 6, heads_back, 0)
        grad_a = dot_nt(qkv_s[m], wq[...]) + f_s[...]

        @pl.when(second)
        def _():
            send_s[m] = bf16(grad_a)
            hand_back(m).start()

        @pl.when(first)
        def _():
            out_s[m] = grad_a
            out_copy(m).start()

        for copy in spill_back(m):
            copy.start()
        return carry

    lax.fori_loop(0, 2, backward, 0)
    for k in range(8):
        o_vec[k:k + 1] = jnp.sum(vec_s[k], 0, keepdims=True)

    for m in range(2):
        for copy in spill(m) + spill_back(m):
            copy.wait()

        @pl.when(second)
        def _():
            hand_back(m).wait_send()

        @pl.when(first)
        def _():
            out_copy(m).wait()


def run_layers(short_lens, long_lens, tokens, cotangent, w_qkv, w_out, w_gate_up, w_down, gains, biases):
    low, wide = jnp.bfloat16, jnp.float32
    hbm = pl.BlockSpec(memory_space=pl.ANY)
    vmem = pl.BlockSpec(memory_space=pltpu.VMEM)
    smem = pl.BlockSpec(memory_space=pltpu.SMEM)
    dma = pltpu.SemaphoreType.DMA
    slopes = jnp.exp2(-8.0 * (jnp.arange(HEADS).astype(wide) + 1.0) / HEADS)

    def of(shape, dtype):
        return pltpu.VMEM(shape, dtype)

    return pl.pallas_call(
        layers_kernel,
        out_shape=[
            jax.ShapeDtypeStruct((2, 256, 768), wide),
            jax.ShapeDtypeStruct((2, 768, 256), low),
            jax.ShapeDtypeStruct((2, 768, 256), low),
            jax.ShapeDtypeStruct((2, 768, 256), low),
            jax.ShapeDtypeStruct((2, 3072, 256), low),
            jax.ShapeDtypeStruct((2, 256, 2304), low),
            jax.ShapeDtypeStruct((2, 256, 768), low),
            jax.ShapeDtypeStruct((2, 256, 6144), low),
            jax.ShapeDtypeStruct((2, 256, 768), low),
            jax.ShapeDtypeStruct((8, 768), wide),
        ],
        in_specs=[smem] * 3 + [hbm] * 6 + [vmem] * 2,
        out_specs=[hbm] * 9 + [vmem],
        scratch_shapes=[
            of((768, 2304), low), of((768, 768), low), of((768, 6144), low), of((3072, 768), low),
            of((2, 256, 768), low), of((2, 256, 768), low), of((2, 256, 2304), low), of((2, 12, 256, 256), low),
            of((2, 256, 768), low), of((256, 768), low), of((2, 256, 768), low), of((2, 256, 768), low),
            of((2, 256, 1), wide), of((2, 256, 1), wide), of((2, 256, 6144), low),
            of((2, 768, 256), low), of((2, 768, 256), low), of((2, 768, 256), low), of((2, 3072, 256), low),
            of((2, 256, 768), low), of((2, 256, 768), low), of((2, 256, 768), low), of((2, 256, 768), wide),
            of((256, 768), wide), of((256, 768), wide), of((256, 512), wide), of((256, 512), wide),
            of((256, 256), wide), of((2, 256, 256), wide), of((8, 8, 768), wide),
            dma((4,)), dma((2,)), dma((2,)), dma((2,)), dma((2, 8)), dma((2,)), dma((2,)), dma((2,)), dma((2,)),
        ],
        compiler_params=pltpu.CompilerParams(
            collective_id=1, has_side_effects=True, vmem_limit_bytes=60 * 1024 * 1024
        ),
        cost_estimate=pl.CostEstimate(flops=2 * 10 ** 10, bytes_accessed=4 * 10 ** 7, transcendentals=10 ** 7),
        name="run_layers",
    )(short_lens, long_lens, slopes, tokens, cotangent, w_qkv, w_out, w_gate_up, w_down, gains, biases)


S_SLOTS = 5
OWN_SLOTS = 3
N_CHUNKS = 12
MESH_IDS = pl.DeviceIdType.MESH


def reduce_kernel(
    xa, xm, xn, xh, gq, go, gg, gf, vec,
    o_qkv, o_out, o_gu, o_dn, o_vec,
    t_a, t_m, t_n, t_h, w_q, w_o, w_g, w_f,
    own, ra_relay, ra_fin, sa, own_b, rb_relay, rb_fin, sb, x_send, x_keep, x_recv, c_tmp, c_send, c_keep, c_recv,
    v_acc, v_recv,
    in_sem, peer_send, peer_recv,
    a_send, a_relay_recv, a_fin_recv, a2_send,
    b_send, b_relay_recv, b_fin_recv, b2_send,
    xs_sem, xr_sem, cs_sem, cr_sem, vs_sem, vr_sem,
):
    me = lax.axis_index("dp")
    core = me % 2
    xhi = (me // 2) % 2
    zz = (me // 4) % 4
    yy = me // 16

    def dev(y, z, x, c):
        return ((y * 4 + z) * 2 + x) * 2 + c

    peer_core = dev(yy, zz, xhi, 1 - core)
    peer_x = dev(yy, zz, 1 - xhi, core)
    y_ids = [dev((yy + k) % 4, zz, xhi, core) for k in (1, 2, 3)]
    z_ids = [dev(yy, (zz + k) % 4, xhi, core) for k in (1, 2, 3)]
    peers = [peer_core, peer_x] + y_ids + z_ids

    def remote(src, dst, send, recv, target):
        return pltpu.make_async_remote_copy(
            src_ref=src, dst_ref=dst, send_sem=send, recv_sem=recv,
            device_id={"dp": target}, device_id_type=MESH_IDS,
        )

    half = 512
    other = 1 - core

    def operand_pair(k):
        parts = []
        for m in range(2):
            to = pl.ds(m * 256, 256)
            to_far = pl.ds(half + m * 256, 256)
            src_own, src_far, dst_own, dst_far = (
                (xn.at[m], xn.at[m], t_n.at[:, to], t_n.at[:, to_far]),
                (gg.at[m, :, pl.ds(core * 3072, 3072)], gg.at[m, :, pl.ds(other * 3072, 3072)], w_g.at[to], w_g.at[to_far]),
                (xa.at[m], xa.at[m], t_a.at[:, to], t_a.at[:, to_far]),
                (gq.at[m, :, pl.ds(core * 1152, 1152)], gq.at[m, :, pl.ds(other * 1152, 1152)], w_q.at[to], w_q.at[to_far]),
                (xm.at[m], xm.at[m], t_m.at[:, to], t_m.at[:, to_far]),
                (go.at[m, :, pl.ds(core * 384, 384)], go.at[m, :, pl.ds(other * 384, 384)], w_o.at[to], w_o.at[to_far]),
                (xh.at[m, :, core], xh.at[m, :, other], t_h.at[:, :, to], t_h.at[:, :, to_far]),
                (gf.at[m], gf.at[m], w_f.at[to], w_f.at[to_far]),
            )[k]
            parts.append((
                pltpu.make_async_copy(src_own, dst_own, in_sem.at[k, m]),
                remote(src_far, dst_far, peer_send.at[k, m], peer_recv.at[k, m], peer_core),
            ))
        return parts

    pairs = [operand_pair(k) for k in range(8)]
    local = [pair[0] for both in pairs for pair in both]
    across = [pair[1] for both in pairs for pair in both]
    for copy in local:
        copy.start()
    barrier = pltpu.get_barrier_semaphore()
    for peer in peers:
        pl.semaphore_signal(barrier, inc=1, device_id={"dp": peer}, device_id_type=MESH_IDS)
    pl.semaphore_wait(barrier, len(peers))
    for copy in across:
        copy.start()

    def v_sends(stage):
        targets = ([peer_core], [peer_x], y_ids, z_ids)[stage]
        base = (0, 1, 2, 5)[stage]
        count = len(targets)
        return [
            remote(
                v_acc.at[stage], v_recv.at[base + (count - 1 - k)],
                vs_sem.at[base + k], vr_sem.at[base + (count - 1 - k)], targets[k],
            )
            for k in range(count)
        ]

    def v_start(stage):
        for copy in v_sends(stage):
            copy.start()

    def v_finish(stage):
        base = (0, 1, 2, 5)[stage]
        count = (1, 1, 3, 3)[stage]
        copies = v_sends(stage)
        for copy in copies:
            copy.wait_send()
        total = v_acc[stage]
        for k in range(count):
            copies[count - 1 - k].wait_recv()
        for k in range(count):
            total = total + v_recv[base + k]
        v_acc[stage + 1] = total

    v_acc[0] = vec[...]
    v_start(0)

    def ring(par):
        right = y_ids[0] * (1 - par) + z_ids[0] * par
        left = y_ids[2] * (1 - par) + z_ids[2] * par
        place = yy * (1 - par) + zz * par
        return right, left, place

    def a1_copies(j):
        slot, mine = j % S_SLOTS, j % OWN_SLOTS
        right, left, p = ring(j % 2)
        far, nxt, prv = (p + 2) % 4, (p + 1) % 4, (p + 3) % 4
        return (
            remote(own.at[mine, 0, far], ra_relay.at[slot, 0], a_send.at[slot, 0], a_relay_recv.at[slot, 0], right),
            remote(own.at[mine, 1, far], ra_relay.at[slot, 1], a_send.at[slot, 1], a_relay_recv.at[slot, 1], left),
            remote(own.at[mine, 1, nxt], ra_fin.at[slot, 0, 1], a_send.at[slot, 2], a_fin_recv.at[slot, 0, 1], right),
            remote(own.at[mine, 0, prv], ra_fin.at[slot, 1, 0], a_send.at[slot, 3], a_fin_recv.at[slot, 1, 0], left),
        )

    def a2_copies(j):
        slot = j % S_SLOTS
        right, left, _ = ring(j % 2)
        return (
            remote(sa.at[slot, 0], ra_fin.at[slot, 0, 0], a2_send.at[slot, 0], a_fin_recv.at[slot, 0, 0], right),
            remote(sa.at[slot, 1], ra_fin.at[slot, 1, 1], a2_send.at[slot, 1], a_fin_recv.at[slot, 1, 1], left),
        )

    def b1_copies(j):
        slot = j % S_SLOTS
        right, left, p = ring(1 - j % 2)
        far, nxt, prv = (p + 2) % 4, (p + 1) % 4, (p + 3) % 4
        return (
            remote(own_b.at[slot, 0, far], rb_relay.at[slot, 0], b_send.at[slot, 0], b_relay_recv.at[slot, 0], right),
            remote(own_b.at[slot, 1, far], rb_relay.at[slot, 1], b_send.at[slot, 1], b_relay_recv.at[slot, 1], left),
            remote(own_b.at[slot, 1, nxt], rb_fin.at[slot, 0, 1], b_send.at[slot, 2], b_fin_recv.at[slot, 0, 1], right),
            remote(own_b.at[slot, 0, prv], rb_fin.at[slot, 1, 0], b_send.at[slot, 3], b_fin_recv.at[slot, 1, 0], left),
        )

    def b2_copies(j):
        slot = j % S_SLOTS
        right, left, _ = ring(1 - j % 2)
        return (
            remote(sb.at[slot, 0], rb_fin.at[slot, 0, 0], b2_send.at[slot, 0], b_fin_recv.at[slot, 0, 0], right),
            remote(sb.at[slot, 1], rb_fin.at[slot, 1, 1], b2_send.at[slot, 1], b_fin_recv.at[slot, 1, 1], left),
        )

    def x_copy(j):
        slot = j % S_SLOTS
        return remote(x_send.at[slot], x_recv.at[slot], xs_sem.at[slot], xr_sem.at[slot], peer_x)

    def c_copy(j):
        slot = j % S_SLOTS
        return remote(c_send.at[slot], c_recv.at[slot], cs_sem.at[slot], cr_sem.at[slot], peer_core)

    def wait_operands(*which):
        for k in which:
            for pair in pairs[k]:
                pair[0].wait()
                pair[1].wait()

    def store_rows(j, halves):
        mine = j % OWN_SLOTS
        par = j % 2
        for y in range(4):
            for z in range(4):
                first = y * (1 - par) + z * par
                second = z * (1 - par) + y * par
                for h in range(2):
                    own[mine, h, first, second] = halves[h][y * 4 + z]

    def product(lhs, rhs):
        return jnp.dot(lhs, rhs, preferred_element_type=jnp.float32).astype(jnp.bfloat16)

    def split_halves(result):
        return [result[:, h * 256:(h + 1) * 256].reshape(16, 48, 256) for h in range(2)]

    def compute(j):
        @pl.when(j < 6)
        def _():
            @pl.when(j == 0)
            def _():
                wait_operands(0, 1)
            rhs = w_g[:, pl.ds(pl.multiple_of(j * 512, 512), 512)]
            store_rows(j, split_halves(product(t_n[...], rhs)))

        @pl.when((j >= 6) & (j < 8))
        def _():
            @pl.when(j == 6)
            def _():
                wait_operands(2, 3)
            rhs = w_q[:, pl.ds(pl.multiple_of((j - 6) * 512, 512), 512)]
            store_rows(j, split_halves(product(t_a[...], rhs)))

        @pl.when(j == 8)
        def _():
            wait_operands(4, 5)
            one = product(t_a[...], w_q[:, pl.ds(1024, 128)])
            two = product(t_m[...], w_o[...])
            store_rows(j, split_halves(jnp.concatenate([one, two], axis=1)))

        @pl.when(j >= 9)
        def _():
            @pl.when(j == 9)
            def _():
                wait_operands(6, 7)
            rhs = w_f[:, pl.ds(pl.multiple_of((j - 9) * 256, 256), 256)]
            result = product(t_h[...].reshape(1536, 1024), rhs).reshape(16, 2, 48, 256)
            store_rows(j, [result[:, 0], result[:, 1]])

    def step(i, carry):
        @pl.when(i < N_CHUNKS)
        def _():
            compute(i)
            for copy in a1_copies(i):
                copy.start()

        j1 = i - 1

        @pl.when((j1 >= 0) & (j1 < N_CHUNKS))
        def _():
            slot, mine = j1 % S_SLOTS, j1 % OWN_SLOTS
            _, _, p = ring(j1 % 2)
            first = a1_copies(j1)
            second = a2_copies(j1)
            first[0].wait_recv()
            sa[slot, 0] = (f32(own[mine, 0, (p + 1) % 4]) + f32(ra_relay[slot, 0])).astype(jnp.bfloat16)
            second[0].start()
            first[1].wait_recv()
            sa[slot, 1] = (f32(own[mine, 1, (p + 3) % 4]) + f32(ra_relay[slot, 1])).astype(jnp.bfloat16)
            second[1].start()

        j2 = i - 2

        @pl.when((j2 >= 0) & (j2 < N_CHUNKS))
        def _():
            slot, mine = j2 % S_SLOTS, j2 % OWN_SLOTS
            _, _, p = ring(j2 % 2)
            first = a1_copies(j2)
            second = a2_copies(j2)
            for copy in first + second:
                copy.wait_send()
            first[2].wait_recv()
            first[3].wait_recv()
            second[0].wait_recv()
            second[1].wait_recv()
            for h in range(2):
                own_b[slot, h] = (
                    f32(own[mine, h, p]) + f32(ra_fin[slot, 0, h]) + f32(ra_fin[slot, 1, h])
                ).astype(jnp.bfloat16)
            for copy in b1_copies(j2):
                copy.start()

        j3 = i - 3

        @pl.when((j3 >= 0) & (j3 < N_CHUNKS))
        def _():
            slot = j3 % S_SLOTS
            _, _, p = ring(1 - j3 % 2)
            first = b1_copies(j3)
            second = b2_copies(j3)
            first[0].wait_recv()
            sb[slot, 0] = (f32(own_b[slot, 0, (p + 1) % 4]) + f32(rb_relay[slot, 0])).astype(jnp.bfloat16)
            second[0].start()
            first[1].wait_recv()
            sb[slot, 1] = (f32(own_b[slot, 1, (p + 3) % 4]) + f32(rb_relay[slot, 1])).astype(jnp.bfloat16)
            second[1].start()

        j4 = i - 4

        @pl.when((j4 >= 0) & (j4 < N_CHUNKS))
        def _():
            slot = j4 % S_SLOTS
            _, _, p = ring(1 - j4 % 2)
            first = b1_copies(j4)
            second = b2_copies(j4)
            for copy in first + second:
                copy.wait_send()
            first[2].wait_recv()
            first[3].wait_recv()
            second[0].wait_recv()
            second[1].wait_recv()
            total = [
                f32(own_b[slot, h, p]) + f32(rb_fin[slot, 0, h]) + f32(rb_fin[slot, 1, h])
                for h in range(2)
            ]
            low = xhi == 0

            @pl.when(j4 < 9)
            def _():
                for h in range(2):
                    x_send[slot, h] = jnp.where(low, total[h][24:], total[h][:24])
                    x_keep[slot, h] = jnp.where(low, total[h][:24], total[h][24:])

            @pl.when(j4 >= 9)
            def _():
                sent = jnp.where(low, total[1], total[0])
                kept = jnp.where(low, total[0], total[1])
                for h in range(2):
                    x_send[slot, h] = sent[h * 24:(h + 1) * 24]
                    x_keep[slot, h] = kept[h * 24:(h + 1) * 24]

            x_copy(j4).start()

        j5 = i - 5

        @pl.when((j5 >= 0) & (j5 < N_CHUNKS))
        def _():
            slot = j5 % S_SLOTS
            x_copy(j5).wait()

            @pl.when(j5 < 9)
            def _():
                for h in range(2):
                    c_tmp[h] = x_keep[slot, h] + x_recv[slot, h]
                low = core == 0
                for h in range(2):
                    upper, lower = c_tmp[h, 0:12], c_tmp[h, 12:24]
                    c_send[slot, h, 0:12] = jnp.where(low, lower, upper)
                    c_keep[slot, h, 0:12] = jnp.where(low, upper, lower)
                c_copy(j5).start()

            @pl.when(j5 >= 9)
            def _():
                column = pl.ds(pl.multiple_of((j5 - 9) * 256, 256), 256)
                for h in range(2):
                    o_dn[h * 24:(h + 1) * 24, column] = x_keep[slot, h] + x_recv[slot, h]

        j6 = i - 6

        @pl.when((j6 >= 0) & (j6 < 9))
        def _():
            slot = j6 % S_SLOTS
            c_copy(j6).wait()
            for source, who in ((c_keep, core), (c_recv, 1 - core)):
                @pl.when(j6 < 6)
                def _():
                    for h in range(2):
                        column = pl.multiple_of(who * 3072 + j6 * 512 + h * 256, 256)
                        o_gu[:, pl.ds(column, 256)] = source[slot, h, 0:12]

                @pl.when((j6 >= 6) & (j6 < 8))
                def _():
                    for h in range(2):
                        column = pl.multiple_of(who * 1152 + (j6 - 6) * 512 + h * 256, 128)
                        o_qkv[:, pl.ds(column, 256)] = source[slot, h, 0:12]

                @pl.when(j6 == 8)
                def _():
                    o_qkv[:, pl.ds(pl.multiple_of(who * 1152 + 1024, 128), 128)] = source[slot, 0, 0:12, 0:128]
                    o_out[:, pl.ds(pl.multiple_of(who * 384, 128), 128)] = source[slot, 0, 0:12, 128:256]
                    o_out[:, pl.ds(pl.multiple_of(who * 384 + 128, 128), 256)] = source[slot, 1, 0:12]

        for stage in range(4):
            @pl.when(i == 2 * stage + 2)
            def _():
                v_finish(stage)
                if stage < 3:
                    v_start(stage + 1)

        return carry

    lax.fori_loop(0, N_CHUNKS + 6, step, 0)
    o_vec[...] = v_acc[4]


def reduce_weights(xa, xm, xn, xh, gq, go, gg, gf, vec):
    low, wide = jnp.bfloat16, jnp.float32
    hbm = pl.BlockSpec(memory_space=pl.ANY)
    vmem = pl.BlockSpec(memory_space=pltpu.VMEM)
    dma = pltpu.SemaphoreType.DMA
    s = S_SLOTS
    return pl.pallas_call(
        reduce_kernel,
        out_shape=[
            jax.ShapeDtypeStruct((12, 2304), wide),
            jax.ShapeDtypeStruct((12, 768), wide),
            jax.ShapeDtypeStruct((12, 6144), wide),
            jax.ShapeDtypeStruct((48, 768), wide),
            jax.ShapeDtypeStruct((8, 768), wide),
        ],
        in_specs=[hbm] * 8 + [vmem],
        out_specs=[vmem] * 5,
        scratch_shapes=[
            pltpu.VMEM((768, 1024), low),
            pltpu.VMEM((768, 1024), low),
            pltpu.VMEM((768, 1024), low),
            pltpu.VMEM((32, 48, 1024), low),
            pltpu.VMEM((1024, 1152), low),
            pltpu.VMEM((1024, 384), low),
            pltpu.VMEM((1024, 3072), low),
            pltpu.VMEM((1024, 768), low),
            pltpu.VMEM((OWN_SLOTS, 2, 4, 4, 48, 256), low),
            pltpu.VMEM((s, 2, 4, 48, 256), low),
            pltpu.VMEM((s, 2, 2, 4, 48, 256), low),
            pltpu.VMEM((s, 2, 4, 48, 256), low),
            pltpu.VMEM((s, 2, 4, 48, 256), low),
            pltpu.VMEM((s, 2, 48, 256), low),
            pltpu.VMEM((s, 2, 2, 48, 256), low),
            pltpu.VMEM((s, 2, 48, 256), low),
            pltpu.VMEM((s, 2, 24, 256), wide),
            pltpu.VMEM((s, 2, 24, 256), wide),
            pltpu.VMEM((s, 2, 24, 256), wide),
            pltpu.VMEM((2, 24, 256), wide),
            pltpu.VMEM((s, 2, 16, 256), wide),
            pltpu.VMEM((s, 2, 16, 256), wide),
            pltpu.VMEM((s, 2, 16, 256), wide),
            pltpu.VMEM((5, 8, 768), wide),
            pltpu.VMEM((8, 8, 768), wide),
            dma((8, 2)), dma((8, 2)), dma((8, 2)),
            dma((s, 4)), dma((s, 2)), dma((s, 2, 2)), dma((s, 2)),
            dma((s, 4)), dma((s, 2)), dma((s, 2, 2)), dma((s, 2)),
            dma((s,)), dma((s,)), dma((s,)), dma((s,)),
            dma((8,)), dma((8,)),
        ],
        compiler_params=pltpu.CompilerParams(
            collective_id=0, has_side_effects=True, vmem_limit_bytes=56 * 1024 * 1024
        ),
        cost_estimate=pl.CostEstimate(flops=10 ** 10, bytes_accessed=2 * 10 ** 7, transcendentals=0),
        name="reduce_weights",
    )(xa, xm, xn, xh.reshape(2, 32, 2, 48, 256), gq, go, gg, gf, vec)


def on_device(
    tokens, cotangent, short_lens, long_lens, w_qkv, w_out, w_gate_up, w_down, gains, biases
):
    boundary, x_a, x_m, x_n, x_h, g_q, g_o, g_g, g_f, vec = run_layers(
        short_lens, long_lens, tokens, cotangent, w_qkv[0], w_out[0], w_gate_up[0], w_down[0], gains[0], biases[0]
    )
    g_qkv, g_out, g_gu, g_dn, g_vec = reduce_weights(x_a, x_m, x_n, x_h, g_q, g_o, g_g, g_f, vec)
    mine = lax.dynamic_slice_in_dim(g_vec, lax.axis_index("dp") * 12, 12, axis=1)
    return (boundary[None], g_qkv[None], g_out[None], g_gu[None], g_dn[None], mine[None, :2], mine[None, 2:])


def solution(mesh):
    placed = (
        P(None, "dp", None),
        P(None, "dp", None),
        P("dp"),
        P("dp"),
        P("section", None, None),
        P("section", None, None),
        P("section", None, None),
        P("section", None, None),
        P("section", None, None),
        P("section", None, None),
    )
    return jax.shard_map(
        on_device,
        mesh=mesh,
        in_specs=placed,
        out_specs=(
            P("section", None, "dp", None),
            P("section", "dp", None),
            P("section", "dp", None),
            P("section", "dp", None),
            P("section", "dp", None),
            P("section", None, "dp"),
            P("section", None, "dp"),
        ),
        check_vma=False,
    )
```

```python
import jax
import jax.numpy as jnp
from jax import lax
from jax.experimental import pallas as pl
from jax.experimental.pallas import tpu as pltpu
from jax.sharding import PartitionSpec as P

D = 768
HEADS = 12
HEAD = 64
FF = 3072


epsilon = 1e-05
masked_value = -1000000000.0


ROWS_DEV = 256
BLOCK = 512
BAND = 32


def dot_nn(lhs, rhs):
    return jnp.dot(lhs, rhs, preferred_element_type=jnp.float32)


def dot_nt(lhs, rhs):
    return lax.dot_general(lhs, rhs, (((1,), (1,)), ((), ())), preferred_element_type=jnp.float32)


def dot_tn(lhs, rhs):
    return lax.dot_general(lhs, rhs, (((0,), (0,)), ((), ())), preferred_element_type=jnp.float32)


def f32(value):
    return value.astype(jnp.float32)


def bf16(value):
    return value.astype(jnp.bfloat16)


def fold_rows(value):
    return jnp.sum(value.reshape(value.shape[0] // 8, 8, value.shape[1]), 0)


def gelu_terms(gate):
    cdf = 0.5 * (1.0 + lax.erf(gate * 0.7071067811865476))
    density = jnp.exp(-0.5 * gate * gate) * 0.3989422804014327
    return gate * cdf, cdf + gate * density


def layers_kernel(
    short_lens, long_lens, tokens, cotangent, w_qkv, w_out, w_gate_up, w_down, gains, biases,
    boundary, o_at, o_mt, o_nt, o_ht, o_gq, o_go, o_gg, o_gf, o_vec,
    wq, wo, wg, wd, x_s, g_s, qkv_s, p_s, mixed_s, nl_s, low_s, n1_s, n2_s, r1_s, r2_s, gu_s, ht_s,
    gf_s, ga_s, send_s, out_s, acc_s, f_s, gate_s, up_s, dist_s, mask_s, vec_s,
    w_sem, x_sem, g_sem, out_sem, spill_sem, f_send, f_recv, b_send, b_recv,
):
    sec = lax.axis_index("section")
    first = sec == 0
    second = sec == 1
    w_copies = [
        pltpu.make_async_copy(w_qkv, wq, w_sem.at[0]),
        pltpu.make_async_copy(w_out, wo, w_sem.at[1]),
        pltpu.make_async_copy(w_gate_up, wg, w_sem.at[2]),
        pltpu.make_async_copy(w_down, wd, w_sem.at[3]),
    ]

    def token_copy(m):
        return pltpu.make_async_copy(tokens.at[m], x_s.at[m], x_sem.at[m])

    def cot_copy(m):
        return pltpu.make_async_copy(cotangent.at[m], g_s.at[m], g_sem.at[m])

    def across(src, dst, send, recv):
        return pltpu.make_async_remote_copy(
            src_ref=src, dst_ref=dst, send_sem=send, recv_sem=recv,
            device_id={"section": 1 - sec}, device_id_type=pl.DeviceIdType.MESH,
        )

    def hand_on(m):
        return across(send_s.at[m], x_s.at[m], f_send.at[m], f_recv.at[m])

    def hand_back(m):
        return across(send_s.at[m], g_s.at[m], b_send.at[m], b_recv.at[m])

    @pl.when(first)
    def _():
        token_copy(0).start()

    w_copies[0].start()
    w_copies[1].start()

    @pl.when(first)
    def _():
        token_copy(1).start()

    w_copies[2].start()
    w_copies[3].start()

    @pl.when(second)
    def _():
        cot_copy(0).start()
        cot_copy(1).start()

    barrier = pltpu.get_barrier_semaphore()
    pl.semaphore_signal(
        barrier, inc=1, device_id={"section": 1 - sec}, device_id_type=pl.DeviceIdType.MESH
    )
    pl.semaphore_wait(barrier, 1)

    vec_s[...] = jnp.zeros_like(vec_s)
    rows_j = lax.broadcasted_iota(jnp.int32, (256, 256), 0)
    cols_i = lax.broadcasted_iota(jnp.int32, (256, 256), 1)
    dist_s[...] = jnp.abs(rows_j - cols_i).astype(jnp.float32)
    length_a, length_b, length_long = short_lens[0], short_lens[1], long_lens[0]
    for m in range(2):
        if m == 0:
            limit = jnp.where(rows_j < 128, length_a, length_b + 128)
            apart = jnp.where((rows_j >> 7) == (cols_i >> 7), 0, 1024)
            ok = rows_j + apart < limit
        else:
            ok = rows_j < length_long
        mask_s[m] = jnp.where(ok, 1.0, 0.0)

    def band(k):
        return pl.ds(pl.multiple_of(k * BAND, BAND), BAND)

    def normalise(value):
        average = jnp.mean(value, -1, keepdims=True)
        centred = value - average
        inverse = lax.rsqrt(jnp.mean(centred * centred, -1, keepdims=True) + epsilon)
        return centred * inverse, inverse

    def spill(m):
        return [
            pltpu.make_async_copy(x_s.at[m], o_at.at[m], spill_sem.at[m, 0]),
            pltpu.make_async_copy(mixed_s.at[m], o_mt.at[m], spill_sem.at[m, 1]),
            pltpu.make_async_copy(nl_s.at[m], o_nt.at[m], spill_sem.at[m, 2]),
            pltpu.make_async_copy(ht_s.at[m], o_ht.at[m], spill_sem.at[m, 3]),
        ]

    def spill_back(m):
        return [
            pltpu.make_async_copy(qkv_s.at[m], o_gq.at[m], spill_sem.at[m, 4]),
            pltpu.make_async_copy(ga_s.at[m], o_go.at[m], spill_sem.at[m, 5]),
            pltpu.make_async_copy(gu_s.at[m], o_gg.at[m], spill_sem.at[m, 6]),
            pltpu.make_async_copy(gf_s.at[m], o_gf.at[m], spill_sem.at[m, 7]),
        ]

    def out_copy(m):
        return pltpu.make_async_copy(out_s.at[m], boundary.at[m], out_sem.at[m])

    lanes = lax.broadcasted_iota(jnp.int32, (256, 128), 1)

    def forward(m, carry):
        @pl.when(first)
        def _():
            token_copy(m).wait()

        @pl.when(second)
        def _():
            hand_on(m).wait_recv()

        @pl.when(m == 0)
        def _():
            w_copies[0].wait()

        x = x_s[m]
        query = dot_nn(x, wq[:, 0:768]) + biases[0]
        qkv_s[m, :, 0:768] = bf16(f32(bf16(query)) * 0.125)
        qkv_s[m, :, 768:1536] = bf16(dot_nn(x, wq[:, 768:1536]))
        qkv_s[m, :, 1536:2304] = bf16(dot_nn(x, wq[:, 1536:2304]) + biases[1])

        def heads(hp, carry):
            lane0 = hp * 128
            q2 = qkv_s[m, :, pl.ds(lane0, 128)]
            k2 = qkv_s[m, :, pl.ds(lane0 + 768, 128)]
            v2 = qkv_s[m, :, pl.ds(lane0 + 1536, 128)]
            outs = []
            for e in range(2):
                keep = (lanes < 64) if e == 0 else (lanes >= 64)
                qm = jnp.where(keep, q2, jnp.zeros_like(q2))
                scores = dot_nt(k2, qm) - 2.0 ** (-8.0 * (2 * hp + e + 1) / HEADS) * dist_s[...]
                scores = jnp.where(mask_s[m] > 0.5, scores, masked_value)
                expo = jnp.exp(scores - jnp.max(scores, 0, keepdims=True))
                total = jnp.sum(expo, 0, keepdims=True)
                probs = bf16(expo * (1.0 / total))
                p_s[m, 2 * hp + e] = probs
                outs.append(dot_tn(probs, v2))
            mixed_s[m, :, pl.ds(lane0, 128)] = bf16(jnp.where(lanes < 64, outs[0], outs[1]))
            return carry

        for index in range(6):
            heads(index, 0)

        @pl.when(m == 0)
        def _():
            w_copies[1].wait()

        mixed = mixed_s[m]
        acc_s[...] = dot_nn(mixed, wo[...])

        def norm_one(k, carry):
            r = band(k)
            value = f32(x_s[m, r]) + (acc_s[r] + biases[2])
            unit, inverse = normalise(value)
            normed = unit * gains[0:1] + biases[3]
            n1_s[m, r] = bf16(unit)
            r1_s[m, r] = inverse
            f_s[r] = normed
            nl_s[m, r] = bf16(normed)
            return carry

        lax.fori_loop(0, 8, norm_one, 0, unroll=True)

        @pl.when(m == 0)
        def _():
            w_copies[2].wait()
            w_copies[3].wait()

        acc_s[...] = jnp.zeros_like(acc_s)

        def ffn(jb, carry):
            c0 = jb * BLOCK
            low = nl_s[m]
            gate_s[...] = dot_nn(low, wg[:, pl.ds(c0, BLOCK)])
            up_s[...] = dot_nn(low, wg[:, pl.ds(c0 + FF, BLOCK)])
            for k in range(8):
                r = pl.ds(k * BAND, BAND)
                gate, up = gate_s[r], up_s[r]
                act, slope = gelu_terms(gate)
                gu_s[m, r, pl.ds(c0, BLOCK)] = bf16(up * slope)
                gu_s[m, r, pl.ds(c0 + FF, BLOCK)] = bf16(act)
                gate_s[r] = act * up
            hid = bf16(gate_s[...])
            ht_s[m, pl.ds(c0, BLOCK)] = hid.T
            acc_s[...] += dot_nn(hid, wd[pl.ds(c0, BLOCK)])
            return carry

        for index in range(6):
            ffn(index, 0)

        def norm_two(k, carry):
            r = band(k)
            value = f_s[r] + (acc_s[r] + biases[4])
            unit, inverse = normalise(value)
            n2_s[m, r] = bf16(unit)
            r2_s[m, r] = inverse
            result = unit * gains[1:2] + biases[5]
            out_s[m, r] = result
            send_s[m, r] = bf16(result)
            return carry

        lax.fori_loop(0, 8, norm_two, 0, unroll=True)

        @pl.when(first)
        def _():
            hand_on(m).start()

        @pl.when(second)
        def _():
            out_copy(m).start()

        for copy in spill(m):
            copy.start()
        return carry

    lax.fori_loop(0, 2, forward, 0)

    def norm_back(grad, unit, inverse, gain):
        scaled = grad * gain
        mean_one = jnp.mean(scaled, -1, keepdims=True)
        mean_two = jnp.mean(scaled * unit, -1, keepdims=True)
        return inverse * (scaled - mean_one - unit * mean_two)

    def backward(m, carry):
        @pl.when(first)
        def _():
            hand_on(m).wait_send()
            hand_back(m).wait_recv()

        @pl.when(second)
        def _():
            cot_copy(m).wait()
            out_copy(m).wait()

        def back_two(k, carry):
            r = band(k)
            row = lax.broadcasted_iota(jnp.int32, (BAND, 1), 0) + k * BAND
            limit = jnp.where(m == 0, jnp.where(row < 128, length_a, length_b + 128), length_long)
            live = jnp.where((row < limit) | first, 1.0, 0.0)
            grad = f32(g_s[m, r]) * live
            unit = f32(n2_s[m, r])
            vec_s[1] += fold_rows(grad * unit)
            vec_s[7] += fold_rows(grad)
            grad_in = norm_back(grad, unit, r2_s[m, r], gains[1:2])
            f_s[r] = grad_in
            low = bf16(grad_in)
            gf_s[m, r] = low
            vec_s[6] += fold_rows(f32(low))
            return carry

        lax.fori_loop(0, 8, back_two, 0, unroll=True)
        acc_s[...] = jnp.zeros_like(acc_s)

        def ffn_back(jb, carry):
            c0 = jb * BLOCK
            gate_s[...] = dot_nt(gf_s[m], wd[pl.ds(c0, BLOCK)])
            for k in range(8):
                r = pl.ds(k * BAND, BAND)
                hid = gate_s[r]
                gu_s[m, r, pl.ds(c0, BLOCK)] = bf16(hid * f32(gu_s[m, r, pl.ds(c0, BLOCK)]))
                gu_s[m, r, pl.ds(c0 + FF, BLOCK)] = bf16(hid * f32(gu_s[m, r, pl.ds(c0 + FF, BLOCK)]))
            acc_s[...] += dot_nt(gu_s[m, :, pl.ds(c0, BLOCK)], wg[:, pl.ds(c0, BLOCK)])
            acc_s[...] += dot_nt(gu_s[m, :, pl.ds(c0 + FF, BLOCK)], wg[:, pl.ds(c0 + FF, BLOCK)])
            return carry

        for index in range(6):
            ffn_back(index, 0)

        def back_one(k, carry):
            r = band(k)
            grad = acc_s[r] + f_s[r]
            unit = f32(n1_s[m, r])
            vec_s[0] += fold_rows(grad * unit)
            vec_s[5] += fold_rows(grad)
            grad_in = norm_back(grad, unit, r1_s[m, r], gains[0:1])
            f_s[r] = grad_in
            low = bf16(grad_in)
            ga_s[m, r] = low
            vec_s[4] += fold_rows(f32(low))
            return carry

        lax.fori_loop(0, 8, back_one, 0, unroll=True)
        low_s[...] = bf16(dot_nt(ga_s[m], wo[...]))

        def heads_back(hp, carry):
            lane0 = hp * 128
            q2 = qkv_s[m, :, pl.ds(lane0, 128)]
            k2 = qkv_s[m, :, pl.ds(lane0 + 768, 128)]
            v2 = qkv_s[m, :, pl.ds(lane0 + 1536, 128)]
            do2 = low_s[:, pl.ds(lane0, 128)]
            dq, dk, dv = [], [], []
            for e in range(2):
                keep = (lanes < 64) if e == 0 else (lanes >= 64)
                vm = jnp.where(keep, v2, jnp.zeros_like(v2))
                probs = p_s[m, 2 * hp + e]
                grad_probs = dot_nt(vm, do2)
                weighted = f32(probs) * grad_probs
                total = jnp.sum(weighted, 0, keepdims=True)
                grad_scores = bf16(weighted - f32(probs) * total)
                dv.append(dot_nn(probs, do2))
                dk.append(dot_nn(grad_scores, q2))
                dq.append(dot_tn(grad_scores, k2))
            grad_q = bf16(jnp.where(lanes < 64, dq[0], dq[1]) * 0.125)
            grad_k = bf16(jnp.where(lanes < 64, dk[0], dk[1]))
            grad_v = bf16(jnp.where(lanes < 64, dv[0], dv[1]))
            vec_s[2, :, pl.ds(lane0, 128)] += fold_rows(f32(grad_q))
            vec_s[3, :, pl.ds(lane0, 128)] += fold_rows(f32(grad_v))
            qkv_s[m, :, pl.ds(lane0, 128)] = grad_q
            qkv_s[m, :, pl.ds(lane0 + 768, 128)] = grad_k
            qkv_s[m, :, pl.ds(lane0 + 1536, 128)] = grad_v
            return carry

        for index in range(6):
            heads_back(index, 0)
        grad_a = dot_nt(qkv_s[m], wq[...]) + f_s[...]

        @pl.when(second)
        def _():
            send_s[m] = bf16(grad_a)
            hand_back(m).start()

        @pl.when(first)
        def _():
            out_s[m] = grad_a
            out_copy(m).start()

        for copy in spill_back(m):
            copy.start()
        return carry

    lax.fori_loop(0, 2, backward, 0)
    for k in range(8):
        o_vec[k:k + 1] = jnp.sum(vec_s[k], 0, keepdims=True)

    for m in range(2):
        for copy in spill(m) + spill_back(m):
            copy.wait()

        @pl.when(second)
        def _():
            hand_back(m).wait_send()

        @pl.when(first)
        def _():
            out_copy(m).wait()


def run_layers(short_lens, long_lens, tokens, cotangent, w_qkv, w_out, w_gate_up, w_down, gains, biases):
    low, wide = jnp.bfloat16, jnp.float32
    hbm = pl.BlockSpec(memory_space=pl.ANY)
    vmem = pl.BlockSpec(memory_space=pltpu.VMEM)
    smem = pl.BlockSpec(memory_space=pltpu.SMEM)
    dma = pltpu.SemaphoreType.DMA

    def of(shape, dtype):
        return pltpu.VMEM(shape, dtype)

    return pl.pallas_call(
        layers_kernel,
        out_shape=[
            jax.ShapeDtypeStruct((2, 256, 768), wide),
            jax.ShapeDtypeStruct((2, 256, 768), low),
            jax.ShapeDtypeStruct((2, 256, 768), low),
            jax.ShapeDtypeStruct((2, 256, 768), low),
            jax.ShapeDtypeStruct((2, 3072, 256), low),
            jax.ShapeDtypeStruct((2, 256, 2304), low),
            jax.ShapeDtypeStruct((2, 256, 768), low),
            jax.ShapeDtypeStruct((2, 256, 6144), low),
            jax.ShapeDtypeStruct((2, 256, 768), low),
            jax.ShapeDtypeStruct((8, 768), wide),
        ],
        in_specs=[smem] * 2 + [hbm] * 6 + [vmem] * 2,
        out_specs=[hbm] * 9 + [vmem],
        scratch_shapes=[
            of((768, 2304), low), of((768, 768), low), of((768, 6144), low), of((3072, 768), low),
            of((2, 256, 768), low), of((2, 256, 768), low), of((2, 256, 2304), low), of((2, 12, 256, 256), low),
            of((2, 256, 768), low), of((2, 256, 768), low), of((256, 768), low), of((2, 256, 768), low), of((2, 256, 768), low),
            of((2, 256, 1), wide), of((2, 256, 1), wide), of((2, 256, 6144), low),
            of((2, 3072, 256), low),
            of((2, 256, 768), low), of((2, 256, 768), low), of((2, 256, 768), low), of((2, 256, 768), wide),
            of((256, 768), wide), of((256, 768), wide), of((256, 512), wide), of((256, 512), wide),
            of((256, 256), wide), of((2, 256, 256), wide), of((8, 8, 768), wide),
            dma((4,)), dma((2,)), dma((2,)), dma((2,)), dma((2, 8)), dma((2,)), dma((2,)), dma((2,)), dma((2,)),
        ],
        compiler_params=pltpu.CompilerParams(
            collective_id=1, has_side_effects=True, vmem_limit_bytes=60 * 1024 * 1024
        ),
        cost_estimate=pl.CostEstimate(flops=2 * 10 ** 10, bytes_accessed=4 * 10 ** 7, transcendentals=10 ** 7),
        name="run_layers",
    )(short_lens, long_lens, tokens, cotangent, w_qkv, w_out, w_gate_up, w_down, gains, biases)


S_SLOTS = 5
OWN_SLOTS = 3
N_CHUNKS = 12
MESH_IDS = pl.DeviceIdType.MESH


def reduce_kernel(
    xa, xm, xn, xh, gq, go, gg, gf, vec,
    o_qkv, o_out, o_gu, o_dn, o_vec,
    t_a, t_m, t_n, t_h, w_q, w_o, w_g, w_f,
    own, ra_relay, ra_fin, sa, own_b, rb_relay, rb_fin, sb, x_send, x_keep, x_recv, c_tmp, c_send, c_keep, c_recv,
    v_acc, v_recv,
    in_sem, peer_send, peer_recv,
    a_send, a_relay_recv, a_fin_recv, a2_send,
    b_send, b_relay_recv, b_fin_recv, b2_send,
    xs_sem, xr_sem, cs_sem, cr_sem, vs_sem, vr_sem,
):
    me = lax.axis_index("dp")
    core = me % 2
    xhi = (me // 2) % 2
    zz = (me // 4) % 4
    yy = me // 16

    def dev(y, z, x, c):
        return ((y * 4 + z) * 2 + x) * 2 + c

    peer_core = dev(yy, zz, xhi, 1 - core)
    peer_x = dev(yy, zz, 1 - xhi, core)
    y_ids = [dev((yy + k) % 4, zz, xhi, core) for k in (1, 2, 3)]
    z_ids = [dev(yy, (zz + k) % 4, xhi, core) for k in (1, 2, 3)]
    peers = [peer_core, peer_x] + y_ids + z_ids

    def remote(src, dst, send, recv, target):
        return pltpu.make_async_remote_copy(
            src_ref=src, dst_ref=dst, send_sem=send, recv_sem=recv,
            device_id={"dp": target}, device_id_type=MESH_IDS,
        )

    half = 512
    other = 1 - core

    def operand_pair(k):
        parts = []
        for m in range(2):
            to = pl.ds(m * 256, 256)
            to_far = pl.ds(half + m * 256, 256)
            src_own, src_far, dst_own, dst_far = (
                (xn.at[m], xn.at[m], t_n.at[to], t_n.at[to_far]),
                (gg.at[m, :, pl.ds(core * 3072, 3072)], gg.at[m, :, pl.ds(other * 3072, 3072)], w_g.at[to], w_g.at[to_far]),
                (xa.at[m], xa.at[m], t_a.at[to], t_a.at[to_far]),
                (gq.at[m, :, pl.ds(core * 1152, 1152)], gq.at[m, :, pl.ds(other * 1152, 1152)], w_q.at[to], w_q.at[to_far]),
                (xm.at[m], xm.at[m], t_m.at[to], t_m.at[to_far]),
                (go.at[m, :, pl.ds(core * 384, 384)], go.at[m, :, pl.ds(other * 384, 384)], w_o.at[to], w_o.at[to_far]),
                (xh.at[m, :, core], xh.at[m, :, other], t_h.at[:, :, to], t_h.at[:, :, to_far]),
                (gf.at[m], gf.at[m], w_f.at[to], w_f.at[to_far]),
            )[k]
            parts.append((
                pltpu.make_async_copy(src_own, dst_own, in_sem.at[k, m]),
                remote(src_far, dst_far, peer_send.at[k, m], peer_recv.at[k, m], peer_core),
            ))
        return parts

    pairs = [operand_pair(k) for k in range(8)]
    local = [pair[0] for both in pairs for pair in both]
    across = [pair[1] for both in pairs for pair in both]
    for copy in local:
        copy.start()
    barrier = pltpu.get_barrier_semaphore()
    for peer in peers:
        pl.semaphore_signal(barrier, inc=1, device_id={"dp": peer}, device_id_type=MESH_IDS)
    pl.semaphore_wait(barrier, len(peers))
    for copy in across:
        copy.start()

    def v_sends(stage):
        targets = ([peer_core], [peer_x], y_ids, z_ids)[stage]
        base = (0, 1, 2, 5)[stage]
        count = len(targets)
        return [
            remote(
                v_acc.at[stage], v_recv.at[base + (count - 1 - k)],
                vs_sem.at[base + k], vr_sem.at[base + (count - 1 - k)], targets[k],
            )
            for k in range(count)
        ]

    def v_start(stage):
        for copy in v_sends(stage):
            copy.start()

    def v_finish(stage):
        base = (0, 1, 2, 5)[stage]
        count = (1, 1, 3, 3)[stage]
        copies = v_sends(stage)
        for copy in copies:
            copy.wait_send()
        total = v_acc[stage]
        for k in range(count):
            copies[count - 1 - k].wait_recv()
        for k in range(count):
            total = total + v_recv[base + k]
        v_acc[stage + 1] = total

    v_acc[0] = vec[...]
    v_start(0)

    def ring(par):
        right = y_ids[0] * (1 - par) + z_ids[0] * par
        left = y_ids[2] * (1 - par) + z_ids[2] * par
        place = yy * (1 - par) + zz * par
        return right, left, place

    def a1_copies(j):
        slot, mine = j % S_SLOTS, j % OWN_SLOTS
        right, left, p = ring(j % 2)
        far, nxt, prv = (p + 2) % 4, (p + 1) % 4, (p + 3) % 4
        return (
            remote(own.at[mine, 0, far], ra_relay.at[slot, 0], a_send.at[slot, 0], a_relay_recv.at[slot, 0], right),
            remote(own.at[mine, 1, far], ra_relay.at[slot, 1], a_send.at[slot, 1], a_relay_recv.at[slot, 1], left),
            remote(own.at[mine, 1, nxt], ra_fin.at[slot, 0, 1], a_send.at[slot, 2], a_fin_recv.at[slot, 0, 1], right),
            remote(own.at[mine, 0, prv], ra_fin.at[slot, 1, 0], a_send.at[slot, 3], a_fin_recv.at[slot, 1, 0], left),
        )

    def a2_copies(j):
        slot = j % S_SLOTS
        right, left, _ = ring(j % 2)
        return (
            remote(sa.at[slot, 0], ra_fin.at[slot, 0, 0], a2_send.at[slot, 0], a_fin_recv.at[slot, 0, 0], right),
            remote(sa.at[slot, 1], ra_fin.at[slot, 1, 1], a2_send.at[slot, 1], a_fin_recv.at[slot, 1, 1], left),
        )

    def b1_copies(j):
        slot = j % S_SLOTS
        right, left, p = ring(1 - j % 2)
        far, nxt, prv = (p + 2) % 4, (p + 1) % 4, (p + 3) % 4
        return (
            remote(own_b.at[slot, 0, far], rb_relay.at[slot, 0], b_send.at[slot, 0], b_relay_recv.at[slot, 0], right),
            remote(own_b.at[slot, 1, far], rb_relay.at[slot, 1], b_send.at[slot, 1], b_relay_recv.at[slot, 1], left),
            remote(own_b.at[slot, 1, nxt], rb_fin.at[slot, 0, 1], b_send.at[slot, 2], b_fin_recv.at[slot, 0, 1], right),
            remote(own_b.at[slot, 0, prv], rb_fin.at[slot, 1, 0], b_send.at[slot, 3], b_fin_recv.at[slot, 1, 0], left),
        )

    def b2_copies(j):
        slot = j % S_SLOTS
        right, left, _ = ring(1 - j % 2)
        return (
            remote(sb.at[slot, 0], rb_fin.at[slot, 0, 0], b2_send.at[slot, 0], b_fin_recv.at[slot, 0, 0], right),
            remote(sb.at[slot, 1], rb_fin.at[slot, 1, 1], b2_send.at[slot, 1], b_fin_recv.at[slot, 1, 1], left),
        )

    def x_copy(j):
        slot = j % S_SLOTS
        return remote(x_send.at[slot], x_recv.at[slot], xs_sem.at[slot], xr_sem.at[slot], peer_x)

    def c_copy(j):
        slot = j % S_SLOTS
        return remote(c_send.at[slot], c_recv.at[slot], cs_sem.at[slot], cr_sem.at[slot], peer_core)

    def wait_operands(*which):
        for k in which:
            for pair in pairs[k]:
                pair[0].wait()
                pair[1].wait()

    def store_rows(j, halves):
        mine = j % OWN_SLOTS
        par = j % 2
        for y in range(4):
            for z in range(4):
                first = y * (1 - par) + z * par
                second = z * (1 - par) + y * par
                for h in range(2):
                    own[mine, h, first, second] = halves[h][y * 4 + z]

    def product(lhs, rhs):
        return bf16(dot_tn(lhs, rhs))

    def split_halves(result):
        return [result[:, h * 256:(h + 1) * 256].reshape(16, 48, 256) for h in range(2)]

    def compute(j):
        @pl.when(j < 6)
        def _():
            @pl.when(j == 0)
            def _():
                wait_operands(0, 1)
            rhs = w_g[:, pl.ds(pl.multiple_of(j * 512, 512), 512)]
            store_rows(j, split_halves(product(t_n[...], rhs)))

        @pl.when((j >= 6) & (j < 8))
        def _():
            @pl.when(j == 6)
            def _():
                wait_operands(2, 3)
            rhs = w_q[:, pl.ds(pl.multiple_of((j - 6) * 512, 512), 512)]
            store_rows(j, split_halves(product(t_a[...], rhs)))

        @pl.when(j == 8)
        def _():
            wait_operands(4, 5)
            one = product(t_a[...], w_q[:, pl.ds(1024, 128)])
            two = product(t_m[...], w_o[...])
            store_rows(j, split_halves(jnp.concatenate([one, two], axis=1)))

        @pl.when(j >= 9)
        def _():
            @pl.when(j == 9)
            def _():
                wait_operands(6, 7)
            rhs = w_f[:, pl.ds(pl.multiple_of((j - 9) * 256, 256), 256)]
            result = bf16(dot_nn(t_h[...].reshape(1536, 1024), rhs)).reshape(16, 2, 48, 256)
            store_rows(j, [result[:, 0], result[:, 1]])

    def step(i, carry):
        @pl.when(i < N_CHUNKS)
        def _():
            compute(i)
            for copy in a1_copies(i):
                copy.start()

        j1 = i - 1

        @pl.when((j1 >= 0) & (j1 < N_CHUNKS))
        def _():
            slot, mine = j1 % S_SLOTS, j1 % OWN_SLOTS
            _, _, p = ring(j1 % 2)
            first = a1_copies(j1)
            second = a2_copies(j1)
            first[0].wait_recv()
            sa[slot, 0] = (f32(own[mine, 0, (p + 1) % 4]) + f32(ra_relay[slot, 0])).astype(jnp.bfloat16)
            second[0].start()
            first[1].wait_recv()
            sa[slot, 1] = (f32(own[mine, 1, (p + 3) % 4]) + f32(ra_relay[slot, 1])).astype(jnp.bfloat16)
            second[1].start()

        j2 = i - 2

        @pl.when((j2 >= 0) & (j2 < N_CHUNKS))
        def _():
            slot, mine = j2 % S_SLOTS, j2 % OWN_SLOTS
            _, _, p = ring(j2 % 2)
            first = a1_copies(j2)
            second = a2_copies(j2)
            for copy in first + second:
                copy.wait_send()
            first[2].wait_recv()
            first[3].wait_recv()
            second[0].wait_recv()
            second[1].wait_recv()
            for h in range(2):
                own_b[slot, h] = (
                    f32(own[mine, h, p]) + f32(ra_fin[slot, 0, h]) + f32(ra_fin[slot, 1, h])
                ).astype(jnp.bfloat16)
            for copy in b1_copies(j2):
                copy.start()

        j3 = i - 3

        @pl.when((j3 >= 0) & (j3 < N_CHUNKS))
        def _():
            slot = j3 % S_SLOTS
            _, _, p = ring(1 - j3 % 2)
            first = b1_copies(j3)
            second = b2_copies(j3)
            first[0].wait_recv()
            sb[slot, 0] = (f32(own_b[slot, 0, (p + 1) % 4]) + f32(rb_relay[slot, 0])).astype(jnp.bfloat16)
            second[0].start()
            first[1].wait_recv()
            sb[slot, 1] = (f32(own_b[slot, 1, (p + 3) % 4]) + f32(rb_relay[slot, 1])).astype(jnp.bfloat16)
            second[1].start()

        j4 = i - 4

        @pl.when((j4 >= 0) & (j4 < N_CHUNKS))
        def _():
            slot = j4 % S_SLOTS
            _, _, p = ring(1 - j4 % 2)
            first = b1_copies(j4)
            second = b2_copies(j4)
            for copy in first + second:
                copy.wait_send()
            first[2].wait_recv()
            first[3].wait_recv()
            second[0].wait_recv()
            second[1].wait_recv()
            total = [
                f32(own_b[slot, h, p]) + f32(rb_fin[slot, 0, h]) + f32(rb_fin[slot, 1, h])
                for h in range(2)
            ]
            low = xhi == 0

            @pl.when(j4 < 9)
            def _():
                for h in range(2):
                    x_send[slot, h] = jnp.where(low, total[h][24:], total[h][:24])
                    x_keep[slot, h] = jnp.where(low, total[h][:24], total[h][24:])

            @pl.when(j4 >= 9)
            def _():
                sent = jnp.where(low, total[1], total[0])
                kept = jnp.where(low, total[0], total[1])
                for h in range(2):
                    x_send[slot, h] = sent[h * 24:(h + 1) * 24]
                    x_keep[slot, h] = kept[h * 24:(h + 1) * 24]

            x_copy(j4).start()

        j5 = i - 5

        @pl.when((j5 >= 0) & (j5 < N_CHUNKS))
        def _():
            slot = j5 % S_SLOTS
            x_copy(j5).wait()

            @pl.when(j5 < 9)
            def _():
                for h in range(2):
                    c_tmp[h] = x_keep[slot, h] + x_recv[slot, h]
                low = core == 0
                for h in range(2):
                    upper, lower = c_tmp[h, 0:12], c_tmp[h, 12:24]
                    c_send[slot, h, 0:12] = jnp.where(low, lower, upper)
                    c_keep[slot, h, 0:12] = jnp.where(low, upper, lower)
                c_copy(j5).start()

            @pl.when(j5 >= 9)
            def _():
                column = pl.ds(pl.multiple_of((j5 - 9) * 256, 256), 256)
                for h in range(2):
                    o_dn[h * 24:(h + 1) * 24, column] = x_keep[slot, h] + x_recv[slot, h]

        j6 = i - 6

        @pl.when((j6 >= 0) & (j6 < 9))
        def _():
            slot = j6 % S_SLOTS
            c_copy(j6).wait()
            for source, who in ((c_keep, core), (c_recv, 1 - core)):
                @pl.when(j6 < 6)
                def _():
                    for h in range(2):
                        column = pl.multiple_of(who * 3072 + j6 * 512 + h * 256, 256)
                        o_gu[:, 0, pl.ds(column, 256)] = source[slot, h, 0:12]

                @pl.when((j6 >= 6) & (j6 < 8))
                def _():
                    for h in range(2):
                        column = pl.multiple_of(who * 1152 + (j6 - 6) * 512 + h * 256, 128)
                        o_qkv[:, 0, pl.ds(column, 256)] = source[slot, h, 0:12]

                @pl.when(j6 == 8)
                def _():
                    o_qkv[:, 0, pl.ds(pl.multiple_of(who * 1152 + 1024, 128), 128)] = source[slot, 0, 0:12, 0:128]
                    o_out[:, 0, pl.ds(pl.multiple_of(who * 384, 128), 128)] = source[slot, 0, 0:12, 128:256]
                    o_out[:, 0, pl.ds(pl.multiple_of(who * 384 + 128, 128), 256)] = source[slot, 1, 0:12]

        for stage in range(4):
            @pl.when(i == 2 * stage + 2)
            def _():
                v_finish(stage)
                if stage < 3:
                    v_start(stage + 1)

        return carry

    lax.fori_loop(0, N_CHUNKS + 6, step, 0)
    o_vec[...] = v_acc[4]


def reduce_weights(xa, xm, xn, xh, gq, go, gg, gf, vec):
    low, wide = jnp.bfloat16, jnp.float32
    hbm = pl.BlockSpec(memory_space=pl.ANY)
    vmem = pl.BlockSpec(memory_space=pltpu.VMEM)
    dma = pltpu.SemaphoreType.DMA
    s = S_SLOTS
    return pl.pallas_call(
        reduce_kernel,
        out_shape=[
            jax.ShapeDtypeStruct((12, 1, 2304), wide),
            jax.ShapeDtypeStruct((12, 1, 768), wide),
            jax.ShapeDtypeStruct((12, 1, 6144), wide),
            jax.ShapeDtypeStruct((48, 768), wide),
            jax.ShapeDtypeStruct((8, 768), wide),
        ],
        in_specs=[hbm] * 8 + [vmem],
        out_specs=[vmem] * 5,
        scratch_shapes=[
            pltpu.VMEM((1024, 768), low),
            pltpu.VMEM((1024, 768), low),
            pltpu.VMEM((1024, 768), low),
            pltpu.VMEM((32, 48, 1024), low),
            pltpu.VMEM((1024, 1152), low),
            pltpu.VMEM((1024, 384), low),
            pltpu.VMEM((1024, 3072), low),
            pltpu.VMEM((1024, 768), low),
            pltpu.VMEM((OWN_SLOTS, 2, 4, 4, 48, 256), low),
            pltpu.VMEM((s, 2, 4, 48, 256), low),
            pltpu.VMEM((s, 2, 2, 4, 48, 256), low),
            pltpu.VMEM((s, 2, 4, 48, 256), low),
            pltpu.VMEM((s, 2, 4, 48, 256), low),
            pltpu.VMEM((s, 2, 48, 256), low),
            pltpu.VMEM((s, 2, 2, 48, 256), low),
            pltpu.VMEM((s, 2, 48, 256), low),
            pltpu.VMEM((s, 2, 24, 256), wide),
            pltpu.VMEM((s, 2, 24, 256), wide),
            pltpu.VMEM((s, 2, 24, 256), wide),
            pltpu.VMEM((2, 24, 256), wide),
            pltpu.VMEM((s, 2, 16, 256), wide),
            pltpu.VMEM((s, 2, 16, 256), wide),
            pltpu.VMEM((s, 2, 16, 256), wide),
            pltpu.VMEM((5, 8, 768), wide),
            pltpu.VMEM((8, 8, 768), wide),
            dma((8, 2)), dma((8, 2)), dma((8, 2)),
            dma((s, 4)), dma((s, 2)), dma((s, 2, 2)), dma((s, 2)),
            dma((s, 4)), dma((s, 2)), dma((s, 2, 2)), dma((s, 2)),
            dma((s,)), dma((s,)), dma((s,)), dma((s,)),
            dma((8,)), dma((8,)),
        ],
        compiler_params=pltpu.CompilerParams(
            collective_id=0, has_side_effects=True, vmem_limit_bytes=56 * 1024 * 1024
        ),
        cost_estimate=pl.CostEstimate(flops=10 ** 10, bytes_accessed=2 * 10 ** 7, transcendentals=0),
        name="reduce_weights",
    )(xa, xm, xn, xh.reshape(2, 32, 2, 48, 256), gq, go, gg, gf, vec)


def place_kernel(start, boundary, qkv, out, gate_up, down, vec, o_b, o_q, o_o, o_g, o_d, o_gains, o_biases, sems):
    copies = [
        pltpu.make_async_copy(source, target, sems.at[k])
        for k, (source, target) in enumerate(
            ((boundary, o_b.at[0]), (gate_up, o_g), (qkv, o_q), (out, o_o), (down, o_d.at[0]))
        )
    ]
    for copy in copies:
        copy.start()
    mine = pltpu.roll(vec[...], lax.rem(D - start[0], D), axis=1)
    o_gains[0] = mine[:2, :12]
    o_biases[:, 0] = mine[2:, :12]
    for copy in copies:
        copy.wait()


def place(start, boundary, qkv, out, gate_up, down, vec):
    wide = jnp.float32
    hbm = pl.BlockSpec(memory_space=pl.ANY)
    vmem = pl.BlockSpec(memory_space=pltpu.VMEM)
    return pl.pallas_call(
        place_kernel,
        out_shape=[
            jax.ShapeDtypeStruct((1, 2, 256, 768), wide),
            jax.ShapeDtypeStruct((12, 1, 2304), wide),
            jax.ShapeDtypeStruct((12, 1, 768), wide),
            jax.ShapeDtypeStruct((12, 1, 6144), wide),
            jax.ShapeDtypeStruct((1, 48, 768), wide),
            jax.ShapeDtypeStruct((1, 2, 12), wide),
            jax.ShapeDtypeStruct((6, 1, 12), wide),
        ],
        in_specs=[pl.BlockSpec(memory_space=pltpu.SMEM)] + [hbm] * 5 + [vmem],
        out_specs=[hbm] * 5 + [vmem] * 2,
        scratch_shapes=[pltpu.SemaphoreType.DMA((5,))],
        name="place",
    )(start, boundary, qkv, out, gate_up, down, vec)


def on_device(
    tokens, cotangent, short_lens, long_lens, w_qkv, w_out, w_gate_up, w_down, gains, biases
):
    boundary, x_a, x_m, x_n, x_h, g_q, g_o, g_g, g_f, vec = run_layers(
        short_lens, long_lens, tokens, cotangent, w_qkv[0], w_out[0], w_gate_up[0], w_down[0], gains[0],
        jnp.transpose(biases, (1, 0, 2)),
    )
    g_qkv, g_out, g_gu, g_dn, g_vec = reduce_weights(x_a, x_m, x_n, x_h, g_q, g_o, g_g, g_f, vec)
    start = jnp.full((1,), lax.axis_index("dp") * 12, jnp.int32)
    b, q, o, g, d, gains_out, biases_out = place(start, boundary, g_qkv, g_out, g_gu, g_dn, g_vec)
    q, o, g, biases_out = (jnp.transpose(rows, (1, 0, 2)) for rows in (q, o, g, biases_out))
    return (b, q, o, g, d, gains_out, biases_out)


def solution(mesh):
    placed = (
        P(None, "dp", None),
        P(None, "dp", None),
        P("dp"),
        P("dp"),
        P("section", None, None),
        P("section", None, None),
        P("section", None, None),
        P("section", None, None),
        P("section", None, None),
        P("section", None, None),
    )
    return jax.shard_map(
        on_device,
        mesh=mesh,
        in_specs=placed,
        out_specs=(
            P("section", None, "dp", None),
            P("section", "dp", None),
            P("section", "dp", None),
            P("section", "dp", None),
            P("section", "dp", None),
            P("section", None, "dp"),
            P("section", None, "dp"),
        ),
        check_vma=False,
    )
```

```python
import jax
import jax.numpy as jnp
from jax import lax
from jax.experimental import pallas as pl
from jax.experimental.pallas import tpu as pltpu
from jax.sharding import PartitionSpec as P

D = 768
HEADS = 12
FF = 3072
BLOCK = 768
BAND = 32
N_CHUNKS = 12
N_DOWN = 3
SLOTS = 5
OWN_SLOTS = 3
VMEM_LIMIT = 62 * 1024 * 1024
MESH_IDS = pl.DeviceIdType.MESH

epsilon = 1e-05
masked_value = -1000000000.0


def dot_nn(lhs, rhs):
    return jnp.dot(lhs, rhs, preferred_element_type=jnp.float32)


def dot_nt(lhs, rhs):
    return lax.dot_general(lhs, rhs, (((1,), (1,)), ((), ())), preferred_element_type=jnp.float32)


def dot_tn(lhs, rhs):
    return lax.dot_general(lhs, rhs, (((0,), (0,)), ((), ())), preferred_element_type=jnp.float32)


def f32(value):
    return value.astype(jnp.float32)


def bf16(value):
    return value.astype(jnp.bfloat16)


def fold_rows(value):
    return jnp.sum(value.reshape(value.shape[0] // 8, 8, value.shape[1]), 0)


def gelu_terms(gate):
    cdf = 0.5 * (1.0 + lax.erf(gate * 0.7071067811865476))
    density = jnp.exp(-0.5 * gate * gate) * 0.3989422804014327
    return gate * cdf, cdf + gate * density


def when(condition):
    if isinstance(condition, bool):
        return (lambda body: body()) if condition else (lambda body: None)
    return pl.when(condition)


def both(value):
    return value.reshape(512, value.shape[-1])


def layers_kernel(
    short_lens, long_lens, tokens, cotangent, w_qkv, w_out, w_gate_up, w_down, gains, biases,
    boundary, o_qkv, o_out, o_gu, o_dn, o_vec,
    wq, wo, wg, wd, x_s, g_s, qkv_s, p_s, mixed_s, nl_s, low_s, n1_s, n2_s, r1_s, r2_s, gu_s, ht_s,
    gf_s, ga_s, send_s, out_s, acc_s, f_s, gate_s, up_s, dist_s, mask_s, vec_s,
    peer_n, peer_h, peer_f, peer_g,
    own, ra_relay, ra_fin, sa, own_b, rb_relay, rb_fin, sb, x_send, x_keep, x_recv, c_tmp, c_send, c_keep, c_recv,
    v_acc, v_recv,
    w_sem, x_sem, g_sem, out_sem, f_send, f_recv, b_send, b_recv, pair_send, pair_recv,
    a_send, a_relay_recv, a_fin_recv, a2_send,
    bb_send, bb_relay_recv, bb_fin_recv, b2_send,
    xs_sem, xr_sem, cs_sem, cr_sem, vs_sem, vr_sem,
):
    sec = lax.axis_index("section")
    first = sec == 0
    second = sec == 1
    me = lax.axis_index("dp")
    core = me % 2
    xhi = (me // 2) % 2
    zz = (me // 4) % 4
    yy = me // 16
    other = 1 - core

    def dev(y, z, x, c):
        return ((y * 4 + z) * 2 + x) * 2 + c

    peer_core = dev(yy, zz, xhi, other)
    peer_x = dev(yy, zz, 1 - xhi, core)
    y_ids = [dev((yy + k) % 4, zz, xhi, core) for k in (1, 2, 3)]
    z_ids = [dev(yy, (zz + k) % 4, xhi, core) for k in (1, 2, 3)]

    def remote(src, dst, send, recv, target):
        return pltpu.make_async_remote_copy(
            src_ref=src, dst_ref=dst, send_sem=send, recv_sem=recv,
            device_id={"dp": target}, device_id_type=MESH_IDS,
        )

    def across(src, dst, send, recv):
        return pltpu.make_async_remote_copy(
            src_ref=src, dst_ref=dst, send_sem=send, recv_sem=recv,
            device_id={"section": 1 - sec}, device_id_type=MESH_IDS,
        )

    w_copies = [
        pltpu.make_async_copy(w_qkv, wq, w_sem.at[0]),
        pltpu.make_async_copy(w_out, wo, w_sem.at[1]),
        pltpu.make_async_copy(w_gate_up, wg, w_sem.at[2]),
        pltpu.make_async_copy(w_down, wd, w_sem.at[3]),
    ]

    def token_copy(m):
        return pltpu.make_async_copy(tokens.at[m], x_s.at[m], x_sem.at[m])

    def cot_copy(m):
        return pltpu.make_async_copy(cotangent.at[m], g_s.at[m], g_sem.at[m])

    def hand_on(m):
        return across(send_s.at[m], x_s.at[m], f_send.at[m], f_recv.at[m])

    def hand_back(m):
        return across(send_s.at[m], g_s.at[m], b_send.at[m], b_recv.at[m])

    def out_copy(m):
        return pltpu.make_async_copy(out_s, boundary.at[m], out_sem.at[m])

    def pair(k, m):
        rows = pl.ds(m * 256, 256)
        src, dst = (
            lambda: (nl_s.at[m], peer_n.at[m]),
            lambda: (ht_s.at[m, :, other], peer_h.at[m]),
            lambda: (gf_s.at[m], peer_f.at[m]),
            lambda: (gu_s.at[m, :, pl.ds(other * FF, FF)], peer_g.at[m]),
            lambda: (x_s.at[m], wg.at[rows, pl.ds(0, 768)]),
            lambda: (mixed_s.at[m], wg.at[rows, pl.ds(768, 768)]),
            lambda: (qkv_s.at[m, :, pl.ds(other * 1152, 1152)], wg.at[rows, pl.ds(1536, 1152)]),
            lambda: (ga_s.at[m, :, pl.ds(other * 384, 384)], wg.at[rows, pl.ds(2688, 384)]),
        )[k]()
        return remote(src, dst, pair_send.at[k, m], pair_recv.at[k, m], peer_core)

    def pair_wait(*which):
        for k in which:
            for m in range(2):
                pair(k, m).wait()

    @pl.when(first)
    def _():
        token_copy(0).start()

    w_copies[0].start()
    w_copies[1].start()

    @pl.when(first)
    def _():
        token_copy(1).start()

    w_copies[2].start()
    w_copies[3].start()

    @pl.when(second)
    def _():
        cot_copy(0).start()
        cot_copy(1).start()

    barrier = pltpu.get_barrier_semaphore()
    pl.semaphore_signal(barrier, inc=1, device_id={"section": 1 - sec}, device_id_type=MESH_IDS)
    for target in [peer_core, peer_x] + y_ids + z_ids:
        pl.semaphore_signal(barrier, inc=1, device_id={"dp": target}, device_id_type=MESH_IDS)
    pl.semaphore_wait(barrier, 9)

    vec_s[...] = jnp.zeros_like(vec_s)
    rows_j = lax.broadcasted_iota(jnp.int32, (256, 256), 0)
    cols_i = lax.broadcasted_iota(jnp.int32, (256, 256), 1)
    dist_s[...] = f32(jnp.abs(rows_j - cols_i))
    length_a, length_b, length_long = short_lens[0], short_lens[1], long_lens[0]
    for m in range(2):
        if m == 0:
            limit = jnp.where(rows_j < 128, length_a, length_b + 128)
            apart = jnp.where((rows_j >> 7) == (cols_i >> 7), 0, 1024)
            ok = rows_j + apart < limit
        else:
            ok = rows_j < length_long
        mask_s[m] = jnp.where(ok, 1.0, 0.0)


    def v_sends(stage):
        targets = ([peer_core], [peer_x], y_ids, z_ids)[stage]
        base = (0, 1, 2, 5)[stage]
        count = len(targets)
        return [
            remote(
                v_acc.at[stage], v_recv.at[base + (count - 1 - k)],
                vs_sem.at[base + k], vr_sem.at[base + (count - 1 - k)], targets[k],
            )
            for k in range(count)
        ]

    def v_start(stage):
        for copy in v_sends(stage):
            copy.start()

    def v_finish(stage):
        base = (0, 1, 2, 5)[stage]
        copies = v_sends(stage)
        for copy in copies:
            copy.wait_send()
        for copy in copies:
            copy.wait_recv()
        total = v_acc[stage]
        for k in range(len(copies)):
            total = total + v_recv[base + k]
        v_acc[stage + 1] = total

    def ring(par):
        right = y_ids[0] * (1 - par) + z_ids[0] * par
        left = y_ids[2] * (1 - par) + z_ids[2] * par
        place = yy * (1 - par) + zz * par
        return right, left, place

    def a1_copies(j):
        slot, mine = j % SLOTS, j % OWN_SLOTS
        right, left, p = ring(j % 2)
        far, nxt, prv = (p + 2) % 4, (p + 1) % 4, (p + 3) % 4
        return (
            remote(own.at[mine, 0, far], ra_relay.at[slot, 0], a_send.at[slot, 0], a_relay_recv.at[slot, 0], right),
            remote(own.at[mine, 1, far], ra_relay.at[slot, 1], a_send.at[slot, 1], a_relay_recv.at[slot, 1], left),
            remote(own.at[mine, 1, nxt], ra_fin.at[slot, 0, 1], a_send.at[slot, 2], a_fin_recv.at[slot, 0, 1], right),
            remote(own.at[mine, 0, prv], ra_fin.at[slot, 1, 0], a_send.at[slot, 3], a_fin_recv.at[slot, 1, 0], left),
        )

    def a2_copies(j):
        slot, mine = j % SLOTS, j % 2
        right, left, _ = ring(j % 2)
        return (
            remote(sa.at[mine, 0], ra_fin.at[slot, 0, 0], a2_send.at[mine, 0], a_fin_recv.at[slot, 0, 0], right),
            remote(sa.at[mine, 1], ra_fin.at[slot, 1, 1], a2_send.at[mine, 1], a_fin_recv.at[slot, 1, 1], left),
        )

    def b1_copies(j):
        slot, mine = j % SLOTS, j % OWN_SLOTS
        right, left, p = ring(1 - j % 2)
        far, nxt, prv = (p + 2) % 4, (p + 1) % 4, (p + 3) % 4
        return (
            remote(own_b.at[mine, 0, far], rb_relay.at[slot, 0], bb_send.at[slot, 0], bb_relay_recv.at[slot, 0], right),
            remote(own_b.at[mine, 1, far], rb_relay.at[slot, 1], bb_send.at[slot, 1], bb_relay_recv.at[slot, 1], left),
            remote(own_b.at[mine, 1, nxt], rb_fin.at[slot, 0, 1], bb_send.at[slot, 2], bb_fin_recv.at[slot, 0, 1], right),
            remote(own_b.at[mine, 0, prv], rb_fin.at[slot, 1, 0], bb_send.at[slot, 3], bb_fin_recv.at[slot, 1, 0], left),
        )

    def b2_copies(j):
        slot, mine = j % SLOTS, j % 2
        right, left, _ = ring(1 - j % 2)
        return (
            remote(sb.at[mine, 0], rb_fin.at[slot, 0, 0], b2_send.at[mine, 0], bb_fin_recv.at[slot, 0, 0], right),
            remote(sb.at[mine, 1], rb_fin.at[slot, 1, 1], b2_send.at[mine, 1], bb_fin_recv.at[slot, 1, 1], left),
        )

    def x_copy(j):
        slot, mine = j % SLOTS, j % 2
        return remote(x_send.at[mine], x_recv.at[slot], xs_sem.at[mine], xr_sem.at[slot], peer_x)

    def c_copy(j):
        slot, mine = j % SLOTS, j % 2
        return remote(c_send.at[mine], c_recv.at[slot], cs_sem.at[mine], cr_sem.at[slot], peer_core)

    def place_rows(j, piece):
        mine = j % OWN_SLOTS
        par = j % 2
        for y in range(4):
            for z in range(4):
                i1 = y * (1 - par) + z * par
                i2 = z * (1 - par) + y * par
                for x in range(2):
                    own[mine, x, i1, i2] = bf16(piece(y * 4 + z, x))

    def place_regular(j, result):
        def piece(block, x):
            rows = result[block * 48 + x * 24:block * 48 + x * 24 + 24]
            return jnp.concatenate([rows[:, :256], rows[:, 256:]], 0)

        place_rows(j, piece)

    def compute(j):
        @when(j < N_DOWN)
        def _():
            @when(j == 0)
            def _():
                pair_wait(1, 2)

            cols = pl.ds(pl.multiple_of(j * 256, 256), 256) if not isinstance(j, int) else pl.ds(j * 256, 256)
            result = None
            for m in range(2):
                for left, right in ((ht_s[m, :, core], gf_s[m, :, cols]), (peer_h[m], peer_f[m, :, cols])):
                    term = dot_nn(left.reshape(1536, 256), right)
                    result = term if result is None else result + term
            place_rows(j, lambda block, x: result[(block * 2 + x) * 48:(block * 2 + x + 1) * 48])

        @when((j >= N_DOWN) & (j < N_DOWN + 6))
        def _():
            @when(j == N_DOWN)
            def _():
                pair_wait(0, 3)
                for k in (4, 5, 6, 7):
                    for m in range(2):
                        pair(k, m).start()

            column = pl.multiple_of((j - N_DOWN) * 512, 512)
            mine = gu_s[:, :, pl.ds(pl.multiple_of(core * FF + column, 512), 512)]
            place_regular(j, dot_tn(both(nl_s[...]), both(mine)) + dot_tn(both(peer_n[...]), both(peer_g[:, :, pl.ds(column, 512)])))

        def qkv_part(column, width):
            mine = qkv_s[:, :, pl.ds(pl.multiple_of(core * 1152 + column, 128), width)]
            far = wg[0:512, pl.ds(pl.multiple_of(1536 + column, 128), width)]
            return dot_tn(both(x_s[...]), both(mine)) + dot_tn(wg[0:512, 0:768], far)

        @when((j >= N_DOWN + 6) & (j < N_DOWN + 8))
        def _():
            @when(j == N_DOWN + 6)
            def _():
                pair_wait(4, 5, 6, 7)

            place_regular(j, qkv_part((j - N_DOWN - 6) * 512, 512))

        @when(j == N_DOWN + 8)
        def _():
            mine = ga_s[:, :, pl.ds(pl.multiple_of(core * 384, 128), 384)]
            out_part = dot_tn(both(mixed_s[...]), both(mine)) + dot_tn(wg[0:512, 768:1536], wg[0:512, 2688:3072])
            place_regular(j, jnp.concatenate([qkv_part(1024, 128), out_part], 1))

    def step(i, carry):
        @when(i < N_CHUNKS)
        def _():
            compute(i)
            for copy in a1_copies(i):
                copy.start()

        j1 = i - 1

        @when((j1 >= 0) & (j1 < N_CHUNKS))
        def _():
            slot, mine, buf = j1 % SLOTS, j1 % OWN_SLOTS, j1 % 2
            _, _, p = ring(j1 % 2)
            before = a1_copies(j1)
            after = a2_copies(j1)
            before[0].wait_recv()
            sa[buf, 0] = bf16(f32(own[mine, 0, (p + 1) % 4]) + f32(ra_relay[slot, 0]))
            after[0].start()
            before[1].wait_recv()
            sa[buf, 1] = bf16(f32(own[mine, 1, (p + 3) % 4]) + f32(ra_relay[slot, 1]))
            after[1].start()

        j2 = i - 2

        @when((j2 >= 0) & (j2 < N_CHUNKS))
        def _():
            slot, mine = j2 % SLOTS, j2 % OWN_SLOTS
            _, _, p = ring(j2 % 2)
            before = a1_copies(j2)
            after = a2_copies(j2)
            for copy in before + after:
                copy.wait_send()
            for copy in before[2:] + after:
                copy.wait_recv()
            for h in range(2):
                own_b[mine, h] = bf16(f32(own[mine, h, p]) + f32(ra_fin[slot, 0, h]) + f32(ra_fin[slot, 1, h]))
            for copy in b1_copies(j2):
                copy.start()

        j3 = i - 3

        @when((j3 >= 0) & (j3 < N_CHUNKS))
        def _():
            slot, mine, buf = j3 % SLOTS, j3 % OWN_SLOTS, j3 % 2
            _, _, p = ring(1 - j3 % 2)
            before = b1_copies(j3)
            after = b2_copies(j3)
            before[0].wait_recv()
            sb[buf, 0] = bf16(f32(own_b[mine, 0, (p + 1) % 4]) + f32(rb_relay[slot, 0]))
            after[0].start()
            before[1].wait_recv()
            sb[buf, 1] = bf16(f32(own_b[mine, 1, (p + 3) % 4]) + f32(rb_relay[slot, 1]))
            after[1].start()

        j4 = i - 4

        @when((j4 >= 0) & (j4 < N_CHUNKS))
        def _():
            slot, mine, buf = j4 % SLOTS, j4 % OWN_SLOTS, j4 % 2
            _, _, p = ring(1 - j4 % 2)
            before = b1_copies(j4)
            after = b2_copies(j4)
            for copy in before + after:
                copy.wait_send()
            for copy in before[2:] + after:
                copy.wait_recv()
            total = [f32(own_b[mine, h, p]) + f32(rb_fin[slot, 0, h]) + f32(rb_fin[slot, 1, h]) for h in range(2)]
            x_send[buf] = jnp.where(xhi == 0, total[1], total[0])
            x_keep[buf] = jnp.where(xhi == 0, total[0], total[1])
            x_copy(j4).start()

        j5 = i - 5

        @when((j5 >= 0) & (j5 < N_CHUNKS))
        def _():
            slot, buf = j5 % SLOTS, j5 % 2
            x_copy(j5).wait()

            @when(j5 < N_DOWN)
            def _():
                cols = pl.ds(pl.multiple_of(j5 * 256, 256), 256)
                o_dn[:, cols] = x_keep[buf] + x_recv[slot]

            @when(j5 >= N_DOWN)
            def _():
                c_tmp[...] = x_keep[buf] + x_recv[slot]
                for h in range(2):
                    upper, lower = c_tmp[24 * h:24 * h + 12], c_tmp[24 * h + 12:24 * h + 24]
                    c_send[buf, h, 0:12] = jnp.where(core == 0, lower, upper)
                    c_keep[buf, h, 0:12] = jnp.where(core == 0, upper, lower)
                c_copy(j5).start()

        j6 = i - 6

        @when((j6 >= N_DOWN) & (j6 < N_CHUNKS))
        def _():
            slot, buf = j6 % SLOTS, j6 % 2
            c_copy(j6).wait()
            for source, at, who in ((c_keep, buf, core), (c_recv, slot, other)):
                @when(j6 < N_DOWN + 6)
                def _():
                    for h in range(2):
                        column = pl.multiple_of(who * FF + (j6 - N_DOWN) * 512 + h * 256, 256)
                        o_gu[:, 0, pl.ds(column, 256)] = source[at, h, 0:12]

                @when((j6 >= N_DOWN + 6) & (j6 < N_DOWN + 8))
                def _():
                    for h in range(2):
                        column = pl.multiple_of(who * 1152 + (j6 - N_DOWN - 6) * 512 + h * 256, 128)
                        o_qkv[:, 0, pl.ds(column, 256)] = source[at, h, 0:12]

                @when(j6 == N_DOWN + 8)
                def _():
                    o_qkv[:, 0, pl.ds(pl.multiple_of(who * 1152 + 1024, 128), 128)] = source[at, 0, 0:12, 0:128]
                    o_out[:, 0, pl.ds(pl.multiple_of(who * 384, 128), 128)] = source[at, 0, 0:12, 128:256]
                    o_out[:, 0, pl.ds(pl.multiple_of(who * 384 + 128, 128), 256)] = source[at, 1, 0:12]

        return carry


    def band(k):
        return pl.ds(k * BAND, BAND)

    def normalise(value):
        average = jnp.mean(value, -1, keepdims=True)
        centred = value - average
        inverse = lax.rsqrt(jnp.mean(centred * centred, -1, keepdims=True) + epsilon)
        return centred * inverse, inverse

    lanes = lax.broadcasted_iota(jnp.int32, (256, 128), 1)

    def own_lanes(e):
        return (lanes < 64) if e == 0 else (lanes >= 64)

    def forward(m, carry):
        @pl.when(first)
        def _():
            token_copy(m).wait()

        @pl.when(second)
        def _():
            hand_on(m).wait_recv()

        @pl.when(m == 0)
        def _():
            w_copies[0].wait()

        x = x_s[m]
        query = dot_nn(x, wq[:, 0:768]) + biases[0]
        qkv_s[m, :, 0:768] = bf16(f32(bf16(query)) * 0.125)
        qkv_s[m, :, 768:1536] = bf16(dot_nn(x, wq[:, 768:1536]))
        qkv_s[m, :, 1536:2304] = bf16(dot_nn(x, wq[:, 1536:2304]) + biases[1])

        for hp in range(6):
            at = pl.ds(hp * 128, 128)
            q2 = qkv_s[m, :, at]
            k2 = qkv_s[m, :, pl.ds(hp * 128 + 768, 128)]
            v2 = qkv_s[m, :, pl.ds(hp * 128 + 1536, 128)]
            outs = []
            for e in range(2):
                head = 2 * hp + e
                qm = jnp.where(own_lanes(e), q2, jnp.zeros_like(q2))
                scores = dot_nt(k2, qm) - 2.0 ** (-8.0 * (head + 1) / HEADS) * dist_s[...]
                scores = jnp.where(mask_s[m] > 0.5, scores, masked_value)
                expo = jnp.exp(scores - jnp.max(scores, 0, keepdims=True))
                probs = bf16(expo * (1.0 / jnp.sum(expo, 0, keepdims=True)))
                p_s[m, head] = probs
                outs.append(dot_tn(probs, v2))
            mixed_s[m, :, at] = bf16(jnp.where(lanes < 64, outs[0], outs[1]))

        @pl.when(m == 0)
        def _():
            w_copies[1].wait()

        acc_s[...] = dot_nn(mixed_s[m], wo[...])
        for k in range(256 // BAND):
            r = band(k)
            value = f32(x_s[m, r]) + (acc_s[r] + biases[2])
            unit, inverse = normalise(value)
            normed = unit * gains[0:1] + biases[3]
            n1_s[m, r] = bf16(unit)
            r1_s[m, r] = inverse
            f_s[r] = normed
            nl_s[m, r] = bf16(normed)

        pair(0, m).start()

        @pl.when(m == 0)
        def _():
            w_copies[2].wait()
            w_copies[3].wait()

        for jb in range(FF // BLOCK):
            c0 = jb * BLOCK
            low = nl_s[m]
            gate_s[...] = dot_nn(low, wg[:, c0:c0 + BLOCK])
            up_s[...] = dot_nn(low, wg[:, c0 + FF:c0 + FF + BLOCK])
            for k in range(256 // BAND):
                r = band(k)
                gate, up = gate_s[r], up_s[r]
                act, slope = gelu_terms(gate)
                gu_s[m, r, c0:c0 + BLOCK] = bf16(up * slope)
                gu_s[m, r, c0 + FF:c0 + FF + BLOCK] = bf16(act)
                gate_s[r] = act * up
            hid = bf16(gate_s[...])
            ht_s[m, 8 * jb:8 * jb + 8] = hid.T.reshape(8, 2, 48, 256)
            term = dot_nn(hid, wd[c0:c0 + BLOCK])
            if jb == 0:
                acc_s[...] = term
            else:
                acc_s[...] += term

        @pl.when(second & (m == 1))
        def _():
            out_copy(0).wait()

        for k in range(256 // BAND):
            r = band(k)
            value = f_s[r] + (acc_s[r] + biases[4])
            unit, inverse = normalise(value)
            n2_s[m, r] = bf16(unit)
            r2_s[m, r] = inverse
            result = unit * gains[1:2] + biases[5]
            out_s[r] = result
            send_s[m, r] = bf16(result)

        @pl.when(first)
        def _():
            hand_on(m).start()

        @pl.when(second)
        def _():
            out_copy(m).start()

        pair(1, m).start()
        return carry

    lax.fori_loop(0, 2, forward, 0)

    def norm_back(grad, unit, inverse, gain):
        scaled = grad * gain
        mean_one = jnp.mean(scaled, -1, keepdims=True)
        mean_two = jnp.mean(scaled * unit, -1, keepdims=True)
        return inverse * (scaled - mean_one - unit * mean_two)

    def backward(m, carry):
        early = first & (m == 1)

        @pl.when(first)
        def _():
            hand_on(m).wait_send()
            hand_back(m).wait_recv()

        @pl.when(second)
        def _():
            cot_copy(m).wait()

        for k in range(256 // BAND):
            r = band(k)
            row = lax.broadcasted_iota(jnp.int32, (BAND, 1), 0) + k * BAND
            limit = jnp.where(m == 0, jnp.where(row < 128, length_a, length_b + 128), length_long)
            live = jnp.where((row < limit) | first, 1.0, 0.0)
            grad = f32(g_s[m, r]) * live
            unit = f32(n2_s[m, r])
            vec_s[1] += fold_rows(grad * unit)
            vec_s[7] += fold_rows(grad)
            grad_in = norm_back(grad, unit, r2_s[m, r], gains[1:2])
            f_s[r] = grad_in
            low = bf16(grad_in)
            gf_s[m, r] = low
            vec_s[6] += fold_rows(f32(low))

        pair(2, m).start()

        for jb in range(FF // BLOCK):
            c0 = jb * BLOCK
            gate_s[...] = dot_nt(gf_s[m], wd[c0:c0 + BLOCK])
            for k in range(256 // BAND):
                r = band(k)
                hid = gate_s[r]
                for c in (c0, c0 + FF):
                    gu_s[m, r, c:c + BLOCK] = bf16(hid * f32(gu_s[m, r, c:c + BLOCK]))
            term = dot_nt(gu_s[m, :, c0:c0 + BLOCK], wg[:, c0:c0 + BLOCK])
            term = term + dot_nt(gu_s[m, :, c0 + FF:c0 + FF + BLOCK], wg[:, c0 + FF:c0 + FF + BLOCK])
            if jb == 0:
                acc_s[...] = term
            else:
                acc_s[...] += term
            if jb == 1:
                @pl.when(early)
                def _():
                    step(0, 0)

        pair(3, m).start()

        @pl.when(early)
        def _():
            step(1, 0)

        for k in range(256 // BAND):
            r = band(k)
            grad = acc_s[r] + f_s[r]
            unit = f32(n1_s[m, r])
            vec_s[0] += fold_rows(grad * unit)
            vec_s[5] += fold_rows(grad)
            grad_in = norm_back(grad, unit, r1_s[m, r], gains[0:1])
            f_s[r] = grad_in
            low = bf16(grad_in)
            ga_s[m, r] = low
            vec_s[4] += fold_rows(f32(low))

        low_s[...] = bf16(dot_nt(ga_s[m], wo[...]))

        for hp in range(6):
            at = pl.ds(hp * 128, 128)
            q2 = qkv_s[m, :, at]
            k2 = qkv_s[m, :, pl.ds(hp * 128 + 768, 128)]
            v2 = qkv_s[m, :, pl.ds(hp * 128 + 1536, 128)]
            do2 = low_s[:, at]
            dq, dk, dv = [], [], []
            for e in range(2):
                vm = jnp.where(own_lanes(e), v2, jnp.zeros_like(v2))
                probs = p_s[m, 2 * hp + e]
                weighted = f32(probs) * dot_nt(vm, do2)
                total = jnp.sum(weighted, 0, keepdims=True)
                grad_scores = bf16(weighted - f32(probs) * total)
                dv.append(dot_nn(probs, do2))
                dk.append(dot_nn(grad_scores, q2))
                dq.append(dot_tn(grad_scores, k2))
            grad_q = bf16(jnp.where(lanes < 64, dq[0], dq[1]) * 0.125)
            grad_k = bf16(jnp.where(lanes < 64, dk[0], dk[1]))
            grad_v = bf16(jnp.where(lanes < 64, dv[0], dv[1]))
            vec_s[2, :, at] += fold_rows(f32(grad_q))
            vec_s[3, :, at] += fold_rows(f32(grad_v))
            qkv_s[m, :, at] = grad_q
            qkv_s[m, :, pl.ds(hp * 128 + 768, 128)] = grad_k
            qkv_s[m, :, pl.ds(hp * 128 + 1536, 128)] = grad_v

        @pl.when(early)
        def _():
            step(2, 0)

        @pl.when(first & (m == 1))
        def _():
            out_copy(0).wait()

        grad_a = dot_nt(qkv_s[m], wq[...]) + f_s[...]

        @pl.when(second)
        def _():
            send_s[m] = bf16(grad_a)
            hand_back(m).start()

        @pl.when(first)
        def _():
            out_s[...] = grad_a
            out_copy(m).start()

        return carry

    lax.fori_loop(0, 2, backward, 0)
    for k in range(8):
        v_acc[0, k:k + 1] = jnp.sum(vec_s[k], 0, keepdims=True)
    v_start(0)

    def tail_step(i, carry):
        step(i, carry)
        for stage in range(4):
            @pl.when(i == 2 * stage + 5)
            def _():
                v_finish(stage)
                if stage < 3:
                    v_start(stage + 1)

        return carry

    lax.fori_loop(3 * (1 - sec), N_CHUNKS + 6, tail_step, 0)
    o_vec[...] = v_acc[4]

    @pl.when(second)
    def _():
        hand_back(0).wait_send()
        hand_back(1).wait_send()

    out_copy(1).wait()


def run_layers(short_lens, long_lens, tokens, cotangent, w_qkv, w_out, w_gate_up, w_down, gains, biases):
    low, wide = jnp.bfloat16, jnp.float32
    hbm = pl.BlockSpec(memory_space=pl.ANY)
    vmem = pl.BlockSpec(memory_space=pltpu.VMEM)
    smem = pl.BlockSpec(memory_space=pltpu.SMEM)
    dma = pltpu.SemaphoreType.DMA
    of = pltpu.VMEM
    s = SLOTS
    return pl.pallas_call(
        layers_kernel,
        out_shape=[
            jax.ShapeDtypeStruct((2, 256, 768), wide),
            jax.ShapeDtypeStruct((12, 1, 2304), wide),
            jax.ShapeDtypeStruct((12, 1, 768), wide),
            jax.ShapeDtypeStruct((12, 1, 6144), wide),
            jax.ShapeDtypeStruct((48, 768), wide),
            jax.ShapeDtypeStruct((8, 768), wide),
        ],
        in_specs=[smem] * 2 + [hbm] * 6 + [vmem] * 2,
        out_specs=[hbm] + [vmem] * 5,
        scratch_shapes=[
            of((768, 2304), low), of((768, 768), low), of((768, 6144), low), of((3072, 768), low),
            of((2, 256, 768), low), of((2, 256, 768), low), of((2, 256, 2304), low), of((2, 12, 256, 256), low),
            of((2, 256, 768), low), of((2, 256, 768), low), of((256, 768), low),
            of((2, 256, 768), low), of((2, 256, 768), low),
            of((2, 256, 1), wide), of((2, 256, 1), wide), of((2, 256, 6144), low), of((2, 32, 2, 48, 256), low),
            of((2, 256, 768), low), of((2, 256, 768), low), of((2, 256, 768), low), of((256, 768), wide),
            of((256, 768), wide), of((256, 768), wide), of((256, BLOCK), wide), of((256, BLOCK), wide),
            of((256, 256), wide), of((2, 256, 256), wide), of((8, 8, 768), wide),
            of((2, 256, 768), low), of((2, 32, 48, 256), low), of((2, 256, 768), low), of((2, 256, 3072), low),
            of((OWN_SLOTS, 2, 4, 4, 48, 256), low),
            of((s, 2, 4, 48, 256), low), of((s, 2, 2, 4, 48, 256), low), of((2, 2, 4, 48, 256), low),
            of((OWN_SLOTS, 2, 4, 48, 256), low),
            of((s, 2, 48, 256), low), of((s, 2, 2, 48, 256), low), of((2, 2, 48, 256), low),
            of((2, 48, 256), wide), of((2, 48, 256), wide), of((s, 48, 256), wide),
            of((48, 256), wide), of((2, 2, 16, 256), wide), of((2, 2, 16, 256), wide), of((s, 2, 16, 256), wide),
            of((5, 8, 768), wide), of((8, 8, 768), wide),
            dma((4,)), dma((2,)), dma((2,)), dma((2,)), dma((2,)), dma((2,)), dma((2,)), dma((2,)),
            dma((8, 2)), dma((8, 2)),
            dma((s, 4)), dma((s, 2)), dma((s, 2, 2)), dma((2, 2)),
            dma((s, 4)), dma((s, 2)), dma((s, 2, 2)), dma((2, 2)),
            dma((2,)), dma((s,)), dma((2,)), dma((s,)), dma((8,)), dma((8,)),
        ],
        compiler_params=pltpu.CompilerParams(
            collective_id=0, has_side_effects=True, vmem_limit_bytes=VMEM_LIMIT
        ),
        cost_estimate=pl.CostEstimate(flops=3 * 10 ** 10, bytes_accessed=4 * 10 ** 7, transcendentals=10 ** 7),
        name="run_layers",
    )(short_lens, long_lens, tokens, cotangent, w_qkv, w_out, w_gate_up, w_down, gains, biases)


def place_kernel(start, boundary, qkv, out, gate_up, down, vec, o_b, o_q, o_o, o_g, o_d, o_gains, o_biases):
    o_b[0] = boundary[...]
    o_g[...] = gate_up[...]
    o_q[...] = qkv[...]
    o_o[...] = out[...]
    o_d[0] = down[...]
    mine = pltpu.roll(vec[...], lax.rem(D - start[0], D), axis=1)
    o_gains[0] = mine[:2, :12]
    o_biases[:, 0] = mine[2:, :12]


def place(start, boundary, qkv, out, gate_up, down, vec):
    wide = jnp.float32
    vmem = pl.BlockSpec(memory_space=pltpu.VMEM)
    return pl.pallas_call(
        place_kernel,
        out_shape=[
            jax.ShapeDtypeStruct((1, 2, 256, 768), wide),
            jax.ShapeDtypeStruct((12, 1, 2304), wide),
            jax.ShapeDtypeStruct((12, 1, 768), wide),
            jax.ShapeDtypeStruct((12, 1, 6144), wide),
            jax.ShapeDtypeStruct((1, 48, 768), wide),
            jax.ShapeDtypeStruct((1, 2, 12), wide),
            jax.ShapeDtypeStruct((6, 1, 12), wide),
        ],
        in_specs=[pl.BlockSpec(memory_space=pltpu.SMEM)] + [vmem] * 6,
        out_specs=[vmem] * 7,
        compiler_params=pltpu.CompilerParams(vmem_limit_bytes=32 * 1024 * 1024),
        name="place",
    )(start, boundary, qkv, out, gate_up, down, vec)


def on_device(
    tokens, cotangent, short_lens, long_lens, w_qkv, w_out, w_gate_up, w_down, gains, biases
):
    boundary, q, o, g, d, vec = run_layers(
        short_lens, long_lens, tokens, cotangent, w_qkv[0], w_out[0], w_gate_up[0], w_down[0], gains[0],
        jnp.transpose(biases, (1, 0, 2)),
    )
    start = jnp.full((1,), lax.axis_index("dp") * 12, jnp.int32)
    b, q, o, g, d, gains_out, biases_out = place(start, boundary, q, o, g, d, vec)
    q, o, g, biases_out = (jnp.transpose(rows, (1, 0, 2)) for rows in (q, o, g, biases_out))
    return (b, q, o, g, d, gains_out, biases_out)


def solution(mesh):
    placed = (
        P(None, "dp", None),
        P(None, "dp", None),
        P("dp"),
        P("dp"),
        P("section", None, None),
        P("section", None, None),
        P("section", None, None),
        P("section", None, None),
        P("section", None, None),
        P("section", None, None),
    )
    return jax.shard_map(
        on_device,
        mesh=mesh,
        in_specs=placed,
        out_specs=(
            P("section", None, "dp", None),
            P("section", "dp", None),
            P("section", "dp", None),
            P("section", "dp", None),
            P("section", "dp", None),
            P("section", None, "dp"),
            P("section", None, "dp"),
        ),
        check_vma=False,
    )
```

```python
import jax
import jax.numpy as jnp
from jax import lax
from jax.experimental import pallas as pl
from jax.experimental.pallas import tpu as pltpu
from jax.sharding import PartitionSpec as P

D = 768
HEADS = 12
FF = 3072
BLOCK = 768
BAND = 32
N_CHUNKS = 12
N_DOWN = 3
SLOTS = 5
OWN_SLOTS = 3
VMEM_LIMIT = 62 * 1024 * 1024
MESH_IDS = pl.DeviceIdType.MESH

epsilon = 1e-05
masked_distance = 1e12


def dot_nn(lhs, rhs):
    return jnp.dot(lhs, rhs, preferred_element_type=jnp.float32)


def dot_nt(lhs, rhs):
    return lax.dot_general(lhs, rhs, (((1,), (1,)), ((), ())), preferred_element_type=jnp.float32)


def dot_tn(lhs, rhs):
    return lax.dot_general(lhs, rhs, (((0,), (0,)), ((), ())), preferred_element_type=jnp.float32)


def f32(value):
    return value.astype(jnp.float32)


def bf16(value):
    return value.astype(jnp.bfloat16)


def fold_rows(value):
    return jnp.sum(value.reshape(value.shape[0] // 8, 8, value.shape[1]), 0)


def gelu_terms(gate):
    cdf = 0.5 * (1.0 + lax.erf(gate * 0.7071067811865476))
    density = jnp.exp(-0.5 * gate * gate) * 0.3989422804014327
    return gate * cdf, cdf + gate * density


def when(condition):
    if isinstance(condition, bool):
        return (lambda body: body()) if condition else (lambda body: None)
    return pl.when(condition)


def both(value):
    return value.reshape(512, value.shape[-1])


def layers_kernel(
    short_lens, long_lens, tokens, cotangent, w_qkv, w_out, w_gate_up, w_down, gains, biases,
    boundary, o_qkv, o_out, o_gu, o_dn, o_vec,
    wq, wo, wg, wd, x_s, g_s, qkv_s, p_s, mixed_s, nl_s, low_s, n1_s, n2_s, r1_s, r2_s, gu_s, ht_s,
    gf_s, ga_s, send_s, out_s, acc_s, f_s, gate_s, up_s, dist_s, vec_s,
    peer_n, peer_h, peer_f, peer_g,
    own, ra_relay, ra_fin, sa, own_b, rb_relay, rb_fin, sb, x_send, x_keep, x_recv, c_tmp, c_send, c_keep, c_recv,
    v_acc, v_recv,
    w_sem, x_sem, g_sem, out_sem, f_send, f_recv, b_send, b_recv, pair_send, pair_recv,
    a_send, a_relay_recv, a_fin_recv, a2_send,
    bb_send, bb_relay_recv, bb_fin_recv, b2_send,
    xs_sem, xr_sem, cs_sem, cr_sem, vs_sem, vr_sem,
):
    sec = lax.axis_index("section")
    first = sec == 0
    second = sec == 1
    me = lax.axis_index("dp")
    core = me % 2
    xhi = (me // 2) % 2
    zz = (me // 4) % 4
    yy = me // 16
    other = 1 - core

    def dev(y, z, x, c):
        return ((y * 4 + z) * 2 + x) * 2 + c

    peer_core = dev(yy, zz, xhi, other)
    peer_x = dev(yy, zz, 1 - xhi, core)
    y_ids = [dev((yy + k) % 4, zz, xhi, core) for k in (1, 2, 3)]
    z_ids = [dev(yy, (zz + k) % 4, xhi, core) for k in (1, 2, 3)]

    def remote(src, dst, send, recv, target):
        return pltpu.make_async_remote_copy(
            src_ref=src, dst_ref=dst, send_sem=send, recv_sem=recv,
            device_id={"dp": target}, device_id_type=MESH_IDS,
        )

    def across(src, dst, send, recv):
        return pltpu.make_async_remote_copy(
            src_ref=src, dst_ref=dst, send_sem=send, recv_sem=recv,
            device_id={"section": 1 - sec}, device_id_type=MESH_IDS,
        )

    w_copies = [
        pltpu.make_async_copy(w_qkv, wq, w_sem.at[0]),
        pltpu.make_async_copy(w_out, wo, w_sem.at[1]),
        pltpu.make_async_copy(w_gate_up, wg, w_sem.at[2]),
        pltpu.make_async_copy(w_down, wd, w_sem.at[3]),
    ]

    def token_copy(m):
        return pltpu.make_async_copy(tokens.at[m], x_s.at[m], x_sem.at[m])

    def cot_copy(m):
        return pltpu.make_async_copy(cotangent.at[m], g_s.at[m], g_sem.at[m])

    def hand_on(m):
        return across(send_s.at[m], x_s.at[m], f_send.at[m], f_recv.at[m])

    def hand_back(m):
        return across(send_s.at[m], g_s.at[m], b_send.at[m], b_recv.at[m])

    def out_copy(m):
        return pltpu.make_async_copy(out_s, boundary.at[m], out_sem.at[m])

    def pair(k, m):
        rows = pl.ds(m * 256, 256)
        src, dst = (
            lambda: (nl_s.at[m], peer_n.at[m]),
            lambda: (ht_s.at[m, :, other], peer_h.at[m]),
            lambda: (gf_s.at[m], peer_f.at[m]),
            lambda: (gu_s.at[m, :, pl.ds(other * FF, FF)], peer_g.at[m]),
            lambda: (x_s.at[m], wg.at[rows, pl.ds(0, 768)]),
            lambda: (mixed_s.at[m], wg.at[rows, pl.ds(768, 768)]),
            lambda: (qkv_s.at[m, :, pl.ds(other * 1152, 1152)], wg.at[rows, pl.ds(1536, 1152)]),
            lambda: (ga_s.at[m, :, pl.ds(other * 384, 384)], wg.at[rows, pl.ds(2688, 384)]),
        )[k]()
        return remote(src, dst, pair_send.at[k, m], pair_recv.at[k, m], peer_core)

    def pair_wait(*which):
        for k in which:
            for m in range(2):
                pair(k, m).wait()

    @pl.when(first)
    def _():
        token_copy(0).start()

    w_copies[0].start()
    w_copies[1].start()

    barrier = pltpu.get_barrier_semaphore()
    pl.semaphore_signal(barrier, inc=1, device_id={"section": 1 - sec}, device_id_type=MESH_IDS)
    for target in [peer_core, peer_x] + y_ids + z_ids:
        pl.semaphore_signal(barrier, inc=1, device_id={"dp": target}, device_id_type=MESH_IDS)
    pl.semaphore_wait(barrier, 9)

    vec_s[...] = jnp.zeros_like(vec_s)
    rows_j = lax.broadcasted_iota(jnp.int32, (256, 256), 0)
    cols_i = lax.broadcasted_iota(jnp.int32, (256, 256), 1)
    distance = f32(jnp.abs(rows_j - cols_i))
    length_a, length_b, length_long = short_lens[0], short_lens[1], long_lens[0]
    for m in range(2):
        if m == 0:
            limit = jnp.where(rows_j < 128, length_a, length_b + 128)
            apart = jnp.where((rows_j >> 7) == (cols_i >> 7), 0, 1024)
            ok = rows_j + apart < limit
        else:
            ok = rows_j < length_long
        dist_s[m] = jnp.where(ok, distance, masked_distance)

    w_copies[0].wait()
    w_copies[2].start()
    w_copies[3].start()

    @pl.when(first)
    def _():
        token_copy(1).start()

    @pl.when(second)
    def _():
        cot_copy(0).start()
        cot_copy(1).start()


    def v_sends(stage):
        targets = ([peer_core], [peer_x], y_ids, z_ids)[stage]
        base = (0, 1, 2, 5)[stage]
        count = len(targets)
        return [
            remote(
                v_acc.at[stage], v_recv.at[base + (count - 1 - k)],
                vs_sem.at[base + k], vr_sem.at[base + (count - 1 - k)], targets[k],
            )
            for k in range(count)
        ]

    def v_start(stage):
        for copy in v_sends(stage):
            copy.start()

    def v_finish(stage):
        base = (0, 1, 2, 5)[stage]
        copies = v_sends(stage)
        for copy in copies:
            copy.wait_send()
        for copy in copies:
            copy.wait_recv()
        total = v_acc[stage]
        for k in range(len(copies)):
            total = total + v_recv[base + k]
        v_acc[stage + 1] = total

    def ring(par):
        right = y_ids[0] * (1 - par) + z_ids[0] * par
        left = y_ids[2] * (1 - par) + z_ids[2] * par
        place = yy * (1 - par) + zz * par
        return right, left, place

    def a1_copies(j):
        slot, mine = j % SLOTS, j % OWN_SLOTS
        right, left, p = ring(j % 2)
        far, nxt, prv = (p + 2) % 4, (p + 1) % 4, (p + 3) % 4
        return (
            remote(own.at[mine, 0, far], ra_relay.at[slot, 0], a_send.at[slot, 0], a_relay_recv.at[slot, 0], right),
            remote(own.at[mine, 1, far], ra_relay.at[slot, 1], a_send.at[slot, 1], a_relay_recv.at[slot, 1], left),
            remote(own.at[mine, 1, nxt], ra_fin.at[slot, 0, 1], a_send.at[slot, 2], a_fin_recv.at[slot, 0, 1], right),
            remote(own.at[mine, 0, prv], ra_fin.at[slot, 1, 0], a_send.at[slot, 3], a_fin_recv.at[slot, 1, 0], left),
        )

    def a2_copies(j):
        slot, mine = j % SLOTS, j % 2
        right, left, _ = ring(j % 2)
        return (
            remote(sa.at[mine, 0], ra_fin.at[slot, 0, 0], a2_send.at[mine, 0], a_fin_recv.at[slot, 0, 0], right),
            remote(sa.at[mine, 1], ra_fin.at[slot, 1, 1], a2_send.at[mine, 1], a_fin_recv.at[slot, 1, 1], left),
        )

    def b1_copies(j):
        slot, mine = j % SLOTS, j % OWN_SLOTS
        right, left, p = ring(1 - j % 2)
        far, nxt, prv = (p + 2) % 4, (p + 1) % 4, (p + 3) % 4
        return (
            remote(own_b.at[mine, 0, far], rb_relay.at[slot, 0], bb_send.at[slot, 0], bb_relay_recv.at[slot, 0], right),
            remote(own_b.at[mine, 1, far], rb_relay.at[slot, 1], bb_send.at[slot, 1], bb_relay_recv.at[slot, 1], left),
            remote(own_b.at[mine, 1, nxt], rb_fin.at[slot, 0, 1], bb_send.at[slot, 2], bb_fin_recv.at[slot, 0, 1], right),
            remote(own_b.at[mine, 0, prv], rb_fin.at[slot, 1, 0], bb_send.at[slot, 3], bb_fin_recv.at[slot, 1, 0], left),
        )

    def b2_copies(j):
        slot, mine = j % SLOTS, j % 2
        right, left, _ = ring(1 - j % 2)
        return (
            remote(sb.at[mine, 0], rb_fin.at[slot, 0, 0], b2_send.at[mine, 0], bb_fin_recv.at[slot, 0, 0], right),
            remote(sb.at[mine, 1], rb_fin.at[slot, 1, 1], b2_send.at[mine, 1], bb_fin_recv.at[slot, 1, 1], left),
        )

    def x_copy(j):
        slot, mine = j % SLOTS, j % 2
        return remote(x_send.at[mine], x_recv.at[slot], xs_sem.at[mine], xr_sem.at[slot], peer_x)

    def c_copy(j):
        slot, mine = j % SLOTS, j % 2
        return remote(c_send.at[mine], c_recv.at[slot], cs_sem.at[mine], cr_sem.at[slot], peer_core)

    def place_rows(j, piece):
        mine = j % OWN_SLOTS
        par = j % 2
        for y in range(4):
            for z in range(4):
                i1 = y * (1 - par) + z * par
                i2 = z * (1 - par) + y * par
                for x in range(2):
                    own[mine, x, i1, i2] = bf16(piece(y * 4 + z, x))

    def place_regular(j, result):
        def piece(block, x):
            rows = result[block * 48 + x * 24:block * 48 + x * 24 + 24]
            return jnp.concatenate([rows[:, :256], rows[:, 256:]], 0)

        place_rows(j, piece)

    def compute(j):
        @when(j < N_DOWN)
        def _():
            @when(j == 0)
            def _():
                pair_wait(1, 2)

            cols = pl.ds(pl.multiple_of(j * 256, 256), 256) if not isinstance(j, int) else pl.ds(j * 256, 256)
            result = None
            for m in range(2):
                for left, right in ((ht_s[m, :, core], gf_s[m, :, cols]), (peer_h[m], peer_f[m, :, cols])):
                    term = dot_nn(left.reshape(1536, 256), right)
                    result = term if result is None else result + term
            place_rows(j, lambda block, x: result[(block * 2 + x) * 48:(block * 2 + x + 1) * 48])

        @when((j >= N_DOWN) & (j < N_DOWN + 6))
        def _():
            @when(j == N_DOWN)
            def _():
                pair_wait(0, 3)
                for k in (4, 5, 6, 7):
                    for m in range(2):
                        pair(k, m).start()

            column = pl.multiple_of((j - N_DOWN) * 512, 512)
            mine = gu_s[:, :, pl.ds(pl.multiple_of(core * FF + column, 512), 512)]
            place_regular(j, dot_tn(both(nl_s[...]), both(mine)) + dot_tn(both(peer_n[...]), both(peer_g[:, :, pl.ds(column, 512)])))

        def qkv_part(column, width):
            mine = qkv_s[:, :, pl.ds(pl.multiple_of(core * 1152 + column, 128), width)]
            far = wg[0:512, pl.ds(pl.multiple_of(1536 + column, 128), width)]
            return dot_tn(both(x_s[...]), both(mine)) + dot_tn(wg[0:512, 0:768], far)

        @when((j >= N_DOWN + 6) & (j < N_DOWN + 8))
        def _():
            @when(j == N_DOWN + 6)
            def _():
                pair_wait(4, 5, 6, 7)

            place_regular(j, qkv_part((j - N_DOWN - 6) * 512, 512))

        @when(j == N_DOWN + 8)
        def _():
            mine = ga_s[:, :, pl.ds(pl.multiple_of(core * 384, 128), 384)]
            out_part = dot_tn(both(mixed_s[...]), both(mine)) + dot_tn(wg[0:512, 768:1536], wg[0:512, 2688:3072])
            place_regular(j, jnp.concatenate([qkv_part(1024, 128), out_part], 1))

    def step(i, carry):
        @when(i < N_CHUNKS)
        def _():
            compute(i)
            for copy in a1_copies(i):
                copy.start()

        j1 = i - 1

        @when((j1 >= 0) & (j1 < N_CHUNKS))
        def _():
            slot, mine, buf = j1 % SLOTS, j1 % OWN_SLOTS, j1 % 2
            _, _, p = ring(j1 % 2)
            before = a1_copies(j1)
            after = a2_copies(j1)
            before[0].wait_recv()
            sa[buf, 0] = bf16(f32(own[mine, 0, (p + 1) % 4]) + f32(ra_relay[slot, 0]))
            after[0].start()
            before[1].wait_recv()
            sa[buf, 1] = bf16(f32(own[mine, 1, (p + 3) % 4]) + f32(ra_relay[slot, 1]))
            after[1].start()

        j2 = i - 2

        @when((j2 >= 0) & (j2 < N_CHUNKS))
        def _():
            slot, mine = j2 % SLOTS, j2 % OWN_SLOTS
            _, _, p = ring(j2 % 2)
            before = a1_copies(j2)
            after = a2_copies(j2)
            for copy in before + after:
                copy.wait_send()
            for copy in before[2:] + after:
                copy.wait_recv()
            for h in range(2):
                own_b[mine, h] = bf16(f32(own[mine, h, p]) + f32(ra_fin[slot, 0, h]) + f32(ra_fin[slot, 1, h]))
            for copy in b1_copies(j2):
                copy.start()

        j3 = i - 3

        @when((j3 >= 0) & (j3 < N_CHUNKS))
        def _():
            slot, mine, buf = j3 % SLOTS, j3 % OWN_SLOTS, j3 % 2
            _, _, p = ring(1 - j3 % 2)
            before = b1_copies(j3)
            after = b2_copies(j3)
            before[0].wait_recv()
            sb[buf, 0] = bf16(f32(own_b[mine, 0, (p + 1) % 4]) + f32(rb_relay[slot, 0]))
            after[0].start()
            before[1].wait_recv()
            sb[buf, 1] = bf16(f32(own_b[mine, 1, (p + 3) % 4]) + f32(rb_relay[slot, 1]))
            after[1].start()

        j4 = i - 4

        @when((j4 >= 0) & (j4 < N_CHUNKS))
        def _():
            slot, mine, buf = j4 % SLOTS, j4 % OWN_SLOTS, j4 % 2
            _, _, p = ring(1 - j4 % 2)
            before = b1_copies(j4)
            after = b2_copies(j4)
            for copy in before + after:
                copy.wait_send()
            for copy in before[2:] + after:
                copy.wait_recv()
            total = [f32(own_b[mine, h, p]) + f32(rb_fin[slot, 0, h]) + f32(rb_fin[slot, 1, h]) for h in range(2)]
            x_send[buf] = jnp.where(xhi == 0, total[1], total[0])
            x_keep[buf] = jnp.where(xhi == 0, total[0], total[1])
            x_copy(j4).start()

        j5 = i - 5

        @when((j5 >= 0) & (j5 < N_CHUNKS))
        def _():
            slot, buf = j5 % SLOTS, j5 % 2
            x_copy(j5).wait()

            @when(j5 < N_DOWN)
            def _():
                cols = pl.ds(pl.multiple_of(j5 * 256, 256), 256)
                o_dn[:, cols] = x_keep[buf] + x_recv[slot]

            @when(j5 >= N_DOWN)
            def _():
                c_tmp[...] = x_keep[buf] + x_recv[slot]
                for h in range(2):
                    upper, lower = c_tmp[24 * h:24 * h + 12], c_tmp[24 * h + 12:24 * h + 24]
                    c_send[buf, h, 0:12] = jnp.where(core == 0, lower, upper)
                    c_keep[buf, h, 0:12] = jnp.where(core == 0, upper, lower)
                c_copy(j5).start()

        j6 = i - 6

        @when((j6 >= N_DOWN) & (j6 < N_CHUNKS))
        def _():
            slot, buf = j6 % SLOTS, j6 % 2
            c_copy(j6).wait()
            for source, at, who in ((c_keep, buf, core), (c_recv, slot, other)):
                @when(j6 < N_DOWN + 6)
                def _():
                    for h in range(2):
                        column = pl.multiple_of(who * FF + (j6 - N_DOWN) * 512 + h * 256, 256)
                        o_gu[:, 0, pl.ds(column, 256)] = source[at, h, 0:12]

                @when((j6 >= N_DOWN + 6) & (j6 < N_DOWN + 8))
                def _():
                    for h in range(2):
                        column = pl.multiple_of(who * 1152 + (j6 - N_DOWN - 6) * 512 + h * 256, 128)
                        o_qkv[:, 0, pl.ds(column, 256)] = source[at, h, 0:12]

                @when(j6 == N_DOWN + 8)
                def _():
                    o_qkv[:, 0, pl.ds(pl.multiple_of(who * 1152 + 1024, 128), 128)] = source[at, 0, 0:12, 0:128]
                    o_out[:, 0, pl.ds(pl.multiple_of(who * 384, 128), 128)] = source[at, 0, 0:12, 128:256]
                    o_out[:, 0, pl.ds(pl.multiple_of(who * 384 + 128, 128), 256)] = source[at, 1, 0:12]

        return carry


    def band(k):
        return pl.ds(k * BAND, BAND)

    def normalise(value):
        average = jnp.mean(value, -1, keepdims=True)
        centred = value - average
        inverse = lax.rsqrt(jnp.mean(centred * centred, -1, keepdims=True) + epsilon)
        return centred * inverse, inverse

    lanes = lax.broadcasted_iota(jnp.int32, (256, 128), 1)

    def own_lanes(e):
        return (lanes < 64) if e == 0 else (lanes >= 64)

    def forward(m, carry):
        @pl.when(first)
        def _():
            token_copy(m).wait()

        @pl.when(second)
        def _():
            hand_on(m).wait_recv()

        x = x_s[m]
        query = dot_nn(x, wq[:, 0:768]) + biases[0]
        qkv_s[m, :, 0:768] = bf16(f32(bf16(query)) * 0.125)
        qkv_s[m, :, 768:1536] = bf16(dot_nn(x, wq[:, 768:1536]))
        qkv_s[m, :, 1536:2304] = bf16(dot_nn(x, wq[:, 1536:2304]) + biases[1])

        for hp in range(6):
            at = pl.ds(hp * 128, 128)
            q2 = qkv_s[m, :, at]
            k2 = qkv_s[m, :, pl.ds(hp * 128 + 768, 128)]
            v2 = qkv_s[m, :, pl.ds(hp * 128 + 1536, 128)]
            none = jnp.zeros_like(q2)
            qs = jnp.concatenate([jnp.where(own_lanes(e), q2, none) for e in range(2)], 0)
            vs = jnp.concatenate([jnp.where(own_lanes(e), v2, none) for e in range(2)], 0)
            scores_two = dot_nt(k2, qs)
            probs_two = []
            for e in range(2):
                head = 2 * hp + e
                scores = scores_two[:, 256 * e:256 * e + 256] - 2.0 ** (-8.0 * (head + 1) / HEADS) * dist_s[m]
                expo = jnp.exp(scores - jnp.max(scores, 0, keepdims=True))
                probs = bf16(expo * (1.0 / jnp.sum(expo, 0, keepdims=True)))
                p_s[m, head] = probs
                probs_two.append(probs)
            mixed_s[m, :, at] = bf16(dot_tn(jnp.concatenate(probs_two, 0), vs))

        @pl.when(m == 0)
        def _():
            w_copies[1].wait()

        acc_s[...] = dot_nn(mixed_s[m], wo[...])
        for k in range(256 // BAND):
            r = band(k)
            value = f32(x_s[m, r]) + (acc_s[r] + biases[2])
            unit, inverse = normalise(value)
            normed = unit * gains[0:1] + biases[3]
            n1_s[m, r] = bf16(unit)
            r1_s[m, r] = inverse
            f_s[r] = normed
            nl_s[m, r] = bf16(normed)

        pair(0, m).start()

        @pl.when(m == 0)
        def _():
            w_copies[2].wait()
            w_copies[3].wait()

        for jb in range(FF // BLOCK):
            c0 = jb * BLOCK
            low = nl_s[m]
            gate_s[...] = dot_nn(low, wg[:, c0:c0 + BLOCK])
            up_s[...] = dot_nn(low, wg[:, c0 + FF:c0 + FF + BLOCK])
            for k in range(256 // BAND):
                r = band(k)
                gate, up = gate_s[r], up_s[r]
                act, slope = gelu_terms(gate)
                gu_s[m, r, c0:c0 + BLOCK] = bf16(up * slope)
                gu_s[m, r, c0 + FF:c0 + FF + BLOCK] = bf16(act)
                gate_s[r] = act * up
            hid = bf16(gate_s[...])
            ht_s[m, 8 * jb:8 * jb + 8] = hid.T.reshape(8, 2, 48, 256)
            term = dot_nn(hid, wd[c0:c0 + BLOCK])
            if jb == 0:
                acc_s[...] = term
            else:
                acc_s[...] += term

        @pl.when(second & (m == 1))
        def _():
            out_copy(0).wait()

        for k in range(256 // BAND):
            r = band(k)
            value = f_s[r] + (acc_s[r] + biases[4])
            unit, inverse = normalise(value)
            n2_s[m, r] = bf16(unit)
            r2_s[m, r] = inverse
            result = unit * gains[1:2] + biases[5]
            out_s[r] = result
            send_s[m, r] = bf16(result)

        @pl.when(first)
        def _():
            hand_on(m).start()

        @pl.when(second)
        def _():
            out_copy(m).start()

        pair(1, m).start()
        return carry

    lax.fori_loop(0, 2, forward, 0)

    def norm_back(grad, unit, inverse, gain):
        scaled = grad * gain
        mean_one = jnp.mean(scaled, -1, keepdims=True)
        mean_two = jnp.mean(scaled * unit, -1, keepdims=True)
        return inverse * (scaled - mean_one - unit * mean_two)

    def backward(m, carry):
        early = first & (m == 1)

        @pl.when(first)
        def _():
            hand_on(m).wait_send()
            hand_back(m).wait_recv()

        @pl.when(second)
        def _():
            cot_copy(m).wait()

        for k in range(256 // BAND):
            r = band(k)
            row = lax.broadcasted_iota(jnp.int32, (BAND, 1), 0) + k * BAND
            limit = jnp.where(m == 0, jnp.where(row < 128, length_a, length_b + 128), length_long)
            live = jnp.where((row < limit) | first, 1.0, 0.0)
            grad = f32(g_s[m, r]) * live
            unit = f32(n2_s[m, r])
            vec_s[1] += fold_rows(grad * unit)
            vec_s[7] += fold_rows(grad)
            grad_in = norm_back(grad, unit, r2_s[m, r], gains[1:2])
            f_s[r] = grad_in
            low = bf16(grad_in)
            gf_s[m, r] = low
            vec_s[6] += fold_rows(f32(low))

        pair(2, m).start()

        for jb in range(FF // BLOCK):
            c0 = jb * BLOCK
            gate_s[...] = dot_nt(gf_s[m], wd[c0:c0 + BLOCK])
            for k in range(256 // BAND):
                r = band(k)
                hid = gate_s[r]
                for c in (c0, c0 + FF):
                    gu_s[m, r, c:c + BLOCK] = bf16(hid * f32(gu_s[m, r, c:c + BLOCK]))
            term = dot_nt(gu_s[m, :, c0:c0 + BLOCK], wg[:, c0:c0 + BLOCK])
            term = term + dot_nt(gu_s[m, :, c0 + FF:c0 + FF + BLOCK], wg[:, c0 + FF:c0 + FF + BLOCK])
            if jb == 0:
                acc_s[...] = term
            else:
                acc_s[...] += term
            if jb == 1:
                @pl.when(early)
                def _():
                    step(0, 0)

        pair(3, m).start()

        @pl.when(early)
        def _():
            step(1, 0)

        for k in range(256 // BAND):
            r = band(k)
            grad = acc_s[r] + f_s[r]
            unit = f32(n1_s[m, r])
            vec_s[0] += fold_rows(grad * unit)
            vec_s[5] += fold_rows(grad)
            grad_in = norm_back(grad, unit, r1_s[m, r], gains[0:1])
            f_s[r] = grad_in
            low = bf16(grad_in)
            ga_s[m, r] = low
            vec_s[4] += fold_rows(f32(low))

        def mixed_back(g):
            c = g * 256
            low_s[:, c:c + 256] = bf16(dot_nt(ga_s[m], wo[c:c + 256]))

        def attend_back(hp):
            at = pl.ds(hp * 128, 128)
            q2 = qkv_s[m, :, at]
            k2 = qkv_s[m, :, pl.ds(hp * 128 + 768, 128)]
            v2 = qkv_s[m, :, pl.ds(hp * 128 + 1536, 128)]
            do2 = low_s[:, at]
            none = jnp.zeros_like(q2)
            qs, ks, ds = (
                jnp.concatenate([jnp.where(own_lanes(e), wide, none) for e in range(2)], 0) for wide in (q2, k2, do2)
            )
            grad_probs_two = dot_nt(v2, ds)
            probs_two = [p_s[m, 2 * hp + e] for e in range(2)]
            scores_two = []
            for e in range(2):
                weighted = f32(probs_two[e]) * grad_probs_two[:, 256 * e:256 * e + 256]
                total = jnp.sum(weighted, 0, keepdims=True)
                scores_two.append(bf16(weighted - f32(probs_two[e]) * total))
            grad_v = bf16(dot_nn(jnp.concatenate(probs_two, 1), ds))
            grad_k = bf16(dot_nn(jnp.concatenate(scores_two, 1), qs))
            grad_q = bf16(dot_tn(jnp.concatenate(scores_two, 0), ks) * 0.125)
            vec_s[2, :, at] += fold_rows(f32(grad_q))
            vec_s[3, :, at] += fold_rows(f32(grad_v))
            qkv_s[m, :, at] = grad_q
            qkv_s[m, :, pl.ds(hp * 128 + 768, 128)] = grad_k
            qkv_s[m, :, pl.ds(hp * 128 + 1536, 128)] = grad_v

        mixed_back(0)
        for g in range(3):
            if g < 2:
                mixed_back(g + 1)
            attend_back(2 * g)
            attend_back(2 * g + 1)
            c = g * 256
            term = dot_nt(qkv_s[m, :, c:c + 256], wq[:, c:c + 256])
            for c in (g * 256 + 768, g * 256 + 1536):
                term = term + dot_nt(qkv_s[m, :, c:c + 256], wq[:, c:c + 256])
            if g == 0:
                acc_s[...] = term
            else:
                acc_s[...] += term

        @pl.when(early)
        def _():
            step(2, 0)

        @pl.when(first & (m == 1))
        def _():
            out_copy(0).wait()

        grad_a = acc_s[...] + f_s[...]

        @pl.when(second)
        def _():
            send_s[m] = bf16(grad_a)
            hand_back(m).start()

        @pl.when(first)
        def _():
            out_s[...] = grad_a
            out_copy(m).start()

        return carry

    lax.fori_loop(0, 2, backward, 0)
    for k in range(8):
        v_acc[0, k:k + 1] = jnp.sum(vec_s[k], 0, keepdims=True)
    v_start(0)

    def tail_step(i, carry):
        step(i, carry)
        for stage in range(4):
            @pl.when(i == 2 * stage + 5)
            def _():
                v_finish(stage)
                if stage < 3:
                    v_start(stage + 1)

        return carry

    lax.fori_loop(3 * (1 - sec), N_CHUNKS + 6, tail_step, 0)
    o_vec[...] = v_acc[4]

    @pl.when(second)
    def _():
        hand_back(0).wait_send()
        hand_back(1).wait_send()

    out_copy(1).wait()


def run_layers(short_lens, long_lens, tokens, cotangent, w_qkv, w_out, w_gate_up, w_down, gains, biases):
    low, wide = jnp.bfloat16, jnp.float32
    hbm = pl.BlockSpec(memory_space=pl.ANY)
    vmem = pl.BlockSpec(memory_space=pltpu.VMEM)
    smem = pl.BlockSpec(memory_space=pltpu.SMEM)
    dma = pltpu.SemaphoreType.DMA
    of = pltpu.VMEM
    s = SLOTS
    return pl.pallas_call(
        layers_kernel,
        out_shape=[
            jax.ShapeDtypeStruct((2, 256, 768), wide),
            jax.ShapeDtypeStruct((12, 1, 2304), wide),
            jax.ShapeDtypeStruct((12, 1, 768), wide),
            jax.ShapeDtypeStruct((12, 1, 6144), wide),
            jax.ShapeDtypeStruct((48, 768), wide),
            jax.ShapeDtypeStruct((8, 768), wide),
        ],
        in_specs=[smem] * 2 + [hbm] * 6 + [vmem] * 2,
        out_specs=[hbm] + [vmem] * 5,
        scratch_shapes=[
            of((768, 2304), low), of((768, 768), low), of((768, 6144), low), of((3072, 768), low),
            of((2, 256, 768), low), of((2, 256, 768), low), of((2, 256, 2304), low), of((2, 12, 256, 256), low),
            of((2, 256, 768), low), of((2, 256, 768), low), of((256, 768), low),
            of((2, 256, 768), low), of((2, 256, 768), low),
            of((2, 256, 1), wide), of((2, 256, 1), wide), of((2, 256, 6144), low), of((2, 32, 2, 48, 256), low),
            of((2, 256, 768), low), of((2, 256, 768), low), of((2, 256, 768), low), of((256, 768), wide),
            of((256, 768), wide), of((256, 768), wide), of((256, BLOCK), wide), of((256, BLOCK), wide),
            of((2, 256, 256), wide), of((8, 8, 768), wide),
            of((2, 256, 768), low), of((2, 32, 48, 256), low), of((2, 256, 768), low), of((2, 256, 3072), low),
            of((OWN_SLOTS, 2, 4, 4, 48, 256), low),
            of((s, 2, 4, 48, 256), low), of((s, 2, 2, 4, 48, 256), low), of((2, 2, 4, 48, 256), low),
            of((OWN_SLOTS, 2, 4, 48, 256), low),
            of((s, 2, 48, 256), low), of((s, 2, 2, 48, 256), low), of((2, 2, 48, 256), low),
            of((2, 48, 256), wide), of((2, 48, 256), wide), of((s, 48, 256), wide),
            of((48, 256), wide), of((2, 2, 16, 256), wide), of((2, 2, 16, 256), wide), of((s, 2, 16, 256), wide),
            of((5, 8, 768), wide), of((8, 8, 768), wide),
            dma((4,)), dma((2,)), dma((2,)), dma((2,)), dma((2,)), dma((2,)), dma((2,)), dma((2,)),
            dma((8, 2)), dma((8, 2)),
            dma((s, 4)), dma((s, 2)), dma((s, 2, 2)), dma((2, 2)),
            dma((s, 4)), dma((s, 2)), dma((s, 2, 2)), dma((2, 2)),
            dma((2,)), dma((s,)), dma((2,)), dma((s,)), dma((8,)), dma((8,)),
        ],
        compiler_params=pltpu.CompilerParams(
            collective_id=0, has_side_effects=True, vmem_limit_bytes=VMEM_LIMIT
        ),
        cost_estimate=pl.CostEstimate(flops=3 * 10 ** 10, bytes_accessed=4 * 10 ** 7, transcendentals=10 ** 7),
        name="run_layers",
    )(short_lens, long_lens, tokens, cotangent, w_qkv, w_out, w_gate_up, w_down, gains, biases)


def place_kernel(start, boundary, qkv, out, gate_up, down, vec, o_b, o_q, o_o, o_g, o_d, o_gains, o_biases, sems):
    copies = [
        pltpu.make_async_copy(source, target, sems.at[k])
        for k, (source, target) in enumerate(
            ((boundary, o_b.at[0]), (gate_up, o_g), (qkv, o_q), (out, o_o), (down, o_d.at[0]))
        )
    ]
    for copy in copies:
        copy.start()
    mine = pltpu.roll(vec[...], lax.rem(D - start[0], D), axis=1)
    o_gains[0] = mine[:2, :12]
    o_biases[:, 0] = mine[2:, :12]
    for copy in copies:
        copy.wait()


def place(start, boundary, qkv, out, gate_up, down, vec):
    wide = jnp.float32
    vmem = pl.BlockSpec(memory_space=pltpu.VMEM)
    return pl.pallas_call(
        place_kernel,
        out_shape=[
            jax.ShapeDtypeStruct((1, 2, 256, 768), wide),
            jax.ShapeDtypeStruct((12, 1, 2304), wide),
            jax.ShapeDtypeStruct((12, 1, 768), wide),
            jax.ShapeDtypeStruct((12, 1, 6144), wide),
            jax.ShapeDtypeStruct((1, 48, 768), wide),
            jax.ShapeDtypeStruct((1, 2, 12), wide),
            jax.ShapeDtypeStruct((6, 1, 12), wide),
        ],
        in_specs=[pl.BlockSpec(memory_space=pltpu.SMEM)] + [pl.BlockSpec(memory_space=pltpu.HBM)] * 5 + [vmem],
        out_specs=[vmem] * 7,
        scratch_shapes=[pltpu.SemaphoreType.DMA((5,))],
        compiler_params=pltpu.CompilerParams(vmem_limit_bytes=32 * 1024 * 1024),
        name="place",
    )(start, boundary, qkv, out, gate_up, down, vec)


def on_device(
    tokens, cotangent, short_lens, long_lens, w_qkv, w_out, w_gate_up, w_down, gains, biases
):
    boundary, q, o, g, d, vec = run_layers(
        short_lens, long_lens, tokens, cotangent, w_qkv[0], w_out[0], w_gate_up[0], w_down[0], gains[0],
        jnp.transpose(biases, (1, 0, 2)),
    )
    start = jnp.full((1,), lax.axis_index("dp") * 12, jnp.int32)
    b, q, o, g, d, gains_out, biases_out = place(start, boundary, q, o, g, d, vec)
    q, o, g, biases_out = (jnp.transpose(rows, (1, 0, 2)) for rows in (q, o, g, biases_out))
    return (b, q, o, g, d, gains_out, biases_out)


def solution(mesh):
    placed = (
        P(None, "dp", None),
        P(None, "dp", None),
        P("dp"),
        P("dp"),
        P("section", None, None),
        P("section", None, None),
        P("section", None, None),
        P("section", None, None),
        P("section", None, None),
        P("section", None, None),
    )
    return jax.shard_map(
        on_device,
        mesh=mesh,
        in_specs=placed,
        out_specs=(
            P("section", None, "dp", None),
            P("section", "dp", None),
            P("section", "dp", None),
            P("section", "dp", None),
            P("section", "dp", None),
            P("section", None, "dp"),
            P("section", None, "dp"),
        ),
        check_vma=False,
    )
```

```python
import jax
import jax.numpy as jnp
from jax import lax
from jax.experimental import pallas as pl
from jax.experimental.pallas import tpu as pltpu
from jax.sharding import PartitionSpec as P

D = 768
HEADS = 12
FF = 3072
BLOCK = 768
BAND = 32
N_CHUNKS = 12
N_DOWN = 3
SLOTS = 5
OWN_SLOTS = 3
VMEM_LIMIT = 62 * 1024 * 1024
MESH_IDS = pl.DeviceIdType.MESH

epsilon = 1e-05
masked_distance = 1e12


def dot_nn(lhs, rhs):
    return jnp.dot(lhs, rhs, preferred_element_type=jnp.float32)


def dot_nt(lhs, rhs):
    return lax.dot_general(lhs, rhs, (((1,), (1,)), ((), ())), preferred_element_type=jnp.float32)


def dot_tn(lhs, rhs):
    return lax.dot_general(lhs, rhs, (((0,), (0,)), ((), ())), preferred_element_type=jnp.float32)


def f32(value):
    return value.astype(jnp.float32)


def bf16(value):
    return value.astype(jnp.bfloat16)


def fold_rows(value):
    return jnp.sum(value.reshape(value.shape[0] // 8, 8, value.shape[1]), 0)


def gelu_terms(gate):
    cdf = 0.5 * (1.0 + lax.erf(gate * 0.7071067811865476))
    density = jnp.exp(-0.5 * gate * gate) * 0.3989422804014327
    return gate * cdf, cdf + gate * density


def when(condition):
    if isinstance(condition, bool):
        return (lambda body: body()) if condition else (lambda body: None)
    return pl.when(condition)


def both(value):
    return value.reshape(512, value.shape[-1])


def layers_kernel(
    short_lens, long_lens, tokens, cotangent, w_qkv, w_out, w_gate_up, w_down, gains, biases,
    boundary, o_qkv, o_out, o_gu, o_dn, o_vec,
    wq, wo, wg, wd, x_s, g_s, qkv_s, p_s, mixed_s, nl_s, low_s, n1_s, n2_s, r1_s, r2_s, gu_s, ht_s,
    gf_s, ga_s, send_s, out_s, acc_s, f_s, gate_s, up_s, dist_s, vec_s,
    peer_n, peer_h, peer_f, peer_g,
    own, ra_relay, ra_fin, sa, own_b, rb_relay, rb_fin, sb, x_send, x_keep, x_recv, c_tmp, c_send, c_keep, c_recv,
    v_acc, v_recv,
    w_sem, x_sem, g_sem, out_sem, f_send, f_recv, b_send, b_recv, pair_send, pair_recv,
    a_send, a_relay_recv, a_fin_recv, a2_send,
    bb_send, bb_relay_recv, bb_fin_recv, b2_send,
    xs_sem, xr_sem, cs_sem, cr_sem, vs_sem, vr_sem,
):
    sec = lax.axis_index("section")
    first = sec == 0
    second = sec == 1
    me = lax.axis_index("dp")
    core = me % 2
    xhi = (me // 2) % 2
    zz = (me // 4) % 4
    yy = me // 16
    other = 1 - core

    def dev(y, z, x, c):
        return ((y * 4 + z) * 2 + x) * 2 + c

    peer_core = dev(yy, zz, xhi, other)
    peer_x = dev(yy, zz, 1 - xhi, core)
    y_ids = [dev((yy + k) % 4, zz, xhi, core) for k in (1, 2, 3)]
    z_ids = [dev(yy, (zz + k) % 4, xhi, core) for k in (1, 2, 3)]

    def remote(src, dst, send, recv, target):
        return pltpu.make_async_remote_copy(
            src_ref=src, dst_ref=dst, send_sem=send, recv_sem=recv,
            device_id={"dp": target}, device_id_type=MESH_IDS,
        )

    def across(src, dst, send, recv):
        return pltpu.make_async_remote_copy(
            src_ref=src, dst_ref=dst, send_sem=send, recv_sem=recv,
            device_id={"section": 1 - sec}, device_id_type=MESH_IDS,
        )

    w_copies = [
        pltpu.make_async_copy(w_qkv, wq, w_sem.at[0]),
        pltpu.make_async_copy(w_out, wo, w_sem.at[1]),
        pltpu.make_async_copy(w_gate_up, wg, w_sem.at[2]),
        pltpu.make_async_copy(w_down, wd, w_sem.at[3]),
    ]

    def token_copy(m):
        return pltpu.make_async_copy(tokens.at[m], x_s.at[m], x_sem.at[m])

    def cot_copy(m):
        return pltpu.make_async_copy(cotangent.at[m], g_s.at[m], g_sem.at[m])

    def hand_on(m):
        return across(send_s.at[m], x_s.at[m], f_send.at[m], f_recv.at[m])

    def hand_back(m):
        return across(send_s.at[m], g_s.at[m], b_send.at[m], b_recv.at[m])

    def out_copy(m):
        return pltpu.make_async_copy(out_s, boundary.at[m], out_sem.at[m])

    def pair(k, m):
        rows = pl.ds(m * 256, 256)
        src, dst = (
            lambda: (nl_s.at[m], peer_n.at[m]),
            lambda: (ht_s.at[m, :, other], peer_h.at[m]),
            lambda: (gf_s.at[m], peer_f.at[m]),
            lambda: (gu_s.at[m, :, pl.ds(other * FF, FF)], peer_g.at[m]),
            lambda: (x_s.at[m], wg.at[rows, pl.ds(0, 768)]),
            lambda: (mixed_s.at[m], wg.at[rows, pl.ds(768, 768)]),
            lambda: (qkv_s.at[m, :, pl.ds(other * 1152, 1152)], wg.at[rows, pl.ds(1536, 1152)]),
            lambda: (ga_s.at[m, :, pl.ds(other * 384, 384)], wg.at[rows, pl.ds(2688, 384)]),
        )[k]()
        return remote(src, dst, pair_send.at[k, m], pair_recv.at[k, m], peer_core)

    def pair_wait(*which):
        for k in which:
            for m in range(2):
                pair(k, m).wait()

    @pl.when(first)
    def _():
        token_copy(0).start()

    w_copies[0].start()
    w_copies[1].start()

    barrier = pltpu.get_barrier_semaphore()
    pl.semaphore_signal(barrier, inc=1, device_id={"section": 1 - sec}, device_id_type=MESH_IDS)
    for target in [peer_core, peer_x] + y_ids + z_ids:
        pl.semaphore_signal(barrier, inc=1, device_id={"dp": target}, device_id_type=MESH_IDS)
    pl.semaphore_wait(barrier, 9)

    vec_s[...] = jnp.zeros_like(vec_s)
    rows_j = lax.broadcasted_iota(jnp.int32, (256, 256), 0)
    cols_i = lax.broadcasted_iota(jnp.int32, (256, 256), 1)
    distance = f32(jnp.abs(rows_j - cols_i))
    length_a, length_b, length_long = short_lens[0], short_lens[1], long_lens[0]
    for m in range(2):
        if m == 0:
            limit = jnp.where(rows_j < 128, length_a, length_b + 128)
            apart = jnp.where((rows_j >> 7) == (cols_i >> 7), 0, 1024)
            ok = rows_j + apart < limit
        else:
            ok = rows_j < length_long
        dist_s[m] = jnp.where(ok, distance, masked_distance)

    w_copies[0].wait()
    w_copies[2].start()
    w_copies[3].start()

    @pl.when(first)
    def _():
        token_copy(1).start()

    @pl.when(second)
    def _():
        cot_copy(0).start()
        cot_copy(1).start()


    def v_sends(stage):
        targets = ([peer_core], [peer_x], y_ids, z_ids)[stage]
        base = (0, 1, 2, 5)[stage]
        count = len(targets)
        return [
            remote(
                v_acc.at[stage], v_recv.at[base + (count - 1 - k)],
                vs_sem.at[base + k], vr_sem.at[base + (count - 1 - k)], targets[k],
            )
            for k in range(count)
        ]

    def v_start(stage):
        for copy in v_sends(stage):
            copy.start()

    def v_finish(stage):
        base = (0, 1, 2, 5)[stage]
        copies = v_sends(stage)
        for copy in copies:
            copy.wait_send()
        for copy in copies:
            copy.wait_recv()
        total = v_acc[stage]
        for k in range(len(copies)):
            total = total + v_recv[base + k]
        v_acc[stage + 1] = total

    def ring(par):
        right = y_ids[0] * (1 - par) + z_ids[0] * par
        left = y_ids[2] * (1 - par) + z_ids[2] * par
        place = yy * (1 - par) + zz * par
        return right, left, place

    def a1_copies(j):
        slot, mine = j % SLOTS, j % OWN_SLOTS
        right, left, p = ring(j % 2)
        far, nxt, prv = (p + 2) % 4, (p + 1) % 4, (p + 3) % 4
        return (
            remote(own.at[mine, 0, far], ra_relay.at[slot, 0], a_send.at[slot, 0], a_relay_recv.at[slot, 0], right),
            remote(own.at[mine, 1, far], ra_relay.at[slot, 1], a_send.at[slot, 1], a_relay_recv.at[slot, 1], left),
            remote(own.at[mine, 1, nxt], ra_fin.at[slot, 0, 1], a_send.at[slot, 2], a_fin_recv.at[slot, 0, 1], right),
            remote(own.at[mine, 0, prv], ra_fin.at[slot, 1, 0], a_send.at[slot, 3], a_fin_recv.at[slot, 1, 0], left),
        )

    def a2_copies(j):
        slot, mine = j % SLOTS, j % 2
        right, left, _ = ring(j % 2)
        return (
            remote(sa.at[mine, 0], ra_fin.at[slot, 0, 0], a2_send.at[mine, 0], a_fin_recv.at[slot, 0, 0], right),
            remote(sa.at[mine, 1], ra_fin.at[slot, 1, 1], a2_send.at[mine, 1], a_fin_recv.at[slot, 1, 1], left),
        )

    def b1_copies(j):
        slot, mine = j % SLOTS, j % OWN_SLOTS
        right, left, p = ring(1 - j % 2)
        far, nxt, prv = (p + 2) % 4, (p + 1) % 4, (p + 3) % 4
        return (
            remote(own_b.at[mine, 0, far], rb_relay.at[slot, 0], bb_send.at[slot, 0], bb_relay_recv.at[slot, 0], right),
            remote(own_b.at[mine, 1, far], rb_relay.at[slot, 1], bb_send.at[slot, 1], bb_relay_recv.at[slot, 1], left),
            remote(own_b.at[mine, 1, nxt], rb_fin.at[slot, 0, 1], bb_send.at[slot, 2], bb_fin_recv.at[slot, 0, 1], right),
            remote(own_b.at[mine, 0, prv], rb_fin.at[slot, 1, 0], bb_send.at[slot, 3], bb_fin_recv.at[slot, 1, 0], left),
        )

    def b2_copies(j):
        slot, mine = j % SLOTS, j % 2
        right, left, _ = ring(1 - j % 2)
        return (
            remote(sb.at[mine, 0], rb_fin.at[slot, 0, 0], b2_send.at[mine, 0], bb_fin_recv.at[slot, 0, 0], right),
            remote(sb.at[mine, 1], rb_fin.at[slot, 1, 1], b2_send.at[mine, 1], bb_fin_recv.at[slot, 1, 1], left),
        )

    def x_copy(j):
        slot, mine = j % SLOTS, j % 2
        return remote(x_send.at[mine], x_recv.at[slot], xs_sem.at[mine], xr_sem.at[slot], peer_x)

    def c_copy(j):
        slot, mine = j % SLOTS, j % 2
        return remote(c_send.at[mine], c_recv.at[slot], cs_sem.at[mine], cr_sem.at[slot], peer_core)

    def place_rows(j, piece):
        mine = j % OWN_SLOTS
        par = j % 2
        for y in range(4):
            for z in range(4):
                i1 = y * (1 - par) + z * par
                i2 = z * (1 - par) + y * par
                for x in range(2):
                    own[mine, x, i1, i2] = bf16(piece(y * 4 + z, x))

    def place_regular(j, result):
        def piece(block, x):
            rows = result[block * 48 + x * 24:block * 48 + x * 24 + 24]
            return jnp.concatenate([rows[:, :256], rows[:, 256:]], 0)

        place_rows(j, piece)

    def compute(j):
        @when(j < N_DOWN)
        def _():
            @when(j == 0)
            def _():
                pair_wait(1, 2)

            cols = pl.ds(pl.multiple_of(j * 256, 256), 256) if not isinstance(j, int) else pl.ds(j * 256, 256)
            result = None
            for m in range(2):
                for left, right in ((ht_s[m, :, core], gf_s[m, :, cols]), (peer_h[m], peer_f[m, :, cols])):
                    term = dot_nn(left.reshape(1536, 256), right)
                    result = term if result is None else result + term
            place_rows(j, lambda block, x: result[(block * 2 + x) * 48:(block * 2 + x + 1) * 48])

        @when((j >= N_DOWN) & (j < N_DOWN + 6))
        def _():
            @when(j == N_DOWN)
            def _():
                pair_wait(0, 3)
                for k in (4, 5, 6, 7):
                    for m in range(2):
                        pair(k, m).start()

            column = pl.multiple_of((j - N_DOWN) * 512, 512)
            mine = gu_s[:, :, pl.ds(pl.multiple_of(core * FF + column, 512), 512)]
            place_regular(j, dot_tn(both(nl_s[...]), both(mine)) + dot_tn(both(peer_n[...]), both(peer_g[:, :, pl.ds(column, 512)])))

        def qkv_part(column, width):
            mine = qkv_s[:, :, pl.ds(pl.multiple_of(core * 1152 + column, 128), width)]
            far = wg[0:512, pl.ds(pl.multiple_of(1536 + column, 128), width)]
            return dot_tn(both(x_s[...]), both(mine)) + dot_tn(wg[0:512, 0:768], far)

        @when((j >= N_DOWN + 6) & (j < N_DOWN + 8))
        def _():
            @when(j == N_DOWN + 6)
            def _():
                pair_wait(4, 5, 6, 7)

            place_regular(j, qkv_part((j - N_DOWN - 6) * 512, 512))

        @when(j == N_DOWN + 8)
        def _():
            mine = ga_s[:, :, pl.ds(pl.multiple_of(core * 384, 128), 384)]
            out_part = dot_tn(both(mixed_s[...]), both(mine)) + dot_tn(wg[0:512, 768:1536], wg[0:512, 2688:3072])
            place_regular(j, jnp.concatenate([qkv_part(1024, 128), out_part], 1))

    def step(i, carry):
        @when(i < N_CHUNKS)
        def _():
            compute(i)
            for copy in a1_copies(i):
                copy.start()

        j1 = i - 1

        @when((j1 >= 0) & (j1 < N_CHUNKS))
        def _():
            slot, mine, buf = j1 % SLOTS, j1 % OWN_SLOTS, j1 % 2
            _, _, p = ring(j1 % 2)
            before = a1_copies(j1)
            after = a2_copies(j1)
            before[0].wait_recv()
            sa[buf, 0] = bf16(f32(own[mine, 0, (p + 1) % 4]) + f32(ra_relay[slot, 0]))
            after[0].start()
            before[1].wait_recv()
            sa[buf, 1] = bf16(f32(own[mine, 1, (p + 3) % 4]) + f32(ra_relay[slot, 1]))
            after[1].start()

        j2 = i - 2

        @when((j2 >= 0) & (j2 < N_CHUNKS))
        def _():
            slot, mine = j2 % SLOTS, j2 % OWN_SLOTS
            _, _, p = ring(j2 % 2)
            before = a1_copies(j2)
            after = a2_copies(j2)
            for copy in before + after:
                copy.wait_send()
            for copy in before[2:] + after:
                copy.wait_recv()
            for h in range(2):
                own_b[mine, h] = bf16(f32(own[mine, h, p]) + f32(ra_fin[slot, 0, h]) + f32(ra_fin[slot, 1, h]))
            for copy in b1_copies(j2):
                copy.start()

        j3 = i - 3

        @when((j3 >= 0) & (j3 < N_CHUNKS))
        def _():
            slot, mine, buf = j3 % SLOTS, j3 % OWN_SLOTS, j3 % 2
            _, _, p = ring(1 - j3 % 2)
            before = b1_copies(j3)
            after = b2_copies(j3)
            before[0].wait_recv()
            sb[buf, 0] = bf16(f32(own_b[mine, 0, (p + 1) % 4]) + f32(rb_relay[slot, 0]))
            after[0].start()
            before[1].wait_recv()
            sb[buf, 1] = bf16(f32(own_b[mine, 1, (p + 3) % 4]) + f32(rb_relay[slot, 1]))
            after[1].start()

        j4 = i - 4

        @when((j4 >= 0) & (j4 < N_CHUNKS))
        def _():
            slot, mine, buf = j4 % SLOTS, j4 % OWN_SLOTS, j4 % 2
            _, _, p = ring(1 - j4 % 2)
            before = b1_copies(j4)
            after = b2_copies(j4)
            for copy in before + after:
                copy.wait_send()
            for copy in before[2:] + after:
                copy.wait_recv()
            total = [f32(own_b[mine, h, p]) + f32(rb_fin[slot, 0, h]) + f32(rb_fin[slot, 1, h]) for h in range(2)]
            x_send[buf] = jnp.where(xhi == 0, total[1], total[0])
            x_keep[buf] = jnp.where(xhi == 0, total[0], total[1])
            x_copy(j4).start()

        j5 = i - 5

        @when((j5 >= 0) & (j5 < N_CHUNKS))
        def _():
            slot, buf = j5 % SLOTS, j5 % 2
            x_copy(j5).wait()

            @when(j5 < N_DOWN)
            def _():
                cols = pl.ds(pl.multiple_of(j5 * 256, 256), 256)
                o_dn[:, cols] = x_keep[buf] + x_recv[slot]

            @when(j5 >= N_DOWN)
            def _():
                c_tmp[...] = x_keep[buf] + x_recv[slot]
                for h in range(2):
                    upper, lower = c_tmp[24 * h:24 * h + 12], c_tmp[24 * h + 12:24 * h + 24]
                    c_send[buf, h, 0:12] = jnp.where(core == 0, lower, upper)
                    c_keep[buf, h, 0:12] = jnp.where(core == 0, upper, lower)
                c_copy(j5).start()

        j6 = i - 6

        @when((j6 >= N_DOWN) & (j6 < N_CHUNKS))
        def _():
            slot, buf = j6 % SLOTS, j6 % 2
            c_copy(j6).wait()
            for source, at, who in ((c_keep, buf, core), (c_recv, slot, other)):
                @when(j6 < N_DOWN + 6)
                def _():
                    for h in range(2):
                        column = pl.multiple_of(who * FF + (j6 - N_DOWN) * 512 + h * 256, 256)
                        o_gu[:, 0, pl.ds(column, 256)] = source[at, h, 0:12]

                @when((j6 >= N_DOWN + 6) & (j6 < N_DOWN + 8))
                def _():
                    for h in range(2):
                        column = pl.multiple_of(who * 1152 + (j6 - N_DOWN - 6) * 512 + h * 256, 128)
                        o_qkv[:, 0, pl.ds(column, 256)] = source[at, h, 0:12]

                @when(j6 == N_DOWN + 8)
                def _():
                    o_qkv[:, 0, pl.ds(pl.multiple_of(who * 1152 + 1024, 128), 128)] = source[at, 0, 0:12, 0:128]
                    o_out[:, 0, pl.ds(pl.multiple_of(who * 384, 128), 128)] = source[at, 0, 0:12, 128:256]
                    o_out[:, 0, pl.ds(pl.multiple_of(who * 384 + 128, 128), 256)] = source[at, 1, 0:12]

        return carry


    def band(k):
        return pl.ds(k * BAND, BAND)

    def normalise(value):
        average = jnp.mean(value, -1, keepdims=True)
        centred = value - average
        inverse = lax.rsqrt(jnp.mean(centred * centred, -1, keepdims=True) + epsilon)
        return centred * inverse, inverse

    lanes = lax.broadcasted_iota(jnp.int32, (256, 128), 1)

    def own_lanes(e):
        return (lanes < 64) if e == 0 else (lanes >= 64)

    def forward(m, carry):
        @pl.when(first)
        def _():
            token_copy(m).wait()

        @pl.when(second)
        def _():
            hand_on(m).wait_recv()

        x = x_s[m]
        query = dot_nn(x, wq[:, 0:768]) + biases[0]
        qkv_s[m, :, 0:768] = bf16(f32(bf16(query)) * 0.125)
        qkv_s[m, :, 768:1536] = bf16(dot_nn(x, wq[:, 768:1536]))
        qkv_s[m, :, 1536:2304] = bf16(dot_nn(x, wq[:, 1536:2304]) + biases[1])

        for hp in range(6):
            at = pl.ds(hp * 128, 128)
            q2 = qkv_s[m, :, at]
            k2 = qkv_s[m, :, pl.ds(hp * 128 + 768, 128)]
            v2 = qkv_s[m, :, pl.ds(hp * 128 + 1536, 128)]
            none = jnp.zeros_like(q2)
            qs = jnp.concatenate([jnp.where(own_lanes(e), q2, none) for e in range(2)], 0)
            vs = jnp.concatenate([jnp.where(own_lanes(e), v2, none) for e in range(2)], 0)
            scores_two = dot_nt(k2, qs)
            probs_two = []
            for e in range(2):
                head = 2 * hp + e
                scores = scores_two[:, 256 * e:256 * e + 256] - 2.0 ** (-8.0 * (head + 1) / HEADS) * dist_s[m]
                expo = jnp.exp(scores - jnp.max(scores, 0, keepdims=True))
                probs = bf16(expo * (1.0 / jnp.sum(expo, 0, keepdims=True)))
                p_s[m, head] = probs
                probs_two.append(probs)
            mixed_s[m, :, at] = bf16(dot_tn(jnp.concatenate(probs_two, 0), vs))

        @pl.when(m == 0)
        def _():
            w_copies[1].wait()

        acc_s[...] = dot_nn(mixed_s[m], wo[...])
        for k in range(256 // BAND):
            r = band(k)
            value = f32(x_s[m, r]) + (acc_s[r] + biases[2])
            unit, inverse = normalise(value)
            normed = unit * gains[0:1] + biases[3]
            n1_s[m, r] = bf16(unit)
            r1_s[m, r] = inverse
            f_s[r] = normed
            nl_s[m, r] = bf16(normed)

        pair(0, m).start()

        @pl.when(m == 0)
        def _():
            w_copies[2].wait()
            w_copies[3].wait()

        for jb in range(FF // BLOCK):
            c0 = jb * BLOCK
            low = nl_s[m]
            gate_s[...] = dot_nn(low, wg[:, c0:c0 + BLOCK])
            up_s[...] = dot_nn(low, wg[:, c0 + FF:c0 + FF + BLOCK])
            for k in range(256 // BAND):
                r = band(k)
                gate, up = gate_s[r], up_s[r]
                act, slope = gelu_terms(gate)
                gu_s[m, r, c0:c0 + BLOCK] = bf16(up * slope)
                gu_s[m, r, c0 + FF:c0 + FF + BLOCK] = bf16(act)
                gate_s[r] = act * up
            hid = bf16(gate_s[...])
            ht_s[m, 8 * jb:8 * jb + 8] = hid.T.reshape(8, 2, 48, 256)
            term = dot_nn(hid, wd[c0:c0 + BLOCK])
            if jb == 0:
                acc_s[...] = term
            else:
                acc_s[...] += term

        @pl.when(second & (m == 1))
        def _():
            out_copy(0).wait()

        for k in range(256 // BAND):
            r = band(k)
            value = f_s[r] + (acc_s[r] + biases[4])
            unit, inverse = normalise(value)
            n2_s[m, r] = bf16(unit)
            r2_s[m, r] = inverse
            result = unit * gains[1:2] + biases[5]
            out_s[r] = result
            send_s[m, r] = bf16(result)

        @pl.when(first)
        def _():
            hand_on(m).start()

        @pl.when(second)
        def _():
            out_copy(m).start()

        pair(1, m).start()
        return carry

    lax.fori_loop(0, 2, forward, 0)

    def norm_back(grad, unit, inverse, gain):
        scaled = grad * gain
        mean_one = jnp.mean(scaled, -1, keepdims=True)
        mean_two = jnp.mean(scaled * unit, -1, keepdims=True)
        return inverse * (scaled - mean_one - unit * mean_two)

    def backward(m, carry):
        early = first & (m == 1)

        @pl.when(first)
        def _():
            hand_on(m).wait_send()
            hand_back(m).wait_recv()

        @pl.when(second)
        def _():
            cot_copy(m).wait()

        for k in range(256 // BAND):
            r = band(k)
            row = lax.broadcasted_iota(jnp.int32, (BAND, 1), 0) + k * BAND
            limit = jnp.where(m == 0, jnp.where(row < 128, length_a, length_b + 128), length_long)
            live = jnp.where((row < limit) | first, 1.0, 0.0)
            grad = f32(g_s[m, r]) * live
            unit = f32(n2_s[m, r])
            vec_s[1] += fold_rows(grad * unit)
            vec_s[7] += fold_rows(grad)
            grad_in = norm_back(grad, unit, r2_s[m, r], gains[1:2])
            f_s[r] = grad_in
            low = bf16(grad_in)
            gf_s[m, r] = low
            vec_s[6] += fold_rows(f32(low))

        pair(2, m).start()

        for jb in range(FF // BLOCK):
            c0 = jb * BLOCK
            gate_s[...] = dot_nt(gf_s[m], wd[c0:c0 + BLOCK])
            for k in range(256 // BAND):
                r = band(k)
                hid = gate_s[r]
                for c in (c0, c0 + FF):
                    gu_s[m, r, c:c + BLOCK] = bf16(hid * f32(gu_s[m, r, c:c + BLOCK]))
            term = dot_nt(gu_s[m, :, c0:c0 + BLOCK], wg[:, c0:c0 + BLOCK])
            term = term + dot_nt(gu_s[m, :, c0 + FF:c0 + FF + BLOCK], wg[:, c0 + FF:c0 + FF + BLOCK])
            if jb == 0:
                acc_s[...] = term
            else:
                acc_s[...] += term
            if jb == 1:
                @pl.when(early)
                def _():
                    step(0, 0)

        pair(3, m).start()

        @pl.when(early)
        def _():
            step(1, 0)

        for k in range(256 // BAND):
            r = band(k)
            grad = acc_s[r] + f_s[r]
            unit = f32(n1_s[m, r])
            vec_s[0] += fold_rows(grad * unit)
            vec_s[5] += fold_rows(grad)
            grad_in = norm_back(grad, unit, r1_s[m, r], gains[0:1])
            f_s[r] = grad_in
            low = bf16(grad_in)
            ga_s[m, r] = low
            vec_s[4] += fold_rows(f32(low))

        def mixed_back(g):
            c = g * 256
            low_s[:, c:c + 256] = bf16(dot_nt(ga_s[m], wo[c:c + 256]))

        def attend_back(hp):
            at = pl.ds(hp * 128, 128)
            q2 = qkv_s[m, :, at]
            k2 = qkv_s[m, :, pl.ds(hp * 128 + 768, 128)]
            v2 = qkv_s[m, :, pl.ds(hp * 128 + 1536, 128)]
            do2 = low_s[:, at]
            none = jnp.zeros_like(q2)
            qs, ks, ds = (
                jnp.concatenate([jnp.where(own_lanes(e), wide, none) for e in range(2)], 0) for wide in (q2, k2, do2)
            )
            grad_probs_two = dot_nt(v2, ds)
            probs_two = [p_s[m, 2 * hp + e] for e in range(2)]
            scores_two = []
            for e in range(2):
                weighted = f32(probs_two[e]) * grad_probs_two[:, 256 * e:256 * e + 256]
                total = jnp.sum(weighted, 0, keepdims=True)
                scores_two.append(bf16(weighted - f32(probs_two[e]) * total))
            grad_v = bf16(dot_nn(jnp.concatenate(probs_two, 1), ds))
            grad_k = bf16(dot_nn(jnp.concatenate(scores_two, 1), qs))
            grad_q = bf16(dot_tn(jnp.concatenate(scores_two, 0), ks) * 0.125)
            vec_s[2, :, at] += fold_rows(f32(grad_q))
            vec_s[3, :, at] += fold_rows(f32(grad_v))
            qkv_s[m, :, at] = grad_q
            qkv_s[m, :, pl.ds(hp * 128 + 768, 128)] = grad_k
            qkv_s[m, :, pl.ds(hp * 128 + 1536, 128)] = grad_v

        mixed_back(0)
        for g in range(3):
            if g < 2:
                mixed_back(g + 1)
            attend_back(2 * g)
            attend_back(2 * g + 1)
            c = g * 256
            term = dot_nt(qkv_s[m, :, c:c + 256], wq[:, c:c + 256])
            for c in (g * 256 + 768, g * 256 + 1536):
                term = term + dot_nt(qkv_s[m, :, c:c + 256], wq[:, c:c + 256])
            if g == 0:
                acc_s[...] = term
            else:
                acc_s[...] += term

        @pl.when(early)
        def _():
            step(2, 0)

        @pl.when(first & (m == 1))
        def _():
            out_copy(0).wait()

        grad_a = acc_s[...] + f_s[...]

        @pl.when(second)
        def _():
            send_s[m] = bf16(grad_a)
            hand_back(m).start()

        @pl.when(first)
        def _():
            out_s[...] = grad_a
            out_copy(m).start()

        return carry

    lax.fori_loop(0, 2, backward, 0)
    for k in range(8):
        v_acc[0, k:k + 1] = jnp.sum(vec_s[k], 0, keepdims=True)
    v_start(0)

    def tail_step(i, carry):
        step(i, carry)
        for stage in range(4):
            @pl.when(i == 2 * stage + 5)
            def _():
                v_finish(stage)
                if stage < 3:
                    v_start(stage + 1)

        return carry

    lax.fori_loop(3 * (1 - sec), N_CHUNKS + 6, tail_step, 0)
    o_vec[...] = v_acc[4]

    @pl.when(second)
    def _():
        hand_back(0).wait_send()
        hand_back(1).wait_send()

    out_copy(1).wait()


def run_layers(short_lens, long_lens, tokens, cotangent, w_qkv, w_out, w_gate_up, w_down, gains, biases):
    low, wide = jnp.bfloat16, jnp.float32
    hbm = pl.BlockSpec(memory_space=pl.ANY)
    vmem = pl.BlockSpec(memory_space=pltpu.VMEM)
    smem = pl.BlockSpec(memory_space=pltpu.SMEM)
    dma = pltpu.SemaphoreType.DMA
    of = pltpu.VMEM
    s = SLOTS
    return pl.pallas_call(
        layers_kernel,
        out_shape=[
            jax.ShapeDtypeStruct((2, 256, 768), wide),
            jax.ShapeDtypeStruct((12, 1, 2304), wide),
            jax.ShapeDtypeStruct((12, 1, 768), wide),
            jax.ShapeDtypeStruct((12, 1, 6144), wide),
            jax.ShapeDtypeStruct((48, 768), wide),
            jax.ShapeDtypeStruct((8, 768), wide),
        ],
        in_specs=[smem] * 2 + [hbm] * 6 + [vmem] * 2,
        out_specs=[hbm] + [vmem] * 5,
        scratch_shapes=[
            of((768, 2304), low), of((768, 768), low), of((768, 6144), low), of((3072, 768), low),
            of((2, 256, 768), low), of((2, 256, 768), low), of((2, 256, 2304), low), of((2, 12, 256, 256), low),
            of((2, 256, 768), low), of((2, 256, 768), low), of((256, 768), low),
            of((2, 256, 768), low), of((2, 256, 768), low),
            of((2, 256, 1), wide), of((2, 256, 1), wide), of((2, 256, 6144), low), of((2, 32, 2, 48, 256), low),
            of((2, 256, 768), low), of((2, 256, 768), low), of((2, 256, 768), low), of((256, 768), wide),
            of((256, 768), wide), of((256, 768), wide), of((256, BLOCK), wide), of((256, BLOCK), wide),
            of((2, 256, 256), wide), of((8, 8, 768), wide),
            of((2, 256, 768), low), of((2, 32, 48, 256), low), of((2, 256, 768), low), of((2, 256, 3072), low),
            of((OWN_SLOTS, 2, 4, 4, 48, 256), low),
            of((s, 2, 4, 48, 256), low), of((s, 2, 2, 4, 48, 256), low), of((2, 2, 4, 48, 256), low),
            of((OWN_SLOTS, 2, 4, 48, 256), low),
            of((s, 2, 48, 256), low), of((s, 2, 2, 48, 256), low), of((2, 2, 48, 256), low),
            of((2, 48, 256), wide), of((2, 48, 256), wide), of((s, 48, 256), wide),
            of((48, 256), wide), of((2, 2, 16, 256), wide), of((2, 2, 16, 256), wide), of((s, 2, 16, 256), wide),
            of((5, 8, 768), wide), of((8, 8, 768), wide),
            dma((4,)), dma((2,)), dma((2,)), dma((2,)), dma((2,)), dma((2,)), dma((2,)), dma((2,)),
            dma((8, 2)), dma((8, 2)),
            dma((s, 4)), dma((s, 2)), dma((s, 2, 2)), dma((2, 2)),
            dma((s, 4)), dma((s, 2)), dma((s, 2, 2)), dma((2, 2)),
            dma((2,)), dma((s,)), dma((2,)), dma((s,)), dma((8,)), dma((8,)),
        ],
        compiler_params=pltpu.CompilerParams(
            collective_id=0, has_side_effects=True, vmem_limit_bytes=VMEM_LIMIT
        ),
        cost_estimate=pl.CostEstimate(flops=3 * 10 ** 10, bytes_accessed=4 * 10 ** 7, transcendentals=10 ** 7),
        name="run_layers",
    )(short_lens, long_lens, tokens, cotangent, w_qkv, w_out, w_gate_up, w_down, gains, biases)


def place_kernel(start, boundary, qkv, out, gate_up, down, vec, o_b, o_q, o_o, o_g, o_d, o_gains, o_biases, sems):
    copies = [
        pltpu.make_async_copy(source, target, sems.at[k])
        for k, (source, target) in enumerate(
            ((boundary, o_b.at[0]), (gate_up, o_g), (qkv, o_q), (out, o_o), (down, o_d.at[0]))
        )
    ]
    for copy in copies:
        copy.start()
    mine = pltpu.roll(vec[...], lax.rem(D - start[0], D), axis=1)
    o_gains[0] = mine[:2, :12]
    o_biases[:, 0] = mine[2:, :12]
    for copy in copies:
        copy.wait()


def place(start, boundary, qkv, out, gate_up, down, vec):
    wide = jnp.float32
    vmem = pl.BlockSpec(memory_space=pltpu.VMEM)
    return pl.pallas_call(
        place_kernel,
        out_shape=[
            jax.ShapeDtypeStruct((1, 2, 256, 768), wide),
            jax.ShapeDtypeStruct((12, 1, 2304), wide),
            jax.ShapeDtypeStruct((12, 1, 768), wide),
            jax.ShapeDtypeStruct((12, 1, 6144), wide),
            jax.ShapeDtypeStruct((1, 48, 768), wide),
            jax.ShapeDtypeStruct((1, 2, 12), wide),
            jax.ShapeDtypeStruct((6, 1, 12), wide),
        ],
        in_specs=[pl.BlockSpec(memory_space=pltpu.SMEM)] + [pl.BlockSpec(memory_space=pltpu.HBM)] * 5 + [vmem],
        out_specs=[vmem] * 7,
        scratch_shapes=[pltpu.SemaphoreType.DMA((5,))],
        compiler_params=pltpu.CompilerParams(vmem_limit_bytes=VMEM_LIMIT),
        name="place",
    )(start, boundary, qkv, out, gate_up, down, vec)


def on_device(
    tokens, cotangent, short_lens, long_lens, w_qkv, w_out, w_gate_up, w_down, gains, biases
):
    boundary, q, o, g, d, vec = run_layers(
        short_lens, long_lens, tokens, cotangent, w_qkv[0], w_out[0], w_gate_up[0], w_down[0], gains[0],
        jnp.transpose(biases, (1, 0, 2)),
    )
    start = jnp.full((1,), lax.axis_index("dp") * 12, jnp.int32)
    b, q, o, g, d, gains_out, biases_out = place(start, boundary, q, o, g, d, vec)
    q, o, g, biases_out = (jnp.transpose(rows, (1, 0, 2)) for rows in (q, o, g, biases_out))
    return (b, q, o, g, d, gains_out, biases_out)


def solution(mesh):
    placed = (
        P(None, "dp", None),
        P(None, "dp", None),
        P("dp"),
        P("dp"),
        P("section", None, None),
        P("section", None, None),
        P("section", None, None),
        P("section", None, None),
        P("section", None, None),
        P("section", None, None),
    )
    return jax.shard_map(
        on_device,
        mesh=mesh,
        in_specs=placed,
        out_specs=(
            P("section", None, "dp", None),
            P("section", "dp", None),
            P("section", "dp", None),
            P("section", "dp", None),
            P("section", "dp", None),
            P("section", None, "dp"),
            P("section", None, "dp"),
        ),
        check_vma=False,
    )
```

```python
import jax
import jax.numpy as jnp
from jax import lax
from jax.experimental import pallas as pl
from jax.experimental.pallas import tpu as pltpu
from jax.sharding import PartitionSpec as P

D = 768
HEADS = 12
FF = 3072
BLOCK = 768
BAND = 32
N_CHUNKS = 12
N_DOWN = 3
DIRECT = 9
SLOTS = 5
OWN_SLOTS = 3
VMEM_LIMIT = 62 * 1024 * 1024
MESH_IDS = pl.DeviceIdType.MESH

epsilon = 1e-05
masked_distance = 1e12


def dot_nn(lhs, rhs):
    return jnp.dot(lhs, rhs, preferred_element_type=jnp.float32)


def dot_nt(lhs, rhs):
    return lax.dot_general(lhs, rhs, (((1,), (1,)), ((), ())), preferred_element_type=jnp.float32)


def dot_tn(lhs, rhs):
    return lax.dot_general(lhs, rhs, (((0,), (0,)), ((), ())), preferred_element_type=jnp.float32)


def f32(value):
    return value.astype(jnp.float32)


def bf16(value):
    return value.astype(jnp.bfloat16)


def fold_rows(value):
    return jnp.sum(value.reshape(value.shape[0] // 8, 8, value.shape[1]), 0)


def gelu_terms(gate):
    cdf = 0.5 * (1.0 + lax.erf(gate * 0.7071067811865476))
    density = jnp.exp(-0.5 * gate * gate) * 0.3989422804014327
    return gate * cdf, cdf + gate * density


def when(condition):
    if isinstance(condition, bool):
        return (lambda body: body()) if condition else (lambda body: None)
    return pl.when(condition)


def both(value):
    return value.reshape(512, value.shape[-1])


def layers_kernel(
    short_lens, long_lens, tokens, cotangent, w_qkv, w_out, w_gate_up, w_down, gains, biases,
    boundary, o_qkv, o_out, o_gu, o_dn, o_vec,
    wq, wo, wg, wd, x_s, g_s, qkv_s, p_s, mixed_s, nl_s, n1_s, n2_s, r_s, gu_s, ht_s,
    gf_s, ga_s, send_s, out_s, acc_s, f_s, gate_s, dist_s, vec_s,
    peer_n, peer_h, peer_f, peer_g,
    own, ra_relay, ra_fin, sa, own_b, rb_relay, rb_fin, sb, x_send, x_keep, x_recv, c_tmp, c_send, c_keep, c_recv,
    rz, cz_send, cz_keep, cz_recv,
    v_acc, v_recv,
    w_sem, x_sem, g_sem, out_sem, f_send, f_recv, b_send, b_recv, pair_send, pair_recv,
    a_send, a_relay_recv, a_fin_recv, a2_send,
    bb_send, bb_relay_recv, bb_fin_recv, b2_send,
    xs_sem, xr_sem, cs_sem, cr_sem, vs_sem, vr_sem,
    z_send, z_recv, czs_sem, czr_sem,
):
    sec = lax.axis_index("section")
    first = sec == 0
    second = sec == 1
    me = lax.axis_index("dp")
    core = me % 2
    xhi = (me // 2) % 2
    zz = (me // 4) % 4
    yy = me // 16
    other = 1 - core

    def dev(y, z, x, c):
        return ((y * 4 + z) * 2 + x) * 2 + c

    peer_core = dev(yy, zz, xhi, other)
    peer_x = dev(yy, zz, 1 - xhi, core)
    y_ids = [dev((yy + k) % 4, zz, xhi, core) for k in (1, 2, 3)]
    z_ids = [dev(yy, (zz + k) % 4, xhi, core) for k in (1, 2, 3)]

    yx_ids = [dev((yy + k) % 4, zz, 1 - xhi, core) for k in (1, 2, 3)]
    zx_ids = [dev(yy, (zz + k) % 4, 1 - xhi, core) for k in (1, 2, 3)]

    def remote(src, dst, send, recv, target):
        return pltpu.make_async_remote_copy(
            src_ref=src, dst_ref=dst, send_sem=send, recv_sem=recv,
            device_id={"dp": target}, device_id_type=MESH_IDS,
        )

    def across(src, dst, send, recv):
        return pltpu.make_async_remote_copy(
            src_ref=src, dst_ref=dst, send_sem=send, recv_sem=recv,
            device_id={"section": 1 - sec}, device_id_type=MESH_IDS,
        )

    w_copies = [
        pltpu.make_async_copy(w_qkv, wq, w_sem.at[0]),
        pltpu.make_async_copy(w_out, wo, w_sem.at[1]),
        pltpu.make_async_copy(w_gate_up, wg, w_sem.at[2]),
        pltpu.make_async_copy(w_down, wd, w_sem.at[3]),
    ]

    def token_copy(m):
        return pltpu.make_async_copy(tokens.at[m], x_s.at[m], x_sem.at[m])

    def cot_copy(m):
        return pltpu.make_async_copy(cotangent.at[m], g_s.at[m], g_sem.at[m])

    def hand_on(m):
        return across(send_s.at[m], x_s.at[m], f_send.at[m], f_recv.at[m])

    def hand_back(m):
        return across(send_s.at[m], g_s.at[m], b_send.at[m], b_recv.at[m])

    def out_copy(m):
        return pltpu.make_async_copy(out_s, boundary.at[m], out_sem.at[m])

    def pair(k, m):
        rows = pl.ds(m * 256, 256)
        src, dst = (
            lambda: (nl_s.at[m], peer_n.at[m]),
            lambda: (ht_s.at[m, :, other], peer_h.at[m]),
            lambda: (gf_s.at[m], peer_f.at[m]),
            lambda: (gu_s.at[m, :, pl.ds(other * FF, FF)], peer_g.at[m]),
            lambda: (x_s.at[m], wg.at[rows, pl.ds(0, 768)]),
            lambda: (mixed_s.at[m], wg.at[rows, pl.ds(768, 768)]),
            lambda: (qkv_s.at[m, :, pl.ds(other * 1152, 1152)], wg.at[rows, pl.ds(1536, 1152)]),
            lambda: (ga_s.at[m, :, pl.ds(other * 384, 384)], wg.at[rows, pl.ds(2688, 384)]),
        )[k]()
        return remote(src, dst, pair_send.at[k, m], pair_recv.at[k, m], peer_core)

    def pair_wait(*which):
        for k in which:
            for m in range(2):
                pair(k, m).wait()

    @pl.when(first)
    def _():
        token_copy(0).start()

    w_copies[0].start()
    w_copies[1].start()

    barrier = pltpu.get_barrier_semaphore()
    pl.semaphore_signal(barrier, inc=1, device_id={"section": 1 - sec}, device_id_type=MESH_IDS)
    for target in [peer_core, peer_x] + y_ids + z_ids + yx_ids + zx_ids:
        pl.semaphore_signal(barrier, inc=1, device_id={"dp": target}, device_id_type=MESH_IDS)
    pl.semaphore_wait(barrier, 15)

    vec_s[...] = jnp.zeros_like(vec_s)
    rows_j = lax.broadcasted_iota(jnp.int32, (256, 256), 0)
    cols_i = lax.broadcasted_iota(jnp.int32, (256, 256), 1)
    distance = f32(jnp.abs(rows_j - cols_i))
    length_a, length_b, length_long = short_lens[0], short_lens[1], long_lens[0]
    for m in range(2):
        if m == 0:
            limit = jnp.where(rows_j < 128, length_a, length_b + 128)
            apart = jnp.where((rows_j >> 7) == (cols_i >> 7), 0, 1024)
            ok = rows_j + apart < limit
        else:
            ok = rows_j < length_long
        dist_s[m] = jnp.where(ok, distance, masked_distance)

    w_copies[0].wait()
    w_copies[2].start()
    w_copies[3].start()

    @pl.when(first)
    def _():
        token_copy(1).start()

    @pl.when(second)
    def _():
        cot_copy(0).start()
        cot_copy(1).start()


    def v_sends(stage):
        targets = ([peer_core], [peer_x], y_ids, z_ids)[stage]
        base = (0, 1, 2, 5)[stage]
        count = len(targets)
        return [
            remote(
                v_acc.at[stage], v_recv.at[base + (count - 1 - k)],
                vs_sem.at[base + k], vr_sem.at[base + (count - 1 - k)], targets[k],
            )
            for k in range(count)
        ]

    def v_start(stage):
        for copy in v_sends(stage):
            copy.start()

    def v_finish(stage):
        base = (0, 1, 2, 5)[stage]
        copies = v_sends(stage)
        for copy in copies:
            copy.wait_send()
        for copy in copies:
            copy.wait_recv()
        total = v_acc[stage]
        for k in range(len(copies)):
            total = total + v_recv[base + k]
        v_acc[stage + 1] = total

    def ring(par):
        right = y_ids[0] * (1 - par) + z_ids[0] * par
        left = y_ids[2] * (1 - par) + z_ids[2] * par
        place = yy * (1 - par) + zz * par
        return right, left, place

    def a1_copies(j):
        slot, mine = j % SLOTS, j % OWN_SLOTS
        right, left, p = ring(j % 2)
        far, nxt, prv = (p + 2) % 4, (p + 1) % 4, (p + 3) % 4
        return (
            remote(own.at[mine, 0, far], ra_relay.at[slot, 0], a_send.at[slot, 0], a_relay_recv.at[slot, 0], right),
            remote(own.at[mine, 1, far], ra_relay.at[slot, 1], a_send.at[slot, 1], a_relay_recv.at[slot, 1], left),
            remote(own.at[mine, 1, nxt], ra_fin.at[slot, 0, 1], a_send.at[slot, 2], a_fin_recv.at[slot, 0, 1], right),
            remote(own.at[mine, 0, prv], ra_fin.at[slot, 1, 0], a_send.at[slot, 3], a_fin_recv.at[slot, 1, 0], left),
        )

    def a2_copies(j):
        slot, mine = j % SLOTS, j % 2
        right, left, _ = ring(j % 2)
        return (
            remote(sa.at[mine, 0], ra_fin.at[slot, 0, 0], a2_send.at[mine, 0], a_fin_recv.at[slot, 0, 0], right),
            remote(sa.at[mine, 1], ra_fin.at[slot, 1, 1], a2_send.at[mine, 1], a_fin_recv.at[slot, 1, 1], left),
        )

    def b1_copies(j):
        slot, mine = j % SLOTS, j % OWN_SLOTS
        right, left, p = ring(1 - j % 2)
        far, nxt, prv = (p + 2) % 4, (p + 1) % 4, (p + 3) % 4
        return (
            remote(own_b.at[mine, 0, far], rb_relay.at[slot, 0], bb_send.at[slot, 0], bb_relay_recv.at[slot, 0], right),
            remote(own_b.at[mine, 1, far], rb_relay.at[slot, 1], bb_send.at[slot, 1], bb_relay_recv.at[slot, 1], left),
            remote(own_b.at[mine, 1, nxt], rb_fin.at[slot, 0, 1], bb_send.at[slot, 2], bb_fin_recv.at[slot, 0, 1], right),
            remote(own_b.at[mine, 0, prv], rb_fin.at[slot, 1, 0], bb_send.at[slot, 3], bb_fin_recv.at[slot, 1, 0], left),
        )

    def b2_copies(j):
        slot, mine = j % SLOTS, j % 2
        right, left, _ = ring(1 - j % 2)
        return (
            remote(sb.at[mine, 0], rb_fin.at[slot, 0, 0], b2_send.at[mine, 0], bb_fin_recv.at[slot, 0, 0], right),
            remote(sb.at[mine, 1], rb_fin.at[slot, 1, 1], b2_send.at[mine, 1], bb_fin_recv.at[slot, 1, 1], left),
        )

    def x_copy(j):
        slot, mine = j % SLOTS, j % 2
        return remote(x_send.at[mine], x_recv.at[slot], xs_sem.at[mine], xr_sem.at[slot], peer_x)

    def direct_copies(j):
        late, mine = j - DIRECT, j % OWN_SLOTS
        par = 1 - j % 2
        _, _, p = ring(par)
        copies = []
        for k in range(1, 8):
            ahead, flip = k // 2, k % 2
            if ahead == 0:
                target = peer_x
            else:
                along_y, along_z = ((yx_ids, zx_ids) if flip else (y_ids, z_ids))
                target = along_y[ahead - 1] * (1 - par) + along_z[ahead - 1] * par
            seen = (4 - ahead) % 4 * 2 + flip
            copies.append(remote(
                own_b.at[mine, (xhi + flip) % 2, (p + ahead) % 4], rz.at[late, seen],
                z_send.at[late, k], z_recv.at[late, seen], target,
            ))
        return copies

    def cz_copy(j):
        late = j - DIRECT
        return remote(cz_send.at[late], cz_recv.at[late], czs_sem.at[late], czr_sem.at[late], peer_core)

    def c_copy(j):
        slot, mine = j % SLOTS, j % 2
        return remote(c_send.at[mine], c_recv.at[slot], cs_sem.at[mine], cr_sem.at[slot], peer_core)

    def place_rows(j, piece):
        mine = j % OWN_SLOTS
        par = j % 2
        for y in range(4):
            for z in range(4):
                i1 = y * (1 - par) + z * par
                i2 = z * (1 - par) + y * par
                for x in range(2):
                    own[mine, x, i1, i2] = bf16(piece(y * 4 + z, x))

    def place_regular(j, result):
        def piece(block, x):
            rows = result[block * 48 + x * 24:block * 48 + x * 24 + 24]
            return jnp.concatenate([rows[:, :256], rows[:, 256:]], 0)

        place_rows(j, piece)

    def compute(j):
        @when(j < N_DOWN)
        def _():
            @when(j == 0)
            def _():
                pair_wait(1, 2)

            cols = pl.ds(pl.multiple_of(j * 256, 256), 256) if not isinstance(j, int) else pl.ds(j * 256, 256)
            result = None
            for m in range(2):
                for left, right in ((ht_s[m, :, core], gf_s[m, :, cols]), (peer_h[m], peer_f[m, :, cols])):
                    term = dot_nn(left.reshape(1536, 256), right)
                    result = term if result is None else result + term
            place_rows(j, lambda block, x: result[(block * 2 + x) * 48:(block * 2 + x + 1) * 48])

        @when((j >= N_DOWN) & (j < N_DOWN + 6))
        def _():
            @when(j == N_DOWN)
            def _():
                pair_wait(0, 3)
                for k in (4, 5, 6, 7):
                    for m in range(2):
                        pair(k, m).start()

            column = pl.multiple_of((j - N_DOWN) * 512, 512)
            mine = gu_s[:, :, pl.ds(pl.multiple_of(core * FF + column, 512), 512)]
            place_regular(j, dot_tn(both(nl_s[...]), both(mine)) + dot_tn(both(peer_n[...]), both(peer_g[:, :, pl.ds(column, 512)])))

        def qkv_part(column, width):
            mine = qkv_s[:, :, pl.ds(pl.multiple_of(core * 1152 + column, 128), width)]
            far = wg[0:512, pl.ds(pl.multiple_of(1536 + column, 128), width)]
            return dot_tn(both(x_s[...]), both(mine)) + dot_tn(wg[0:512, 0:768], far)

        @when((j >= N_DOWN + 6) & (j < N_DOWN + 8))
        def _():
            @when(j == N_DOWN + 6)
            def _():
                pair_wait(4, 5, 6, 7)

            place_regular(j, qkv_part((j - N_DOWN - 6) * 512, 512))

        @when(j == N_DOWN + 8)
        def _():
            mine = ga_s[:, :, pl.ds(pl.multiple_of(core * 384, 128), 384)]
            out_part = dot_tn(both(mixed_s[...]), both(mine)) + dot_tn(wg[0:512, 768:1536], wg[0:512, 2688:3072])
            place_regular(j, jnp.concatenate([qkv_part(1024, 128), out_part], 1))

    def step(i, carry):
        @when(i < N_CHUNKS)
        def _():
            compute(i)
            for copy in a1_copies(i):
                copy.start()

        j1 = i - 1

        @when((j1 >= 0) & (j1 < N_CHUNKS))
        def _():
            slot, mine, buf = j1 % SLOTS, j1 % OWN_SLOTS, j1 % 2
            _, _, p = ring(j1 % 2)
            before = a1_copies(j1)
            after = a2_copies(j1)
            before[0].wait_recv()
            sa[buf, 0] = bf16(f32(own[mine, 0, (p + 1) % 4]) + f32(ra_relay[slot, 0]))
            after[0].start()
            before[1].wait_recv()
            sa[buf, 1] = bf16(f32(own[mine, 1, (p + 3) % 4]) + f32(ra_relay[slot, 1]))
            after[1].start()

        j2 = i - 2

        @when((j2 >= 0) & (j2 < N_CHUNKS))
        def _():
            slot, mine = j2 % SLOTS, j2 % OWN_SLOTS
            _, _, p = ring(j2 % 2)
            before = a1_copies(j2)
            after = a2_copies(j2)
            for copy in before + after:
                copy.wait_send()
            for copy in before[2:] + after:
                copy.wait_recv()
            for h in range(2):
                own_b[mine, h] = bf16(f32(own[mine, h, p]) + f32(ra_fin[slot, 0, h]) + f32(ra_fin[slot, 1, h]))
            @when(j2 < DIRECT)
            def _():
                for copy in b1_copies(j2):
                    copy.start()

            @when(j2 >= DIRECT)
            def _():
                for copy in direct_copies(j2):
                    copy.start()

        j3 = i - 3

        @when((j3 >= 0) & (j3 < DIRECT))
        def _():
            slot, mine, buf = j3 % SLOTS, j3 % OWN_SLOTS, j3 % 2
            _, _, p = ring(1 - j3 % 2)
            before = b1_copies(j3)
            after = b2_copies(j3)
            before[0].wait_recv()
            sb[buf, 0] = bf16(f32(own_b[mine, 0, (p + 1) % 4]) + f32(rb_relay[slot, 0]))
            after[0].start()
            before[1].wait_recv()
            sb[buf, 1] = bf16(f32(own_b[mine, 1, (p + 3) % 4]) + f32(rb_relay[slot, 1]))
            after[1].start()

        j4 = i - 4

        @when((j4 >= 0) & (j4 < DIRECT))
        def _():
            slot, mine, buf = j4 % SLOTS, j4 % OWN_SLOTS, j4 % 2
            _, _, p = ring(1 - j4 % 2)
            before = b1_copies(j4)
            after = b2_copies(j4)
            for copy in before + after:
                copy.wait_send()
            for copy in before[2:] + after:
                copy.wait_recv()
            total = [f32(own_b[mine, h, p]) + f32(rb_fin[slot, 0, h]) + f32(rb_fin[slot, 1, h]) for h in range(2)]
            x_send[buf] = jnp.where(xhi == 0, total[1], total[0])
            x_keep[buf] = jnp.where(xhi == 0, total[0], total[1])
            x_copy(j4).start()

        j5 = i - 5

        @when((j5 >= 0) & (j5 < DIRECT))
        def _():
            slot, buf = j5 % SLOTS, j5 % 2
            x_copy(j5).wait()

            @when(j5 < N_DOWN)
            def _():
                cols = pl.ds(pl.multiple_of(j5 * 256, 256), 256)
                o_dn[:, cols] = x_keep[buf] + x_recv[slot]

            @when(j5 >= N_DOWN)
            def _():
                c_tmp[...] = x_keep[buf] + x_recv[slot]
                for h in range(2):
                    upper, lower = c_tmp[24 * h:24 * h + 12], c_tmp[24 * h + 12:24 * h + 24]
                    c_send[buf, h, 0:12] = jnp.where(core == 0, lower, upper)
                    c_keep[buf, h, 0:12] = jnp.where(core == 0, upper, lower)
                c_copy(j5).start()

        j6 = i - 6

        @when((j6 >= N_DOWN) & (j6 < DIRECT))
        def _():
            slot, buf = j6 % SLOTS, j6 % 2
            c_copy(j6).wait()
            for source, at, who in ((c_keep, buf, core), (c_recv, slot, other)):
                for h in range(2):
                    column = pl.multiple_of(who * FF + (j6 - N_DOWN) * 512 + h * 256, 256)
                    o_gu[:, 0, pl.ds(column, 256)] = source[at, h, 0:12]

        j7 = i - 3

        @when((j7 >= DIRECT) & (j7 < N_CHUNKS))
        def _():
            late, mine = j7 - DIRECT, j7 % OWN_SLOTS
            _, _, p = ring(1 - j7 % 2)
            copies = direct_copies(j7)
            for copy in copies:
                copy.wait_send()
            for copy in copies:
                copy.wait_recv()
            total = f32(own_b[mine, xhi, p])
            for k in range(1, 8):
                total = total + f32(rz[late, k])
            c_tmp[...] = total
            for h in range(2):
                upper, lower = c_tmp[24 * h:24 * h + 12], c_tmp[24 * h + 12:24 * h + 24]
                cz_send[late, h, 0:12] = jnp.where(core == 0, lower, upper)
                cz_keep[late, h, 0:12] = jnp.where(core == 0, upper, lower)
            cz_copy(j7).start()

        j8 = i - 4

        @when((j8 >= DIRECT) & (j8 < N_CHUNKS))
        def _():
            late = j8 - DIRECT
            cz_copy(j8).wait()
            for source, who in ((cz_keep, core), (cz_recv, other)):
                @when(j8 < N_DOWN + 8)
                def _():
                    for h in range(2):
                        column = pl.multiple_of(who * 1152 + (j8 - N_DOWN - 6) * 512 + h * 256, 128)
                        o_qkv[:, 0, pl.ds(column, 256)] = source[late, h, 0:12]

                @when(j8 == N_DOWN + 8)
                def _():
                    o_qkv[:, 0, pl.ds(pl.multiple_of(who * 1152 + 1024, 128), 128)] = source[late, 0, 0:12, 0:128]
                    o_out[:, 0, pl.ds(pl.multiple_of(who * 384, 128), 128)] = source[late, 0, 0:12, 128:256]
                    o_out[:, 0, pl.ds(pl.multiple_of(who * 384 + 128, 128), 256)] = source[late, 1, 0:12]

        return carry


    def band(k):
        return pl.ds(k * BAND, BAND)

    def normalise(value):
        average = jnp.mean(value, -1, keepdims=True)
        centred = value - average
        inverse = lax.rsqrt(jnp.mean(centred * centred, -1, keepdims=True) + epsilon)
        return centred * inverse, inverse

    lanes = lax.broadcasted_iota(jnp.int32, (256, 128), 1)

    def own_lanes(e):
        return (lanes < 64) if e == 0 else (lanes >= 64)

    def forward(m, carry):
        @pl.when(first)
        def _():
            token_copy(m).wait()

        @pl.when(second)
        def _():
            hand_on(m).wait_recv()

        x = x_s[m]
        query = dot_nn(x, wq[:, 0:768]) + biases[0]
        qkv_s[m, :, 0:768] = bf16(f32(bf16(query)) * 0.125)
        qkv_s[m, :, 768:1536] = bf16(dot_nn(x, wq[:, 768:1536]))
        qkv_s[m, :, 1536:2304] = bf16(dot_nn(x, wq[:, 1536:2304]) + biases[1])

        for hp in range(6):
            at = pl.ds(hp * 128, 128)
            q2 = qkv_s[m, :, at]
            k2 = qkv_s[m, :, pl.ds(hp * 128 + 768, 128)]
            v2 = qkv_s[m, :, pl.ds(hp * 128 + 1536, 128)]
            none = jnp.zeros_like(q2)
            qs = jnp.concatenate([jnp.where(own_lanes(e), q2, none) for e in range(2)], 0)
            vs = jnp.concatenate([jnp.where(own_lanes(e), v2, none) for e in range(2)], 0)
            scores_two = dot_nt(k2, qs)
            probs_two = []
            for e in range(2):
                head = 2 * hp + e
                scores = scores_two[:, 256 * e:256 * e + 256] - 2.0 ** (-8.0 * (head + 1) / HEADS) * dist_s[m]
                expo = jnp.exp(scores - jnp.max(scores, 0, keepdims=True))
                probs = bf16(expo * (1.0 / jnp.sum(expo, 0, keepdims=True)))
                p_s[m, head] = probs
                probs_two.append(probs)
            mixed_s[m, :, at] = bf16(dot_tn(jnp.concatenate(probs_two, 0), vs))

        @pl.when(m == 0)
        def _():
            w_copies[1].wait()

        acc_s[...] = dot_nn(mixed_s[m], wo[...])
        for k in range(256 // BAND):
            r = band(k)
            value = f32(x_s[m, r]) + (acc_s[r] + biases[2])
            unit, inverse = normalise(value)
            normed = unit * gains[0:1] + biases[3]
            n1_s[m, r] = bf16(unit)
            r_s[m, r, 0:1] = inverse
            f_s[r] = normed
            nl_s[m, r] = bf16(normed)

        pair(0, m).start()

        @pl.when(m == 0)
        def _():
            w_copies[2].wait()
            w_copies[3].wait()

        @pl.when(second & (m == 1))
        def _():
            out_copy(0).wait()

        for jb in range(FF // BLOCK):
            c0 = jb * BLOCK
            low = nl_s[m]
            gate_s[...] = dot_nn(low, wg[:, c0:c0 + BLOCK])
            out_s[...] = dot_nn(low, wg[:, c0 + FF:c0 + FF + BLOCK])
            for k in range(256 // BAND):
                r = band(k)
                gate, up = gate_s[r], out_s[r]
                act, slope = gelu_terms(gate)
                gu_s[m, r, c0:c0 + BLOCK] = bf16(up * slope)
                gu_s[m, r, c0 + FF:c0 + FF + BLOCK] = bf16(act)
                gate_s[r] = act * up
            hid = bf16(gate_s[...])
            ht_s[m, 8 * jb:8 * jb + 8] = hid.T.reshape(8, 2, 48, 256)
            term = dot_nn(hid, wd[c0:c0 + BLOCK])
            if jb == 0:
                acc_s[...] = term
            else:
                acc_s[...] += term

        for k in range(256 // BAND):
            r = band(k)
            value = f_s[r] + (acc_s[r] + biases[4])
            unit, inverse = normalise(value)
            n2_s[m, r] = bf16(unit)
            r_s[m, r, 1:2] = inverse
            result = unit * gains[1:2] + biases[5]
            out_s[r] = result
            send_s[m, r] = bf16(result)

        @pl.when(first)
        def _():
            hand_on(m).start()

        @pl.when(second)
        def _():
            out_copy(m).start()

        pair(1, m).start()
        return carry

    lax.fori_loop(0, 2, forward, 0)

    def norm_back(grad, unit, inverse, gain):
        scaled = grad * gain
        mean_one = jnp.mean(scaled, -1, keepdims=True)
        mean_two = jnp.mean(scaled * unit, -1, keepdims=True)
        return inverse * (scaled - mean_one - unit * mean_two)

    def backward(m, carry):
        early = first & (m == 1)

        @pl.when(first)
        def _():
            hand_on(m).wait_send()
            hand_back(m).wait_recv()

        @pl.when(second)
        def _():
            cot_copy(m).wait()

        for k in range(256 // BAND):
            r = band(k)
            row = lax.broadcasted_iota(jnp.int32, (BAND, 1), 0) + k * BAND
            limit = jnp.where(m == 0, jnp.where(row < 128, length_a, length_b + 128), length_long)
            live = jnp.where((row < limit) | first, 1.0, 0.0)
            grad = f32(g_s[m, r]) * live
            unit = f32(n2_s[m, r])
            vec_s[1] += fold_rows(grad * unit)
            vec_s[7] += fold_rows(grad)
            grad_in = norm_back(grad, unit, r_s[m, r, 1:2], gains[1:2])
            f_s[r] = grad_in
            low = bf16(grad_in)
            gf_s[m, r] = low
            vec_s[6] += fold_rows(f32(low))

        pair(2, m).start()

        for jb in range(FF // BLOCK):
            c0 = jb * BLOCK
            gate_s[...] = dot_nt(gf_s[m], wd[c0:c0 + BLOCK])
            for k in range(256 // BAND):
                r = band(k)
                hid = gate_s[r]
                for c in (c0, c0 + FF):
                    gu_s[m, r, c:c + BLOCK] = bf16(hid * f32(gu_s[m, r, c:c + BLOCK]))
            term = dot_nt(gu_s[m, :, c0:c0 + BLOCK], wg[:, c0:c0 + BLOCK])
            term = term + dot_nt(gu_s[m, :, c0 + FF:c0 + FF + BLOCK], wg[:, c0 + FF:c0 + FF + BLOCK])
            if jb == 0:
                acc_s[...] = term
            else:
                acc_s[...] += term
            if jb == 1:
                @pl.when(early)
                def _():
                    step(0, 0)

        pair(3, m).start()

        @pl.when(early)
        def _():
            step(1, 0)

        for k in range(256 // BAND):
            r = band(k)
            grad = acc_s[r] + f_s[r]
            unit = f32(n1_s[m, r])
            vec_s[0] += fold_rows(grad * unit)
            vec_s[5] += fold_rows(grad)
            grad_in = norm_back(grad, unit, r_s[m, r, 0:1], gains[0:1])
            f_s[r] = grad_in
            low = bf16(grad_in)
            ga_s[m, r] = low
            vec_s[4] += fold_rows(f32(low))

        def mixed_back(g):
            c = g * 256
            send_s[m, :, c:c + 256] = bf16(dot_nt(ga_s[m], wo[c:c + 256]))

        def attend_back(hp):
            at = pl.ds(hp * 128, 128)
            q2 = qkv_s[m, :, at]
            k2 = qkv_s[m, :, pl.ds(hp * 128 + 768, 128)]
            v2 = qkv_s[m, :, pl.ds(hp * 128 + 1536, 128)]
            do2 = send_s[m, :, at]
            none = jnp.zeros_like(q2)
            qs, ks, ds = (
                jnp.concatenate([jnp.where(own_lanes(e), wide, none) for e in range(2)], 0) for wide in (q2, k2, do2)
            )
            grad_probs_two = dot_nt(v2, ds)
            probs_two = [p_s[m, 2 * hp + e] for e in range(2)]
            scores_two = []
            for e in range(2):
                weighted = f32(probs_two[e]) * grad_probs_two[:, 256 * e:256 * e + 256]
                total = jnp.sum(weighted, 0, keepdims=True)
                scores_two.append(bf16(weighted - f32(probs_two[e]) * total))
            grad_v = bf16(dot_nn(jnp.concatenate(probs_two, 1), ds))
            grad_k = bf16(dot_nn(jnp.concatenate(scores_two, 1), qs))
            grad_q = bf16(dot_tn(jnp.concatenate(scores_two, 0), ks) * 0.125)
            vec_s[2, :, at] += fold_rows(f32(grad_q))
            vec_s[3, :, at] += fold_rows(f32(grad_v))
            qkv_s[m, :, at] = grad_q
            qkv_s[m, :, pl.ds(hp * 128 + 768, 128)] = grad_k
            qkv_s[m, :, pl.ds(hp * 128 + 1536, 128)] = grad_v

        mixed_back(0)
        for g in range(3):
            if g < 2:
                mixed_back(g + 1)
            attend_back(2 * g)
            attend_back(2 * g + 1)
            c = g * 256
            term = dot_nt(qkv_s[m, :, c:c + 256], wq[:, c:c + 256])
            for c in (g * 256 + 768, g * 256 + 1536):
                term = term + dot_nt(qkv_s[m, :, c:c + 256], wq[:, c:c + 256])
            if g == 0:
                acc_s[...] = term
            else:
                acc_s[...] += term

        @pl.when(early)
        def _():
            step(2, 0)

        @pl.when(first & (m == 1))
        def _():
            out_copy(0).wait()

        grad_a = acc_s[...] + f_s[...]

        @pl.when(second)
        def _():
            send_s[m] = bf16(grad_a)
            hand_back(m).start()

        @pl.when(first)
        def _():
            out_s[...] = grad_a
            out_copy(m).start()

        return carry

    lax.fori_loop(0, 2, backward, 0)
    for k in range(8):
        v_acc[0, k:k + 1] = jnp.sum(vec_s[k], 0, keepdims=True)
    v_start(0)

    def tail_step(i, carry):
        step(i, carry)
        for stage in range(4):
            @pl.when(i == 2 * stage + 5)
            def _():
                v_finish(stage)
                if stage < 3:
                    v_start(stage + 1)

        return carry

    lax.fori_loop(3 * (1 - sec), N_CHUNKS + 4, tail_step, 0)
    o_vec[...] = v_acc[4]

    @pl.when(second)
    def _():
        hand_back(0).wait_send()
        hand_back(1).wait_send()

    out_copy(1).wait()


def run_layers(short_lens, long_lens, tokens, cotangent, w_qkv, w_out, w_gate_up, w_down, gains, biases):
    low, wide = jnp.bfloat16, jnp.float32
    hbm = pl.BlockSpec(memory_space=pl.ANY)
    vmem = pl.BlockSpec(memory_space=pltpu.VMEM)
    smem = pl.BlockSpec(memory_space=pltpu.SMEM)
    dma = pltpu.SemaphoreType.DMA
    of = pltpu.VMEM
    s = SLOTS
    return pl.pallas_call(
        layers_kernel,
        out_shape=[
            jax.ShapeDtypeStruct((2, 256, 768), wide),
            jax.ShapeDtypeStruct((12, 1, 2304), wide),
            jax.ShapeDtypeStruct((12, 1, 768), wide),
            jax.ShapeDtypeStruct((12, 1, 6144), wide),
            jax.ShapeDtypeStruct((48, 768), wide),
            jax.ShapeDtypeStruct((8, 768), wide),
        ],
        in_specs=[smem] * 2 + [hbm] * 6 + [vmem] * 2,
        out_specs=[hbm] + [vmem] * 5,
        scratch_shapes=[
            of((768, 2304), low), of((768, 768), low), of((768, 6144), low), of((3072, 768), low),
            of((2, 256, 768), low), of((2, 256, 768), low), of((2, 256, 2304), low), of((2, 12, 256, 256), low),
            of((2, 256, 768), low), of((2, 256, 768), low),
            of((2, 256, 768), low), of((2, 256, 768), low),
            of((2, 256, 2), wide), of((2, 256, 6144), low), of((2, 32, 2, 48, 256), low),
            of((2, 256, 768), low), of((2, 256, 768), low), of((2, 256, 768), low), of((256, 768), wide),
            of((256, 768), wide), of((256, 768), wide), of((256, BLOCK), wide),
            of((2, 256, 256), wide), of((8, 8, 768), wide),
            of((2, 256, 768), low), of((2, 32, 48, 256), low), of((2, 256, 768), low), of((2, 256, 3072), low),
            of((OWN_SLOTS, 2, 4, 4, 48, 256), low),
            of((s, 2, 4, 48, 256), low), of((s, 2, 2, 4, 48, 256), low), of((2, 2, 4, 48, 256), low),
            of((OWN_SLOTS, 2, 4, 48, 256), low),
            of((s, 2, 48, 256), low), of((s, 2, 2, 48, 256), low), of((2, 2, 48, 256), low),
            of((2, 48, 256), wide), of((2, 48, 256), wide), of((s, 48, 256), wide),
            of((48, 256), wide), of((2, 2, 16, 256), wide), of((2, 2, 16, 256), wide), of((s, 2, 16, 256), wide),
            of((3, 8, 48, 256), low), of((3, 2, 16, 256), wide), of((3, 2, 16, 256), wide), of((3, 2, 16, 256), wide),
            of((5, 8, 768), wide), of((8, 8, 768), wide),
            dma((4,)), dma((2,)), dma((2,)), dma((2,)), dma((2,)), dma((2,)), dma((2,)), dma((2,)),
            dma((8, 2)), dma((8, 2)),
            dma((s, 4)), dma((s, 2)), dma((s, 2, 2)), dma((2, 2)),
            dma((s, 4)), dma((s, 2)), dma((s, 2, 2)), dma((2, 2)),
            dma((2,)), dma((s,)), dma((2,)), dma((s,)), dma((8,)), dma((8,)),
            dma((3, 8)), dma((3, 8)), dma((3,)), dma((3,)),
        ],
        compiler_params=pltpu.CompilerParams(
            collective_id=0, has_side_effects=True, vmem_limit_bytes=VMEM_LIMIT
        ),
        cost_estimate=pl.CostEstimate(flops=3 * 10 ** 10, bytes_accessed=4 * 10 ** 7, transcendentals=10 ** 7),
        name="run_layers",
    )(short_lens, long_lens, tokens, cotangent, w_qkv, w_out, w_gate_up, w_down, gains, biases)


def place_kernel(start, boundary, qkv, out, gate_up, down, vec, o_b, o_q, o_o, o_g, o_d, o_gains, o_biases, sems):
    copies = [
        pltpu.make_async_copy(source, target, sems.at[k])
        for k, (source, target) in enumerate(
            ((boundary, o_b.at[0]), (gate_up, o_g), (qkv, o_q), (out, o_o), (down, o_d.at[0]))
        )
    ]
    for copy in copies:
        copy.start()
    mine = pltpu.roll(vec[...], lax.rem(D - start[0], D), axis=1)
    o_gains[0] = mine[:2, :12]
    o_biases[:, 0] = mine[2:, :12]
    for copy in copies:
        copy.wait()


def place(start, boundary, qkv, out, gate_up, down, vec):
    wide = jnp.float32
    vmem = pl.BlockSpec(memory_space=pltpu.VMEM)
    return pl.pallas_call(
        place_kernel,
        out_shape=[
            jax.ShapeDtypeStruct((1, 2, 256, 768), wide),
            jax.ShapeDtypeStruct((12, 1, 2304), wide),
            jax.ShapeDtypeStruct((12, 1, 768), wide),
            jax.ShapeDtypeStruct((12, 1, 6144), wide),
            jax.ShapeDtypeStruct((1, 48, 768), wide),
            jax.ShapeDtypeStruct((1, 2, 12), wide),
            jax.ShapeDtypeStruct((6, 1, 12), wide),
        ],
        in_specs=[pl.BlockSpec(memory_space=pltpu.SMEM)] + [pl.BlockSpec(memory_space=pltpu.HBM)] * 5 + [vmem],
        out_specs=[vmem] * 7,
        scratch_shapes=[pltpu.SemaphoreType.DMA((5,))],
        compiler_params=pltpu.CompilerParams(vmem_limit_bytes=VMEM_LIMIT),
        name="place",
    )(start, boundary, qkv, out, gate_up, down, vec)


def on_device(
    tokens, cotangent, short_lens, long_lens, w_qkv, w_out, w_gate_up, w_down, gains, biases
):
    boundary, q, o, g, d, vec = run_layers(
        short_lens, long_lens, tokens, cotangent, w_qkv[0], w_out[0], w_gate_up[0], w_down[0], gains[0],
        jnp.transpose(biases, (1, 0, 2)),
    )
    start = jnp.full((1,), lax.axis_index("dp") * 12, jnp.int32)
    b, q, o, g, d, gains_out, biases_out = place(start, boundary, q, o, g, d, vec)
    q, o, g, biases_out = (jnp.transpose(rows, (1, 0, 2)) for rows in (q, o, g, biases_out))
    return (b, q, o, g, d, gains_out, biases_out)


def solution(mesh):
    placed = (
        P(None, "dp", None),
        P(None, "dp", None),
        P("dp"),
        P("dp"),
        P("section", None, None),
        P("section", None, None),
        P("section", None, None),
        P("section", None, None),
        P("section", None, None),
        P("section", None, None),
    )
    return jax.shard_map(
        on_device,
        mesh=mesh,
        in_specs=placed,
        out_specs=(
            P("section", None, "dp", None),
            P("section", "dp", None),
            P("section", "dp", None),
            P("section", "dp", None),
            P("section", "dp", None),
            P("section", None, "dp"),
            P("section", None, "dp"),
        ),
        check_vma=False,
    )
```

```python
import jax
import jax.numpy as jnp
from jax import lax
from jax.experimental import pallas as pl
from jax.experimental.pallas import tpu as pltpu
from jax.sharding import PartitionSpec as P

D = 768
HEADS = 12
FF = 3072
BLOCK = 768
BAND = 32
N_CHUNKS = 12
N_DOWN = 3
DIRECT = 9
SLOTS = 5
OWN_SLOTS = 3
VMEM_LIMIT = 62 * 1024 * 1024
MESH_IDS = pl.DeviceIdType.MESH

epsilon = 1e-05
masked_distance = 1e12


def dot_nn(lhs, rhs):
    return jnp.dot(lhs, rhs, preferred_element_type=jnp.float32)


def dot_nt(lhs, rhs):
    return lax.dot_general(lhs, rhs, (((1,), (1,)), ((), ())), preferred_element_type=jnp.float32)


def dot_tn(lhs, rhs):
    return lax.dot_general(lhs, rhs, (((0,), (0,)), ((), ())), preferred_element_type=jnp.float32)


def f32(value):
    return value.astype(jnp.float32)


def bf16(value):
    return value.astype(jnp.bfloat16)


def fold_rows(value):
    return jnp.sum(value.reshape(value.shape[0] // 8, 8, value.shape[1]), 0)


def gelu_terms(gate):
    cdf = 0.5 * (1.0 + lax.erf(gate * 0.7071067811865476))
    density = jnp.exp(-0.5 * gate * gate) * 0.3989422804014327
    return gate * cdf, cdf + gate * density


def when(condition):
    if isinstance(condition, bool):
        return (lambda body: body()) if condition else (lambda body: None)
    return pl.when(condition)


def both(value):
    return value.reshape(512, value.shape[-1])


def layers_kernel(
    short_lens, long_lens, tokens, cotangent, w_qkv, w_out, w_gate_up, w_down, gains, biases,
    boundary, o_qkv, o_out, o_gu, o_dn, o_vec,
    wq, wo, wg, wd, x_s, g_s, qkv_s, p_s, mixed_s, nl_s, n1_s, n2_s, r_s, gu_s, ht_s,
    gf_s, ga_s, send_s, out_s, acc_s, f_s, gate_s, dist_s, vec_s,
    peer_n, peer_h, peer_f, peer_g,
    own, ra_relay, ra_fin, sa, own_b, rb_relay, rb_fin, sb, x_send, x_keep, x_recv, c_tmp, c_send, c_keep, c_recv,
    rz, cz_send, cz_keep, cz_recv,
    v_acc, v_recv,
    w_sem, x_sem, g_sem, out_sem, f_send, f_recv, b_send, b_recv, pair_send, pair_recv,
    a_send, a_relay_recv, a_fin_recv, a2_send,
    bb_send, bb_relay_recv, bb_fin_recv, b2_send,
    xs_sem, xr_sem, cs_sem, cr_sem, vs_sem, vr_sem,
    z_send, z_recv, czs_sem, czr_sem,
):
    sec = lax.axis_index("section")
    first = sec == 0
    second = sec == 1
    me = lax.axis_index("dp")
    core = me % 2
    xhi = (me // 2) % 2
    zz = (me // 4) % 4
    yy = me // 16
    other = 1 - core

    def dev(y, z, x, c):
        return ((y * 4 + z) * 2 + x) * 2 + c

    peer_core = dev(yy, zz, xhi, other)
    peer_x = dev(yy, zz, 1 - xhi, core)
    y_ids = [dev((yy + k) % 4, zz, xhi, core) for k in (1, 2, 3)]
    z_ids = [dev(yy, (zz + k) % 4, xhi, core) for k in (1, 2, 3)]

    yx_ids = [dev((yy + k) % 4, zz, 1 - xhi, core) for k in (1, 2, 3)]
    zx_ids = [dev(yy, (zz + k) % 4, 1 - xhi, core) for k in (1, 2, 3)]

    def remote(src, dst, send, recv, target):
        return pltpu.make_async_remote_copy(
            src_ref=src, dst_ref=dst, send_sem=send, recv_sem=recv,
            device_id={"dp": target}, device_id_type=MESH_IDS,
        )

    def across(src, dst, send, recv):
        return pltpu.make_async_remote_copy(
            src_ref=src, dst_ref=dst, send_sem=send, recv_sem=recv,
            device_id={"section": 1 - sec}, device_id_type=MESH_IDS,
        )

    w_copies = [
        pltpu.make_async_copy(w_qkv, wq, w_sem.at[0]),
        pltpu.make_async_copy(w_out, wo, w_sem.at[1]),
        pltpu.make_async_copy(w_gate_up, wg, w_sem.at[2]),
        pltpu.make_async_copy(w_down, wd, w_sem.at[3]),
    ]

    def token_copy(m):
        return pltpu.make_async_copy(tokens.at[m], x_s.at[m], x_sem.at[m])

    def cot_copy(m):
        return pltpu.make_async_copy(cotangent.at[m], g_s.at[m], g_sem.at[m])

    def hand_on(m):
        return across(send_s.at[m], x_s.at[m], f_send.at[m], f_recv.at[m])

    def hand_back(m):
        return across(send_s.at[m], g_s.at[m], b_send.at[m], b_recv.at[m])

    def out_copy(m):
        return pltpu.make_async_copy(out_s, boundary.at[m], out_sem.at[m])

    def pair(k, m):
        rows = pl.ds(m * 256, 256)
        src, dst = (
            lambda: (nl_s.at[m], peer_n.at[m]),
            lambda: (ht_s.at[m, :, other], peer_h.at[m]),
            lambda: (gf_s.at[m], peer_f.at[m]),
            lambda: (gu_s.at[m, :, pl.ds(other * FF, FF)], peer_g.at[m]),
            lambda: (x_s.at[m], wg.at[rows, pl.ds(0, 768)]),
            lambda: (mixed_s.at[m], wg.at[rows, pl.ds(768, 768)]),
            lambda: (qkv_s.at[m, :, pl.ds(other * 1152, 1152)], wg.at[rows, pl.ds(1536, 1152)]),
            lambda: (ga_s.at[m, :, pl.ds(other * 384, 384)], wg.at[rows, pl.ds(2688, 384)]),
        )[k]()
        return remote(src, dst, pair_send.at[k, m], pair_recv.at[k, m], peer_core)

    def pair_wait(*which):
        for k in which:
            for m in range(2):
                pair(k, m).wait()

    @pl.when(first)
    def _():
        token_copy(0).start()

    w_copies[0].start()
    w_copies[1].start()

    barrier = pltpu.get_barrier_semaphore()
    pl.semaphore_signal(barrier, inc=1, device_id={"section": 1 - sec}, device_id_type=MESH_IDS)
    for target in [peer_core, peer_x] + y_ids + z_ids + yx_ids + zx_ids:
        pl.semaphore_signal(barrier, inc=1, device_id={"dp": target}, device_id_type=MESH_IDS)
    pl.semaphore_wait(barrier, 15)

    vec_s[...] = jnp.zeros_like(vec_s)
    rows_j = lax.broadcasted_iota(jnp.int32, (256, 256), 0)
    cols_i = lax.broadcasted_iota(jnp.int32, (256, 256), 1)
    distance = f32(jnp.abs(rows_j - cols_i))
    length_a, length_b, length_long = short_lens[0], short_lens[1], long_lens[0]
    for m in range(2):
        if m == 0:
            limit = jnp.where(rows_j < 128, length_a, length_b + 128)
            apart = jnp.where((rows_j >> 7) == (cols_i >> 7), 0, 1024)
            ok = rows_j + apart < limit
        else:
            ok = rows_j < length_long
        dist_s[m] = jnp.where(ok, distance, masked_distance)

    w_copies[0].wait()
    w_copies[2].start()
    w_copies[3].start()

    @pl.when(first)
    def _():
        token_copy(1).start()

    @pl.when(second)
    def _():
        cot_copy(0).start()
        cot_copy(1).start()


    def v_sends(stage):
        targets = ([peer_core], [peer_x], y_ids, z_ids)[stage]
        base = (0, 1, 2, 5)[stage]
        count = len(targets)
        return [
            remote(
                v_acc.at[stage], v_recv.at[base + (count - 1 - k)],
                vs_sem.at[base + k], vr_sem.at[base + (count - 1 - k)], targets[k],
            )
            for k in range(count)
        ]

    def v_start(stage):
        for copy in v_sends(stage):
            copy.start()

    def v_finish(stage):
        base = (0, 1, 2, 5)[stage]
        copies = v_sends(stage)
        for copy in copies:
            copy.wait_send()
        for copy in copies:
            copy.wait_recv()
        total = v_acc[stage]
        for k in range(len(copies)):
            total = total + v_recv[base + k]
        v_acc[stage + 1] = total

    def ring(par):
        right = y_ids[0] * (1 - par) + z_ids[0] * par
        left = y_ids[2] * (1 - par) + z_ids[2] * par
        place = yy * (1 - par) + zz * par
        return right, left, place

    def a1_copies(j):
        slot, mine = j % SLOTS, j % OWN_SLOTS
        right, left, p = ring(j % 2)
        far, nxt, prv = (p + 2) % 4, (p + 1) % 4, (p + 3) % 4
        return (
            remote(own.at[mine, 0, far], ra_relay.at[slot, 0], a_send.at[slot, 0], a_relay_recv.at[slot, 0], right),
            remote(own.at[mine, 1, far], ra_relay.at[slot, 1], a_send.at[slot, 1], a_relay_recv.at[slot, 1], left),
            remote(own.at[mine, 1, nxt], ra_fin.at[slot, 0, 1], a_send.at[slot, 2], a_fin_recv.at[slot, 0, 1], right),
            remote(own.at[mine, 0, prv], ra_fin.at[slot, 1, 0], a_send.at[slot, 3], a_fin_recv.at[slot, 1, 0], left),
        )

    def a2_copies(j):
        slot, mine = j % SLOTS, j % 2
        right, left, _ = ring(j % 2)
        return (
            remote(sa.at[mine, 0], ra_fin.at[slot, 0, 0], a2_send.at[mine, 0], a_fin_recv.at[slot, 0, 0], right),
            remote(sa.at[mine, 1], ra_fin.at[slot, 1, 1], a2_send.at[mine, 1], a_fin_recv.at[slot, 1, 1], left),
        )

    def b1_copies(j):
        slot, mine = j % SLOTS, j % OWN_SLOTS
        right, left, p = ring(1 - j % 2)
        far, nxt, prv = (p + 2) % 4, (p + 1) % 4, (p + 3) % 4
        return (
            remote(own_b.at[mine, 0, far], rb_relay.at[slot, 0], bb_send.at[slot, 0], bb_relay_recv.at[slot, 0], right),
            remote(own_b.at[mine, 1, far], rb_relay.at[slot, 1], bb_send.at[slot, 1], bb_relay_recv.at[slot, 1], left),
            remote(own_b.at[mine, 1, nxt], rb_fin.at[slot, 0, 1], bb_send.at[slot, 2], bb_fin_recv.at[slot, 0, 1], right),
            remote(own_b.at[mine, 0, prv], rb_fin.at[slot, 1, 0], bb_send.at[slot, 3], bb_fin_recv.at[slot, 1, 0], left),
        )

    def b2_copies(j):
        slot, mine = j % SLOTS, j % 2
        right, left, _ = ring(1 - j % 2)
        return (
            remote(sb.at[mine, 0], rb_fin.at[slot, 0, 0], b2_send.at[mine, 0], bb_fin_recv.at[slot, 0, 0], right),
            remote(sb.at[mine, 1], rb_fin.at[slot, 1, 1], b2_send.at[mine, 1], bb_fin_recv.at[slot, 1, 1], left),
        )

    def x_copy(j):
        slot, mine = j % SLOTS, j % 2
        return remote(x_send.at[mine], x_recv.at[slot], xs_sem.at[mine], xr_sem.at[slot], peer_x)

    def direct_copies(j):
        late, mine = j - DIRECT, j % OWN_SLOTS
        par = 1 - j % 2
        _, _, p = ring(par)
        copies = []
        for k in range(1, 8):
            ahead, flip = k // 2, k % 2
            if ahead == 0:
                target = peer_x
            else:
                along_y, along_z = ((yx_ids, zx_ids) if flip else (y_ids, z_ids))
                target = along_y[ahead - 1] * (1 - par) + along_z[ahead - 1] * par
            seen = (4 - ahead) % 4 * 2 + flip
            copies.append(remote(
                own_b.at[mine, (xhi + flip) % 2, (p + ahead) % 4], rz.at[late, seen],
                z_send.at[late, k], z_recv.at[late, seen], target,
            ))
        return copies

    def cz_copy(j):
        late = j - DIRECT
        return remote(cz_send.at[late], cz_recv.at[late], czs_sem.at[late], czr_sem.at[late], peer_core)

    def c_copy(j):
        slot, mine = j % SLOTS, j % 2
        return remote(c_send.at[mine], c_recv.at[slot], cs_sem.at[mine], cr_sem.at[slot], peer_core)

    def place_rows(j, piece):
        mine = j % OWN_SLOTS
        par = j % 2
        for y in range(4):
            for z in range(4):
                i1 = y * (1 - par) + z * par
                i2 = z * (1 - par) + y * par
                for x in range(2):
                    own[mine, x, i1, i2] = bf16(piece(y * 4 + z, x))

    def place_regular(j, result):
        def piece(block, x):
            rows = result[block * 48 + x * 24:block * 48 + x * 24 + 24]
            return jnp.concatenate([rows[:, :256], rows[:, 256:]], 0)

        place_rows(j, piece)

    def compute(j):
        @when(j < N_DOWN)
        def _():
            @when(j == 0)
            def _():
                pair_wait(1, 2)

            cols = pl.ds(pl.multiple_of(j * 256, 256), 256) if not isinstance(j, int) else pl.ds(j * 256, 256)
            result = None
            for m in range(2):
                for left, right in ((ht_s[m, :, core], gf_s[m, :, cols]), (peer_h[m], peer_f[m, :, cols])):
                    term = dot_nn(left.reshape(1536, 256), right)
                    result = term if result is None else result + term
            place_rows(j, lambda block, x: result[(block * 2 + x) * 48:(block * 2 + x + 1) * 48])

        @when((j >= N_DOWN) & (j < N_DOWN + 6))
        def _():
            @when(j == N_DOWN)
            def _():
                pair_wait(0, 3)
                for k in (4, 5, 6, 7):
                    for m in range(2):
                        pair(k, m).start()

            column = pl.multiple_of((j - N_DOWN) * 512, 512)
            mine = gu_s[:, :, pl.ds(pl.multiple_of(core * FF + column, 512), 512)]
            place_regular(j, dot_tn(both(nl_s[...]), both(mine)) + dot_tn(both(peer_n[...]), both(peer_g[:, :, pl.ds(column, 512)])))

        def qkv_part(column, width):
            mine = qkv_s[:, :, pl.ds(pl.multiple_of(core * 1152 + column, 128), width)]
            far = wg[0:512, pl.ds(pl.multiple_of(1536 + column, 128), width)]
            return dot_tn(both(x_s[...]), both(mine)) + dot_tn(wg[0:512, 0:768], far)

        @when((j >= N_DOWN + 6) & (j < N_DOWN + 8))
        def _():
            @when(j == N_DOWN + 6)
            def _():
                pair_wait(4, 5, 6, 7)

            place_regular(j, qkv_part((j - N_DOWN - 6) * 512, 512))

        @when(j == N_DOWN + 8)
        def _():
            mine = ga_s[:, :, pl.ds(pl.multiple_of(core * 384, 128), 384)]
            out_part = dot_tn(both(mixed_s[...]), both(mine)) + dot_tn(wg[0:512, 768:1536], wg[0:512, 2688:3072])
            place_regular(j, jnp.concatenate([qkv_part(1024, 128), out_part], 1))

    def step(i, carry):
        @when(i < N_CHUNKS)
        def _():
            compute(i)
            for copy in a1_copies(i):
                copy.start()

        j1 = i - 1

        @when((j1 >= 0) & (j1 < N_CHUNKS))
        def _():
            slot, mine, buf = j1 % SLOTS, j1 % OWN_SLOTS, j1 % 2
            _, _, p = ring(j1 % 2)
            before = a1_copies(j1)
            after = a2_copies(j1)
            before[0].wait_recv()
            sa[buf, 0] = bf16(f32(own[mine, 0, (p + 1) % 4]) + f32(ra_relay[slot, 0]))
            after[0].start()
            before[1].wait_recv()
            sa[buf, 1] = bf16(f32(own[mine, 1, (p + 3) % 4]) + f32(ra_relay[slot, 1]))
            after[1].start()

        j2 = i - 2

        @when((j2 >= 0) & (j2 < N_CHUNKS))
        def _():
            slot, mine = j2 % SLOTS, j2 % OWN_SLOTS
            _, _, p = ring(j2 % 2)
            before = a1_copies(j2)
            after = a2_copies(j2)
            for copy in before + after:
                copy.wait_send()
            for copy in before[2:] + after:
                copy.wait_recv()
            for h in range(2):
                own_b[mine, h] = bf16(f32(own[mine, h, p]) + f32(ra_fin[slot, 0, h]) + f32(ra_fin[slot, 1, h]))
            @when(j2 < DIRECT)
            def _():
                for copy in b1_copies(j2):
                    copy.start()

            @when(j2 >= DIRECT)
            def _():
                for copy in direct_copies(j2):
                    copy.start()

        j3 = i - 3

        @when((j3 >= 0) & (j3 < DIRECT))
        def _():
            slot, mine, buf = j3 % SLOTS, j3 % OWN_SLOTS, j3 % 2
            _, _, p = ring(1 - j3 % 2)
            before = b1_copies(j3)
            after = b2_copies(j3)
            before[0].wait_recv()
            sb[buf, 0] = bf16(f32(own_b[mine, 0, (p + 1) % 4]) + f32(rb_relay[slot, 0]))
            after[0].start()
            before[1].wait_recv()
            sb[buf, 1] = bf16(f32(own_b[mine, 1, (p + 3) % 4]) + f32(rb_relay[slot, 1]))
            after[1].start()

        j4 = i - 4

        @when((j4 >= 0) & (j4 < DIRECT))
        def _():
            slot, mine, buf = j4 % SLOTS, j4 % OWN_SLOTS, j4 % 2
            _, _, p = ring(1 - j4 % 2)
            before = b1_copies(j4)
            after = b2_copies(j4)
            for copy in before + after:
                copy.wait_send()
            for copy in before[2:] + after:
                copy.wait_recv()
            total = [f32(own_b[mine, h, p]) + f32(rb_fin[slot, 0, h]) + f32(rb_fin[slot, 1, h]) for h in range(2)]
            x_send[buf] = jnp.where(xhi == 0, total[1], total[0])
            x_keep[buf] = jnp.where(xhi == 0, total[0], total[1])
            x_copy(j4).start()

        j5 = i - 5

        @when((j5 >= 0) & (j5 < DIRECT))
        def _():
            slot, buf = j5 % SLOTS, j5 % 2
            x_copy(j5).wait()

            @when(j5 < N_DOWN)
            def _():
                cols = pl.ds(pl.multiple_of(j5 * 256, 256), 256)
                o_dn[:, cols] = x_keep[buf] + x_recv[slot]

            @when(j5 >= N_DOWN)
            def _():
                c_tmp[...] = x_keep[buf] + x_recv[slot]
                for h in range(2):
                    upper, lower = c_tmp[24 * h:24 * h + 12], c_tmp[24 * h + 12:24 * h + 24]
                    c_send[buf, h, 0:12] = jnp.where(core == 0, lower, upper)
                    c_keep[buf, h, 0:12] = jnp.where(core == 0, upper, lower)
                c_copy(j5).start()

        j6 = i - 6

        @when((j6 >= N_DOWN) & (j6 < DIRECT))
        def _():
            slot, buf = j6 % SLOTS, j6 % 2
            c_copy(j6).wait()
            for source, at, who in ((c_keep, buf, core), (c_recv, slot, other)):
                for h in range(2):
                    column = pl.multiple_of(who * FF + (j6 - N_DOWN) * 512 + h * 256, 256)
                    o_gu[:, 0, pl.ds(column, 256)] = source[at, h, 0:12]

        j7 = i - 3

        @when((j7 >= DIRECT) & (j7 < N_CHUNKS))
        def _():
            late, mine = j7 - DIRECT, j7 % OWN_SLOTS
            _, _, p = ring(1 - j7 % 2)
            copies = direct_copies(j7)
            for copy in copies:
                copy.wait_send()
            for copy in copies:
                copy.wait_recv()
            total = f32(own_b[mine, xhi, p])
            for k in range(1, 8):
                total = total + f32(rz[late, k])
            c_tmp[...] = total
            for h in range(2):
                upper, lower = c_tmp[24 * h:24 * h + 12], c_tmp[24 * h + 12:24 * h + 24]
                cz_send[late, h, 0:12] = jnp.where(core == 0, lower, upper)
                cz_keep[late, h, 0:12] = jnp.where(core == 0, upper, lower)
            cz_copy(j7).start()

        j8 = i - 4

        @when((j8 >= DIRECT) & (j8 < N_CHUNKS))
        def _():
            late = j8 - DIRECT
            cz_copy(j8).wait()
            for source, who in ((cz_keep, core), (cz_recv, other)):
                @when(j8 < N_DOWN + 8)
                def _():
                    for h in range(2):
                        column = pl.multiple_of(who * 1152 + (j8 - N_DOWN - 6) * 512 + h * 256, 128)
                        o_qkv[:, 0, pl.ds(column, 256)] = source[late, h, 0:12]

                @when(j8 == N_DOWN + 8)
                def _():
                    o_qkv[:, 0, pl.ds(pl.multiple_of(who * 1152 + 1024, 128), 128)] = source[late, 0, 0:12, 0:128]
                    o_out[:, 0, pl.ds(pl.multiple_of(who * 384, 128), 128)] = source[late, 0, 0:12, 128:256]
                    o_out[:, 0, pl.ds(pl.multiple_of(who * 384 + 128, 128), 256)] = source[late, 1, 0:12]

        return carry


    def band(k):
        return pl.ds(k * BAND, BAND)

    def normalise(value):
        average = jnp.mean(value, -1, keepdims=True)
        centred = value - average
        inverse = lax.rsqrt(jnp.mean(centred * centred, -1, keepdims=True) + epsilon)
        return centred * inverse, inverse

    lanes = lax.broadcasted_iota(jnp.int32, (256, 128), 1)

    def own_lanes(e):
        return (lanes < 64) if e == 0 else (lanes >= 64)

    def forward(m, carry):
        @pl.when(first)
        def _():
            token_copy(m).wait()

        @pl.when(second)
        def _():
            hand_on(m).wait_recv()

        x = x_s[m]
        query = dot_nn(x, wq[:, 0:768]) + biases[0]
        qkv_s[m, :, 0:768] = bf16(f32(bf16(query)) * 0.125)
        qkv_s[m, :, 768:1536] = bf16(dot_nn(x, wq[:, 768:1536]))
        qkv_s[m, :, 1536:2304] = bf16(dot_nn(x, wq[:, 1536:2304]) + biases[1])

        for hp in range(6):
            at = pl.ds(hp * 128, 128)
            q2 = qkv_s[m, :, at]
            k2 = qkv_s[m, :, pl.ds(hp * 128 + 768, 128)]
            v2 = qkv_s[m, :, pl.ds(hp * 128 + 1536, 128)]
            none = jnp.zeros_like(q2)
            qs = jnp.concatenate([jnp.where(own_lanes(e), q2, none) for e in range(2)], 0)
            vs = jnp.concatenate([jnp.where(own_lanes(e), v2, none) for e in range(2)], 0)
            scores_two = dot_nt(k2, qs)
            probs_two = []
            for e in range(2):
                head = 2 * hp + e
                scores = scores_two[:, 256 * e:256 * e + 256] - 2.0 ** (-8.0 * (head + 1) / HEADS) * dist_s[m]
                expo = jnp.exp(scores - jnp.max(scores, 0, keepdims=True))
                probs = bf16(expo * (1.0 / jnp.sum(expo, 0, keepdims=True)))
                p_s[m, head] = probs
                probs_two.append(probs)
            mixed_s[m, :, at] = bf16(dot_tn(jnp.concatenate(probs_two, 0), vs))

        @pl.when(m == 0)
        def _():
            w_copies[1].wait()

        acc_s[...] = dot_nn(mixed_s[m], wo[...])
        for k in range(256 // BAND):
            r = band(k)
            value = f32(x_s[m, r]) + (acc_s[r] + biases[2])
            unit, inverse = normalise(value)
            normed = unit * gains[0:1] + biases[3]
            n1_s[m, r] = bf16(unit)
            r_s[m, r, 0:1] = inverse
            f_s[r] = normed
            nl_s[m, r] = bf16(normed)

        pair(0, m).start()

        @pl.when(m == 0)
        def _():
            w_copies[2].wait()
            w_copies[3].wait()

        @pl.when(second & (m == 1))
        def _():
            out_copy(0).wait()

        for jb in range(FF // BLOCK):
            c0 = jb * BLOCK
            low = nl_s[m]
            gate_s[...] = dot_nn(low, wg[:, c0:c0 + BLOCK])
            out_s[...] = dot_nn(low, wg[:, c0 + FF:c0 + FF + BLOCK])
            for k in range(256 // BAND):
                r = band(k)
                gate, up = gate_s[r], out_s[r]
                act, slope = gelu_terms(gate)
                gu_s[m, r, c0:c0 + BLOCK] = bf16(up * slope)
                gu_s[m, r, c0 + FF:c0 + FF + BLOCK] = bf16(act)
                gate_s[r] = act * up
            hid = bf16(gate_s[...])
            ht_s[m, 8 * jb:8 * jb + 8] = hid.T.reshape(8, 2, 48, 256)
            term = dot_nn(hid, wd[c0:c0 + BLOCK])
            if jb == 0:
                acc_s[...] = term
            else:
                acc_s[...] += term

        for k in range(256 // BAND):
            r = band(k)
            value = f_s[r] + (acc_s[r] + biases[4])
            unit, inverse = normalise(value)
            n2_s[m, r] = bf16(unit)
            r_s[m, r, 1:2] = inverse
            result = unit * gains[1:2] + biases[5]
            out_s[r] = result
            send_s[m, r] = bf16(result)

        @pl.when(first)
        def _():
            hand_on(m).start()

        @pl.when(second)
        def _():
            out_copy(m).start()

        pair(1, m).start()
        return carry

    lax.fori_loop(0, 2, forward, 0)

    def norm_back(grad, unit, inverse, gain):
        scaled = grad * gain
        mean_one = jnp.mean(scaled, -1, keepdims=True)
        mean_two = jnp.mean(scaled * unit, -1, keepdims=True)
        return inverse * (scaled - mean_one - unit * mean_two)

    def backward(m, carry):
        early = first & (m == 1)

        @pl.when(first)
        def _():
            hand_on(m).wait_send()
            hand_back(m).wait_recv()

        @pl.when(second)
        def _():
            cot_copy(m).wait()

        for k in range(256 // BAND):
            r = band(k)
            row = lax.broadcasted_iota(jnp.int32, (BAND, 1), 0) + k * BAND
            limit = jnp.where(m == 0, jnp.where(row < 128, length_a, length_b + 128), length_long)
            live = jnp.where((row < limit) | first, 1.0, 0.0)
            grad = f32(g_s[m, r]) * live
            unit = f32(n2_s[m, r])
            vec_s[1] += fold_rows(grad * unit)
            vec_s[7] += fold_rows(grad)
            grad_in = norm_back(grad, unit, r_s[m, r, 1:2], gains[1:2])
            f_s[r] = grad_in
            low = bf16(grad_in)
            gf_s[m, r] = low
            vec_s[6] += fold_rows(f32(low))

        pair(2, m).start()

        for jb in range(FF // BLOCK):
            c0 = jb * BLOCK
            gate_s[...] = dot_nt(gf_s[m], wd[c0:c0 + BLOCK])
            for k in range(256 // BAND):
                r = band(k)
                hid = gate_s[r]
                for c in (c0, c0 + FF):
                    gu_s[m, r, c:c + BLOCK] = bf16(hid * f32(gu_s[m, r, c:c + BLOCK]))
            term = dot_nt(gu_s[m, :, c0:c0 + BLOCK], wg[:, c0:c0 + BLOCK])
            term = term + dot_nt(gu_s[m, :, c0 + FF:c0 + FF + BLOCK], wg[:, c0 + FF:c0 + FF + BLOCK])
            if jb == 0:
                acc_s[...] = term
            else:
                acc_s[...] += term
            if jb == 0:
                @pl.when(early)
                def _():
                    step(0, 0)

        pair(3, m).start()

        @pl.when(early)
        def _():
            step(1, 0)

        for k in range(256 // BAND):
            r = band(k)
            grad = acc_s[r] + f_s[r]
            unit = f32(n1_s[m, r])
            vec_s[0] += fold_rows(grad * unit)
            vec_s[5] += fold_rows(grad)
            grad_in = norm_back(grad, unit, r_s[m, r, 0:1], gains[0:1])
            f_s[r] = grad_in
            low = bf16(grad_in)
            ga_s[m, r] = low
            vec_s[4] += fold_rows(f32(low))

        def mixed_back(g):
            c = g * 256
            send_s[m, :, c:c + 256] = bf16(dot_nt(ga_s[m], wo[c:c + 256]))

        def attend_back(hp):
            at = pl.ds(hp * 128, 128)
            q2 = qkv_s[m, :, at]
            k2 = qkv_s[m, :, pl.ds(hp * 128 + 768, 128)]
            v2 = qkv_s[m, :, pl.ds(hp * 128 + 1536, 128)]
            do2 = send_s[m, :, at]
            none = jnp.zeros_like(q2)
            qs, ks, ds = (
                jnp.concatenate([jnp.where(own_lanes(e), wide, none) for e in range(2)], 0) for wide in (q2, k2, do2)
            )
            grad_probs_two = dot_nt(v2, ds)
            probs_two = [p_s[m, 2 * hp + e] for e in range(2)]
            scores_two = []
            for e in range(2):
                weighted = f32(probs_two[e]) * grad_probs_two[:, 256 * e:256 * e + 256]
                total = jnp.sum(weighted, 0, keepdims=True)
                scores_two.append(bf16(weighted - f32(probs_two[e]) * total))
            grad_v = bf16(dot_nn(jnp.concatenate(probs_two, 1), ds))
            grad_k = bf16(dot_nn(jnp.concatenate(scores_two, 1), qs))
            grad_q = bf16(dot_tn(jnp.concatenate(scores_two, 0), ks) * 0.125)
            vec_s[2, :, at] += fold_rows(f32(grad_q))
            vec_s[3, :, at] += fold_rows(f32(grad_v))
            qkv_s[m, :, at] = grad_q
            qkv_s[m, :, pl.ds(hp * 128 + 768, 128)] = grad_k
            qkv_s[m, :, pl.ds(hp * 128 + 1536, 128)] = grad_v

        mixed_back(0)
        for g in range(3):
            if g < 2:
                mixed_back(g + 1)
            attend_back(2 * g)
            attend_back(2 * g + 1)
            c = g * 256
            term = dot_nt(qkv_s[m, :, c:c + 256], wq[:, c:c + 256])
            for c in (g * 256 + 768, g * 256 + 1536):
                term = term + dot_nt(qkv_s[m, :, c:c + 256], wq[:, c:c + 256])
            if g == 0:
                acc_s[...] = term
            else:
                acc_s[...] += term

        @pl.when(early)
        def _():
            step(2, 0)

        @pl.when(first & (m == 1))
        def _():
            out_copy(0).wait()

        grad_a = acc_s[...] + f_s[...]

        @pl.when(second)
        def _():
            send_s[m] = bf16(grad_a)
            hand_back(m).start()

        @pl.when(first)
        def _():
            out_s[...] = grad_a
            out_copy(m).start()

        return carry

    lax.fori_loop(0, 2, backward, 0)
    for k in range(8):
        v_acc[0, k:k + 1] = jnp.sum(vec_s[k], 0, keepdims=True)
    v_start(0)

    def tail_step(i, carry):
        step(i, carry)
        for stage in range(4):
            @pl.when(i == 2 * stage + 5)
            def _():
                v_finish(stage)
                if stage < 3:
                    v_start(stage + 1)

        return carry

    lax.fori_loop(3 * (1 - sec), N_CHUNKS + 4, tail_step, 0)
    o_vec[...] = v_acc[4]

    @pl.when(second)
    def _():
        hand_back(0).wait_send()
        hand_back(1).wait_send()

    out_copy(1).wait()


def run_layers(short_lens, long_lens, tokens, cotangent, w_qkv, w_out, w_gate_up, w_down, gains, biases):
    low, wide = jnp.bfloat16, jnp.float32
    hbm = pl.BlockSpec(memory_space=pl.ANY)
    vmem = pl.BlockSpec(memory_space=pltpu.VMEM)
    smem = pl.BlockSpec(memory_space=pltpu.SMEM)
    dma = pltpu.SemaphoreType.DMA
    of = pltpu.VMEM
    s = SLOTS
    return pl.pallas_call(
        layers_kernel,
        out_shape=[
            jax.ShapeDtypeStruct((2, 256, 768), wide),
            jax.ShapeDtypeStruct((12, 1, 2304), wide),
            jax.ShapeDtypeStruct((12, 1, 768), wide),
            jax.ShapeDtypeStruct((12, 1, 6144), wide),
            jax.ShapeDtypeStruct((48, 768), wide),
            jax.ShapeDtypeStruct((8, 768), wide),
        ],
        in_specs=[smem] * 2 + [hbm] * 6 + [vmem] * 2,
        out_specs=[hbm] + [vmem] * 5,
        scratch_shapes=[
            of((768, 2304), low), of((768, 768), low), of((768, 6144), low), of((3072, 768), low),
            of((2, 256, 768), low), of((2, 256, 768), low), of((2, 256, 2304), low), of((2, 12, 256, 256), low),
            of((2, 256, 768), low), of((2, 256, 768), low),
            of((2, 256, 768), low), of((2, 256, 768), low),
            of((2, 256, 2), wide), of((2, 256, 6144), low), of((2, 32, 2, 48, 256), low),
            of((2, 256, 768), low), of((2, 256, 768), low), of((2, 256, 768), low), of((256, 768), wide),
            of((256, 768), wide), of((256, 768), wide), of((256, BLOCK), wide),
            of((2, 256, 256), wide), of((8, 8, 768), wide),
            of((2, 256, 768), low), of((2, 32, 48, 256), low), of((2, 256, 768), low), of((2, 256, 3072), low),
            of((OWN_SLOTS, 2, 4, 4, 48, 256), low),
            of((s, 2, 4, 48, 256), low), of((s, 2, 2, 4, 48, 256), low), of((2, 2, 4, 48, 256), low),
            of((OWN_SLOTS, 2, 4, 48, 256), low),
            of((s, 2, 48, 256), low), of((s, 2, 2, 48, 256), low), of((2, 2, 48, 256), low),
            of((2, 48, 256), wide), of((2, 48, 256), wide), of((s, 48, 256), wide),
            of((48, 256), wide), of((2, 2, 16, 256), wide), of((2, 2, 16, 256), wide), of((s, 2, 16, 256), wide),
            of((3, 8, 48, 256), low), of((3, 2, 16, 256), wide), of((3, 2, 16, 256), wide), of((3, 2, 16, 256), wide),
            of((5, 8, 768), wide), of((8, 8, 768), wide),
            dma((4,)), dma((2,)), dma((2,)), dma((2,)), dma((2,)), dma((2,)), dma((2,)), dma((2,)),
            dma((8, 2)), dma((8, 2)),
            dma((s, 4)), dma((s, 2)), dma((s, 2, 2)), dma((2, 2)),
            dma((s, 4)), dma((s, 2)), dma((s, 2, 2)), dma((2, 2)),
            dma((2,)), dma((s,)), dma((2,)), dma((s,)), dma((8,)), dma((8,)),
            dma((3, 8)), dma((3, 8)), dma((3,)), dma((3,)),
        ],
        compiler_params=pltpu.CompilerParams(
            collective_id=0, has_side_effects=True, vmem_limit_bytes=VMEM_LIMIT
        ),
        cost_estimate=pl.CostEstimate(flops=3 * 10 ** 10, bytes_accessed=4 * 10 ** 7, transcendentals=10 ** 7),
        name="run_layers",
    )(short_lens, long_lens, tokens, cotangent, w_qkv, w_out, w_gate_up, w_down, gains, biases)


def place_kernel(start, boundary, qkv, out, gate_up, down, vec, o_b, o_q, o_o, o_g, o_d, o_gains, o_biases, sems):
    copies = [
        pltpu.make_async_copy(source, target, sems.at[k])
        for k, (source, target) in enumerate(
            ((boundary, o_b.at[0]), (gate_up, o_g), (qkv, o_q), (out, o_o), (down, o_d.at[0]))
        )
    ]
    for copy in copies:
        copy.start()
    mine = pltpu.roll(vec[...], lax.rem(D - start[0], D), axis=1)
    o_gains[0] = mine[:2, :12]
    o_biases[:, 0] = mine[2:, :12]
    for copy in copies:
        copy.wait()


def place(start, boundary, qkv, out, gate_up, down, vec):
    wide = jnp.float32
    vmem = pl.BlockSpec(memory_space=pltpu.VMEM)
    return pl.pallas_call(
        place_kernel,
        out_shape=[
            jax.ShapeDtypeStruct((1, 2, 256, 768), wide),
            jax.ShapeDtypeStruct((12, 1, 2304), wide),
            jax.ShapeDtypeStruct((12, 1, 768), wide),
            jax.ShapeDtypeStruct((12, 1, 6144), wide),
            jax.ShapeDtypeStruct((1, 48, 768), wide),
            jax.ShapeDtypeStruct((1, 2, 12), wide),
            jax.ShapeDtypeStruct((6, 1, 12), wide),
        ],
        in_specs=[pl.BlockSpec(memory_space=pltpu.SMEM)] + [pl.BlockSpec(memory_space=pltpu.HBM)] * 5 + [vmem],
        out_specs=[vmem] * 7,
        scratch_shapes=[pltpu.SemaphoreType.DMA((5,))],
        compiler_params=pltpu.CompilerParams(vmem_limit_bytes=VMEM_LIMIT),
        name="place",
    )(start, boundary, qkv, out, gate_up, down, vec)


def on_device(
    tokens, cotangent, short_lens, long_lens, w_qkv, w_out, w_gate_up, w_down, gains, biases
):
    boundary, q, o, g, d, vec = run_layers(
        short_lens, long_lens, tokens, cotangent, w_qkv[0], w_out[0], w_gate_up[0], w_down[0], gains[0],
        jnp.transpose(biases, (1, 0, 2)),
    )
    start = jnp.full((1,), lax.axis_index("dp") * 12, jnp.int32)
    b, q, o, g, d, gains_out, biases_out = place(start, boundary, q, o, g, d, vec)
    q, o, g, biases_out = (jnp.transpose(rows, (1, 0, 2)) for rows in (q, o, g, biases_out))
    return (b, q, o, g, d, gains_out, biases_out)


def solution(mesh):
    placed = (
        P(None, "dp", None),
        P(None, "dp", None),
        P("dp"),
        P("dp"),
        P("section", None, None),
        P("section", None, None),
        P("section", None, None),
        P("section", None, None),
        P("section", None, None),
        P("section", None, None),
    )
    return jax.shard_map(
        on_device,
        mesh=mesh,
        in_specs=placed,
        out_specs=(
            P("section", None, "dp", None),
            P("section", "dp", None),
            P("section", "dp", None),
            P("section", "dp", None),
            P("section", "dp", None),
            P("section", None, "dp"),
            P("section", None, "dp"),
        ),
        check_vma=False,
    )
```

```python
import jax
import jax.numpy as jnp
from jax import lax
from jax.experimental import pallas as pl
from jax.experimental.pallas import tpu as pltpu
from jax.sharding import PartitionSpec as P

D = 768
HEADS = 12
FF = 3072
BLOCK = 768
BAND = 32
N_CHUNKS = 12
N_DOWN = 3
DIRECT = 9
SLOTS = 5
OWN_SLOTS = 3
VMEM_LIMIT = 62 * 1024 * 1024
MESH_IDS = pl.DeviceIdType.MESH

epsilon = 1e-05
masked_distance = 1e12


def dot_nn(lhs, rhs):
    return jnp.dot(lhs, rhs, preferred_element_type=jnp.float32)


def dot_nt(lhs, rhs):
    return lax.dot_general(lhs, rhs, (((1,), (1,)), ((), ())), preferred_element_type=jnp.float32)


def dot_tn(lhs, rhs):
    return lax.dot_general(lhs, rhs, (((0,), (0,)), ((), ())), preferred_element_type=jnp.float32)


def f32(value):
    return value.astype(jnp.float32)


def bf16(value):
    return value.astype(jnp.bfloat16)


def fold_rows(value):
    return jnp.sum(value.reshape(value.shape[0] // 8, 8, value.shape[1]), 0)


def gelu_terms(gate):
    cdf = 0.5 * (1.0 + lax.erf(gate * 0.7071067811865476))
    density = jnp.exp(-0.5 * gate * gate) * 0.3989422804014327
    return gate * cdf, cdf + gate * density


def when(condition):
    if isinstance(condition, bool):
        return (lambda body: body()) if condition else (lambda body: None)
    return pl.when(condition)


def both(value):
    return value.reshape(512, value.shape[-1])


def layers_kernel(
    short_lens, long_lens, tokens, cotangent, w_qkv, w_out, w_gate_up, w_down, gains, biases,
    boundary, o_qkv, o_out, o_gu, o_dn, o_vec,
    wq, wo, wg, wd, x_s, g_s, qkv_s, p_s, mixed_s, nl_s, n1_s, n2_s, r_s, gu_s, ht_s,
    gf_s, ga_s, send_s, out_s, acc_s, f_s, gate_s, dist_s, vec_s,
    peer_n, peer_h, peer_f, peer_g,
    own, ra_relay, ra_fin, sa, own_b, rb_relay, rb_fin, sb, x_send, x_keep, x_recv, c_tmp, c_send, c_keep, c_recv,
    rz, cz_send, cz_keep, cz_recv,
    v_acc, v_recv,
    w_sem, x_sem, g_sem, out_sem, f_send, f_recv, b_send, b_recv, pair_send, pair_recv,
    a_send, a_relay_recv, a_fin_recv, a2_send,
    bb_send, bb_relay_recv, bb_fin_recv, b2_send,
    xs_sem, xr_sem, cs_sem, cr_sem, vs_sem, vr_sem,
    z_send, z_recv, czs_sem, czr_sem,
):
    sec = lax.axis_index("section")
    first = sec == 0
    second = sec == 1
    me = lax.axis_index("dp")
    core = me % 2
    xhi = (me // 2) % 2
    zz = (me // 4) % 4
    yy = me // 16
    other = 1 - core

    def dev(y, z, x, c):
        return ((y * 4 + z) * 2 + x) * 2 + c

    peer_core = dev(yy, zz, xhi, other)
    peer_x = dev(yy, zz, 1 - xhi, core)
    y_ids = [dev((yy + k) % 4, zz, xhi, core) for k in (1, 2, 3)]
    z_ids = [dev(yy, (zz + k) % 4, xhi, core) for k in (1, 2, 3)]

    yx_ids = [dev((yy + k) % 4, zz, 1 - xhi, core) for k in (1, 2, 3)]
    zx_ids = [dev(yy, (zz + k) % 4, 1 - xhi, core) for k in (1, 2, 3)]

    def remote(src, dst, send, recv, target):
        return pltpu.make_async_remote_copy(
            src_ref=src, dst_ref=dst, send_sem=send, recv_sem=recv,
            device_id={"dp": target}, device_id_type=MESH_IDS,
        )

    def across(src, dst, send, recv):
        return pltpu.make_async_remote_copy(
            src_ref=src, dst_ref=dst, send_sem=send, recv_sem=recv,
            device_id={"section": 1 - sec}, device_id_type=MESH_IDS,
        )

    w_copies = [
        pltpu.make_async_copy(w_qkv, wq, w_sem.at[0]),
        pltpu.make_async_copy(w_out, wo, w_sem.at[1]),
        pltpu.make_async_copy(w_gate_up, wg, w_sem.at[2]),
        pltpu.make_async_copy(w_down, wd, w_sem.at[3]),
    ]

    def token_copy(m):
        return pltpu.make_async_copy(tokens.at[m], x_s.at[m], x_sem.at[m])

    def cot_copy(m):
        return pltpu.make_async_copy(cotangent.at[m], g_s.at[m], g_sem.at[m])

    def hand_on(m):
        return across(send_s.at[m], x_s.at[m], f_send.at[m], f_recv.at[m])

    def hand_back(m):
        return across(send_s.at[m], g_s.at[m], b_send.at[m], b_recv.at[m])

    def out_copy(m):
        return pltpu.make_async_copy(out_s, boundary.at[m], out_sem.at[m])

    def pair(k, m):
        rows = pl.ds(m * 256, 256)
        src, dst = (
            lambda: (nl_s.at[m], peer_n.at[m]),
            lambda: (ht_s.at[m, :, other], peer_h.at[m]),
            lambda: (gf_s.at[m], peer_f.at[m]),
            lambda: (gu_s.at[m, :, pl.ds(other * FF, FF)], peer_g.at[m]),
            lambda: (x_s.at[m], wg.at[rows, pl.ds(0, 768)]),
            lambda: (mixed_s.at[m], wg.at[rows, pl.ds(768, 768)]),
            lambda: (qkv_s.at[m, :, pl.ds(other * 1152, 1152)], wg.at[rows, pl.ds(1536, 1152)]),
            lambda: (ga_s.at[m, :, pl.ds(other * 384, 384)], wg.at[rows, pl.ds(2688, 384)]),
        )[k]()
        return remote(src, dst, pair_send.at[k, m], pair_recv.at[k, m], peer_core)

    def pair_wait(*which):
        for k in which:
            for m in range(2):
                pair(k, m).wait()

    @pl.when(first)
    def _():
        token_copy(0).start()

    w_copies[0].start()
    w_copies[1].start()

    barrier = pltpu.get_barrier_semaphore()
    pl.semaphore_signal(barrier, inc=1, device_id={"section": 1 - sec}, device_id_type=MESH_IDS)
    for target in [peer_core, peer_x] + y_ids + z_ids + yx_ids + zx_ids:
        pl.semaphore_signal(barrier, inc=1, device_id={"dp": target}, device_id_type=MESH_IDS)
    pl.semaphore_wait(barrier, 15)

    vec_s[...] = jnp.zeros_like(vec_s)
    rows_j = lax.broadcasted_iota(jnp.int32, (256, 256), 0)
    cols_i = lax.broadcasted_iota(jnp.int32, (256, 256), 1)
    distance = f32(jnp.abs(rows_j - cols_i))
    length_a, length_b, length_long = short_lens[0], short_lens[1], long_lens[0]
    for m in range(2):
        if m == 0:
            limit = jnp.where(rows_j < 128, length_a, length_b + 128)
            apart = jnp.where((rows_j >> 7) == (cols_i >> 7), 0, 1024)
            ok = rows_j + apart < limit
        else:
            ok = rows_j < length_long
        dist_s[m] = jnp.where(ok, distance, masked_distance)

    w_copies[0].wait()
    w_copies[2].start()
    w_copies[3].start()

    @pl.when(first)
    def _():
        token_copy(1).start()

    @pl.when(second)
    def _():
        cot_copy(0).start()
        cot_copy(1).start()


    def v_sends(stage):
        targets = ([peer_core], [peer_x], y_ids, z_ids)[stage]
        base = (0, 1, 2, 5)[stage]
        count = len(targets)
        return [
            remote(
                v_acc.at[stage], v_recv.at[base + (count - 1 - k)],
                vs_sem.at[base + k], vr_sem.at[base + (count - 1 - k)], targets[k],
            )
            for k in range(count)
        ]

    def v_start(stage):
        for copy in v_sends(stage):
            copy.start()

    def v_finish(stage):
        base = (0, 1, 2, 5)[stage]
        copies = v_sends(stage)
        for copy in copies:
            copy.wait_send()
        for copy in copies:
            copy.wait_recv()
        total = v_acc[stage]
        for k in range(len(copies)):
            total = total + v_recv[base + k]
        v_acc[stage + 1] = total

    def ring(par):
        right = y_ids[0] * (1 - par) + z_ids[0] * par
        left = y_ids[2] * (1 - par) + z_ids[2] * par
        place = yy * (1 - par) + zz * par
        return right, left, place

    def a1_copies(j):
        slot, mine = j % SLOTS, j % OWN_SLOTS
        right, left, p = ring(j % 2)
        far, nxt, prv = (p + 2) % 4, (p + 1) % 4, (p + 3) % 4
        return (
            remote(own.at[mine, 0, far], ra_relay.at[slot, 0], a_send.at[slot, 0], a_relay_recv.at[slot, 0], right),
            remote(own.at[mine, 1, far], ra_relay.at[slot, 1], a_send.at[slot, 1], a_relay_recv.at[slot, 1], left),
            remote(own.at[mine, 1, nxt], ra_fin.at[slot, 0, 1], a_send.at[slot, 2], a_fin_recv.at[slot, 0, 1], right),
            remote(own.at[mine, 0, prv], ra_fin.at[slot, 1, 0], a_send.at[slot, 3], a_fin_recv.at[slot, 1, 0], left),
        )

    def a2_copies(j):
        slot, mine = j % SLOTS, j % 2
        right, left, _ = ring(j % 2)
        return (
            remote(sa.at[mine, 0], ra_fin.at[slot, 0, 0], a2_send.at[mine, 0], a_fin_recv.at[slot, 0, 0], right),
            remote(sa.at[mine, 1], ra_fin.at[slot, 1, 1], a2_send.at[mine, 1], a_fin_recv.at[slot, 1, 1], left),
        )

    def b1_copies(j):
        slot, mine = j % SLOTS, j % OWN_SLOTS
        right, left, p = ring(1 - j % 2)
        far, nxt, prv = (p + 2) % 4, (p + 1) % 4, (p + 3) % 4
        return (
            remote(own_b.at[mine, 0, far], rb_relay.at[slot, 0], bb_send.at[slot, 0], bb_relay_recv.at[slot, 0], right),
            remote(own_b.at[mine, 1, far], rb_relay.at[slot, 1], bb_send.at[slot, 1], bb_relay_recv.at[slot, 1], left),
            remote(own_b.at[mine, 1, nxt], rb_fin.at[slot, 0, 1], bb_send.at[slot, 2], bb_fin_recv.at[slot, 0, 1], right),
            remote(own_b.at[mine, 0, prv], rb_fin.at[slot, 1, 0], bb_send.at[slot, 3], bb_fin_recv.at[slot, 1, 0], left),
        )

    def b2_copies(j):
        slot, mine = j % SLOTS, j % 2
        right, left, _ = ring(1 - j % 2)
        return (
            remote(sb.at[mine, 0], rb_fin.at[slot, 0, 0], b2_send.at[mine, 0], bb_fin_recv.at[slot, 0, 0], right),
            remote(sb.at[mine, 1], rb_fin.at[slot, 1, 1], b2_send.at[mine, 1], bb_fin_recv.at[slot, 1, 1], left),
        )

    def x_copy(j):
        slot, mine = j % SLOTS, j % 2
        return remote(x_send.at[mine], x_recv.at[slot], xs_sem.at[mine], xr_sem.at[slot], peer_x)

    def direct_copies(j):
        late, mine = j - DIRECT, j % OWN_SLOTS
        par = 1 - j % 2
        _, _, p = ring(par)
        copies = []
        for k in range(1, 8):
            ahead, flip = k // 2, k % 2
            if ahead == 0:
                target = peer_x
            else:
                along_y, along_z = ((yx_ids, zx_ids) if flip else (y_ids, z_ids))
                target = along_y[ahead - 1] * (1 - par) + along_z[ahead - 1] * par
            seen = (4 - ahead) % 4 * 2 + flip
            copies.append(remote(
                own_b.at[mine, (xhi + flip) % 2, (p + ahead) % 4], rz.at[late, seen],
                z_send.at[late, k], z_recv.at[late, seen], target,
            ))
        return copies

    def cz_copy(j):
        late = j - DIRECT
        return remote(cz_send.at[late], cz_recv.at[late], czs_sem.at[late], czr_sem.at[late], peer_core)

    def c_copy(j):
        slot, mine = j % SLOTS, j % 2
        return remote(c_send.at[mine], c_recv.at[slot], cs_sem.at[mine], cr_sem.at[slot], peer_core)

    def place_rows(j, piece):
        mine = j % OWN_SLOTS
        par = j % 2
        for y in range(4):
            for z in range(4):
                i1 = y * (1 - par) + z * par
                i2 = z * (1 - par) + y * par
                for x in range(2):
                    own[mine, x, i1, i2] = bf16(piece(y * 4 + z, x))

    def place_regular(j, result):
        def piece(block, x):
            rows = result[block * 48 + x * 24:block * 48 + x * 24 + 24]
            return jnp.concatenate([rows[:, :256], rows[:, 256:]], 0)

        place_rows(j, piece)

    def compute(j):
        @when(j < N_DOWN)
        def _():
            @when(j == 0)
            def _():
                pair_wait(1, 2)

            cols = pl.ds(pl.multiple_of(j * 256, 256), 256) if not isinstance(j, int) else pl.ds(j * 256, 256)
            result = None
            for m in range(2):
                for left, right in ((ht_s[m, :, core], gf_s[m, :, cols]), (peer_h[m], peer_f[m, :, cols])):
                    term = dot_nn(left.reshape(1536, 256), right)
                    result = term if result is None else result + term
            place_rows(j, lambda block, x: result[(block * 2 + x) * 48:(block * 2 + x + 1) * 48])

        @when((j >= N_DOWN) & (j < N_DOWN + 6))
        def _():
            @when(j == N_DOWN)
            def _():
                pair_wait(0, 3)
                for k in (4, 5, 6, 7):
                    for m in range(2):
                        pair(k, m).start()

            column = pl.multiple_of((j - N_DOWN) * 512, 512)
            mine = gu_s[:, :, pl.ds(pl.multiple_of(core * FF + column, 512), 512)]
            place_regular(j, dot_tn(both(nl_s[...]), both(mine)) + dot_tn(both(peer_n[...]), both(peer_g[:, :, pl.ds(column, 512)])))

        def qkv_part(column, width):
            mine = qkv_s[:, :, pl.ds(pl.multiple_of(core * 1152 + column, 128), width)]
            far = wg[0:512, pl.ds(pl.multiple_of(1536 + column, 128), width)]
            return dot_tn(both(x_s[...]), both(mine)) + dot_tn(wg[0:512, 0:768], far)

        @when((j >= N_DOWN + 6) & (j < N_DOWN + 8))
        def _():
            @when(j == N_DOWN + 6)
            def _():
                pair_wait(4, 5, 6, 7)

            place_regular(j, qkv_part((j - N_DOWN - 6) * 512, 512))

        @when(j == N_DOWN + 8)
        def _():
            mine = ga_s[:, :, pl.ds(pl.multiple_of(core * 384, 128), 384)]
            out_part = dot_tn(both(mixed_s[...]), both(mine)) + dot_tn(wg[0:512, 768:1536], wg[0:512, 2688:3072])
            place_regular(j, jnp.concatenate([qkv_part(1024, 128), out_part], 1))

    def step(i, carry):
        @when(i < N_CHUNKS)
        def _():
            compute(i)
            for copy in a1_copies(i):
                copy.start()

        j1 = i - 1

        @when((j1 >= 0) & (j1 < N_CHUNKS))
        def _():
            slot, mine, buf = j1 % SLOTS, j1 % OWN_SLOTS, j1 % 2
            _, _, p = ring(j1 % 2)
            before = a1_copies(j1)
            after = a2_copies(j1)
            before[0].wait_recv()
            sa[buf, 0] = bf16(f32(own[mine, 0, (p + 1) % 4]) + f32(ra_relay[slot, 0]))
            after[0].start()
            before[1].wait_recv()
            sa[buf, 1] = bf16(f32(own[mine, 1, (p + 3) % 4]) + f32(ra_relay[slot, 1]))
            after[1].start()

        j2 = i - 2

        @when((j2 >= 0) & (j2 < N_CHUNKS))
        def _():
            slot, mine = j2 % SLOTS, j2 % OWN_SLOTS
            _, _, p = ring(j2 % 2)
            before = a1_copies(j2)
            after = a2_copies(j2)
            for copy in before + after:
                copy.wait_send()
            for copy in before[2:] + after:
                copy.wait_recv()
            for h in range(2):
                own_b[mine, h] = bf16(f32(own[mine, h, p]) + f32(ra_fin[slot, 0, h]) + f32(ra_fin[slot, 1, h]))
            @when(j2 < DIRECT)
            def _():
                for copy in b1_copies(j2):
                    copy.start()

            @when(j2 >= DIRECT)
            def _():
                for copy in direct_copies(j2):
                    copy.start()

        j3 = i - 3

        @when((j3 >= 0) & (j3 < DIRECT))
        def _():
            slot, mine, buf = j3 % SLOTS, j3 % OWN_SLOTS, j3 % 2
            _, _, p = ring(1 - j3 % 2)
            before = b1_copies(j3)
            after = b2_copies(j3)
            before[0].wait_recv()
            sb[buf, 0] = bf16(f32(own_b[mine, 0, (p + 1) % 4]) + f32(rb_relay[slot, 0]))
            after[0].start()
            before[1].wait_recv()
            sb[buf, 1] = bf16(f32(own_b[mine, 1, (p + 3) % 4]) + f32(rb_relay[slot, 1]))
            after[1].start()

        j4 = i - 4

        @when((j4 >= 0) & (j4 < DIRECT))
        def _():
            slot, mine, buf = j4 % SLOTS, j4 % OWN_SLOTS, j4 % 2
            _, _, p = ring(1 - j4 % 2)
            before = b1_copies(j4)
            after = b2_copies(j4)
            for copy in before + after:
                copy.wait_send()
            for copy in before[2:] + after:
                copy.wait_recv()
            total = [f32(own_b[mine, h, p]) + f32(rb_fin[slot, 0, h]) + f32(rb_fin[slot, 1, h]) for h in range(2)]
            x_send[buf] = jnp.where(xhi == 0, total[1], total[0])
            x_keep[buf] = jnp.where(xhi == 0, total[0], total[1])
            x_copy(j4).start()

        j5 = i - 5

        @when((j5 >= 0) & (j5 < DIRECT))
        def _():
            slot, buf = j5 % SLOTS, j5 % 2
            x_copy(j5).wait()

            @when(j5 < N_DOWN)
            def _():
                cols = pl.ds(pl.multiple_of(j5 * 256, 256), 256)
                o_dn[:, cols] = x_keep[buf] + x_recv[slot]

            @when(j5 >= N_DOWN)
            def _():
                c_tmp[...] = x_keep[buf] + x_recv[slot]
                for h in range(2):
                    upper, lower = c_tmp[24 * h:24 * h + 12], c_tmp[24 * h + 12:24 * h + 24]
                    c_send[buf, h, 0:12] = jnp.where(core == 0, lower, upper)
                    c_keep[buf, h, 0:12] = jnp.where(core == 0, upper, lower)
                c_copy(j5).start()

        j6 = i - 6

        @when((j6 >= N_DOWN) & (j6 < DIRECT))
        def _():
            slot, buf = j6 % SLOTS, j6 % 2
            c_copy(j6).wait()
            for source, at, who in ((c_keep, buf, core), (c_recv, slot, other)):
                for h in range(2):
                    column = pl.multiple_of(who * FF + (j6 - N_DOWN) * 512 + h * 256, 256)
                    o_gu[:, 0, pl.ds(column, 256)] = source[at, h, 0:12]

        j7 = i - 3

        @when((j7 >= DIRECT) & (j7 < N_CHUNKS))
        def _():
            late, mine = j7 - DIRECT, j7 % OWN_SLOTS
            _, _, p = ring(1 - j7 % 2)
            copies = direct_copies(j7)
            for copy in copies:
                copy.wait_send()
            for copy in copies:
                copy.wait_recv()
            total = f32(own_b[mine, xhi, p])
            for k in range(1, 8):
                total = total + f32(rz[late, k])
            c_tmp[...] = total
            for h in range(2):
                upper, lower = c_tmp[24 * h:24 * h + 12], c_tmp[24 * h + 12:24 * h + 24]
                cz_send[late, h, 0:12] = jnp.where(core == 0, lower, upper)
                cz_keep[late, h, 0:12] = jnp.where(core == 0, upper, lower)
            cz_copy(j7).start()

        j8 = i - 4

        @when((j8 >= DIRECT) & (j8 < N_CHUNKS))
        def _():
            late = j8 - DIRECT
            cz_copy(j8).wait()
            for source, who in ((cz_keep, core), (cz_recv, other)):
                @when(j8 < N_DOWN + 8)
                def _():
                    for h in range(2):
                        column = pl.multiple_of(who * 1152 + (j8 - N_DOWN - 6) * 512 + h * 256, 128)
                        o_qkv[:, 0, pl.ds(column, 256)] = source[late, h, 0:12]

                @when(j8 == N_DOWN + 8)
                def _():
                    o_qkv[:, 0, pl.ds(pl.multiple_of(who * 1152 + 1024, 128), 128)] = source[late, 0, 0:12, 0:128]
                    o_out[:, 0, pl.ds(pl.multiple_of(who * 384, 128), 128)] = source[late, 0, 0:12, 128:256]
                    o_out[:, 0, pl.ds(pl.multiple_of(who * 384 + 128, 128), 256)] = source[late, 1, 0:12]

        return carry


    def band(k):
        return pl.ds(k * BAND, BAND)

    def normalise(value):
        average = jnp.mean(value, -1, keepdims=True)
        centred = value - average
        inverse = lax.rsqrt(jnp.mean(centred * centred, -1, keepdims=True) + epsilon)
        return centred * inverse, inverse

    lanes = lax.broadcasted_iota(jnp.int32, (256, 128), 1)

    def own_lanes(e):
        return (lanes < 64) if e == 0 else (lanes >= 64)

    def forward(m, carry):
        @pl.when(first)
        def _():
            token_copy(m).wait()

        @pl.when(second)
        def _():
            hand_on(m).wait_recv()

        x = x_s[m]
        query = dot_nn(x, wq[:, 0:768]) + biases[0]
        qkv_s[m, :, 0:768] = bf16(f32(bf16(query)) * 0.125)
        qkv_s[m, :, 768:1536] = bf16(dot_nn(x, wq[:, 768:1536]))
        qkv_s[m, :, 1536:2304] = bf16(dot_nn(x, wq[:, 1536:2304]) + biases[1])

        for hp in range(6):
            at = pl.ds(hp * 128, 128)
            q2 = qkv_s[m, :, at]
            k2 = qkv_s[m, :, pl.ds(hp * 128 + 768, 128)]
            v2 = qkv_s[m, :, pl.ds(hp * 128 + 1536, 128)]
            none = jnp.zeros_like(q2)
            qs = jnp.concatenate([jnp.where(own_lanes(e), q2, none) for e in range(2)], 0)
            vs = jnp.concatenate([jnp.where(own_lanes(e), v2, none) for e in range(2)], 0)
            scores_two = dot_nt(k2, qs)
            probs_two = []
            for e in range(2):
                head = 2 * hp + e
                scores = scores_two[:, 256 * e:256 * e + 256] - 2.0 ** (-8.0 * (head + 1) / HEADS) * dist_s[m]
                expo = jnp.exp(scores - jnp.max(scores, 0, keepdims=True))
                probs = bf16(expo * (1.0 / jnp.sum(expo, 0, keepdims=True)))
                p_s[m, head] = probs
                probs_two.append(probs)
            mixed_s[m, :, at] = bf16(dot_tn(jnp.concatenate(probs_two, 0), vs))

        @pl.when(m == 0)
        def _():
            w_copies[1].wait()

        acc_s[...] = dot_nn(mixed_s[m], wo[...])
        for k in range(256 // BAND):
            r = band(k)
            value = f32(x_s[m, r]) + (acc_s[r] + biases[2])
            unit, inverse = normalise(value)
            normed = unit * gains[0:1] + biases[3]
            n1_s[m, r] = bf16(unit)
            r_s[m, r, 0:1] = inverse
            f_s[r] = normed
            nl_s[m, r] = bf16(normed)

        pair(0, m).start()

        @pl.when(m == 0)
        def _():
            w_copies[2].wait()
            w_copies[3].wait()

        @pl.when(second & (m == 1))
        def _():
            out_copy(0).wait()

        for jb in range(FF // BLOCK):
            c0 = jb * BLOCK
            low = nl_s[m]
            gate_s[...] = dot_nn(low, wg[:, c0:c0 + BLOCK])
            out_s[...] = dot_nn(low, wg[:, c0 + FF:c0 + FF + BLOCK])
            for k in range(256 // BAND):
                r = band(k)
                gate, up = gate_s[r], out_s[r]
                act, slope = gelu_terms(gate)
                gu_s[m, r, c0:c0 + BLOCK] = bf16(up * slope)
                gu_s[m, r, c0 + FF:c0 + FF + BLOCK] = bf16(act)
                gate_s[r] = act * up
            hid = bf16(gate_s[...])
            ht_s[m, 8 * jb:8 * jb + 8] = hid.T.reshape(8, 2, 48, 256)
            term = dot_nn(hid, wd[c0:c0 + BLOCK])
            if jb == 0:
                acc_s[...] = term
            else:
                acc_s[...] += term

        for k in range(256 // BAND):
            r = band(k)
            value = f_s[r] + (acc_s[r] + biases[4])
            unit, inverse = normalise(value)
            n2_s[m, r] = bf16(unit)
            r_s[m, r, 1:2] = inverse
            result = unit * gains[1:2] + biases[5]
            out_s[r] = result
            send_s[m, r] = bf16(result)

        @pl.when(first)
        def _():
            hand_on(m).start()

        @pl.when(second)
        def _():
            out_copy(m).start()

        pair(1, m).start()
        return carry

    lax.fori_loop(0, 2, forward, 0)

    def norm_back(grad, unit, inverse, gain):
        scaled = grad * gain
        mean_one = jnp.mean(scaled, -1, keepdims=True)
        mean_two = jnp.mean(scaled * unit, -1, keepdims=True)
        return inverse * (scaled - mean_one - unit * mean_two)

    def backward(m, carry):
        early = first & (m == 1)

        @pl.when(first)
        def _():
            hand_on(m).wait_send()
            hand_back(m).wait_recv()

        @pl.when(second)
        def _():
            cot_copy(m).wait()

        for k in range(256 // BAND):
            r = band(k)
            row = lax.broadcasted_iota(jnp.int32, (BAND, 1), 0) + k * BAND
            limit = jnp.where(m == 0, jnp.where(row < 128, length_a, length_b + 128), length_long)
            live = jnp.where((row < limit) | first, 1.0, 0.0)
            grad = f32(g_s[m, r]) * live
            unit = f32(n2_s[m, r])
            vec_s[1] += fold_rows(grad * unit)
            vec_s[7] += fold_rows(grad)
            grad_in = norm_back(grad, unit, r_s[m, r, 1:2], gains[1:2])
            f_s[r] = grad_in
            low = bf16(grad_in)
            gf_s[m, r] = low
            vec_s[6] += fold_rows(f32(low))

        pair(2, m).start()

        for jb in range(FF // BLOCK):
            c0 = jb * BLOCK
            gate_s[...] = dot_nt(gf_s[m], wd[c0:c0 + BLOCK])
            for k in range(256 // BAND):
                r = band(k)
                hid = gate_s[r]
                for c in (c0, c0 + FF):
                    gu_s[m, r, c:c + BLOCK] = bf16(hid * f32(gu_s[m, r, c:c + BLOCK]))
            term = dot_nt(gu_s[m, :, c0:c0 + BLOCK], wg[:, c0:c0 + BLOCK])
            term = term + dot_nt(gu_s[m, :, c0 + FF:c0 + FF + BLOCK], wg[:, c0 + FF:c0 + FF + BLOCK])
            if jb == 0:
                acc_s[...] = term
            else:
                acc_s[...] += term
            if jb in (0, 2):
                @pl.when(early)
                def _():
                    step(jb // 2, 0)

        pair(3, m).start()

        for k in range(256 // BAND):
            r = band(k)
            grad = acc_s[r] + f_s[r]
            unit = f32(n1_s[m, r])
            vec_s[0] += fold_rows(grad * unit)
            vec_s[5] += fold_rows(grad)
            grad_in = norm_back(grad, unit, r_s[m, r, 0:1], gains[0:1])
            f_s[r] = grad_in
            low = bf16(grad_in)
            ga_s[m, r] = low
            vec_s[4] += fold_rows(f32(low))

        def mixed_back(g):
            c = g * 256
            send_s[m, :, c:c + 256] = bf16(dot_nt(ga_s[m], wo[c:c + 256]))

        def attend_back(hp):
            at = pl.ds(hp * 128, 128)
            q2 = qkv_s[m, :, at]
            k2 = qkv_s[m, :, pl.ds(hp * 128 + 768, 128)]
            v2 = qkv_s[m, :, pl.ds(hp * 128 + 1536, 128)]
            do2 = send_s[m, :, at]
            none = jnp.zeros_like(q2)
            qs, ks, ds = (
                jnp.concatenate([jnp.where(own_lanes(e), wide, none) for e in range(2)], 0) for wide in (q2, k2, do2)
            )
            grad_probs_two = dot_nt(v2, ds)
            probs_two = [p_s[m, 2 * hp + e] for e in range(2)]
            scores_two = []
            for e in range(2):
                weighted = f32(probs_two[e]) * grad_probs_two[:, 256 * e:256 * e + 256]
                total = jnp.sum(weighted, 0, keepdims=True)
                scores_two.append(bf16(weighted - f32(probs_two[e]) * total))
            grad_v = bf16(dot_nn(jnp.concatenate(probs_two, 1), ds))
            grad_k = bf16(dot_nn(jnp.concatenate(scores_two, 1), qs))
            grad_q = bf16(dot_tn(jnp.concatenate(scores_two, 0), ks) * 0.125)
            vec_s[2, :, at] += fold_rows(f32(grad_q))
            vec_s[3, :, at] += fold_rows(f32(grad_v))
            qkv_s[m, :, at] = grad_q
            qkv_s[m, :, pl.ds(hp * 128 + 768, 128)] = grad_k
            qkv_s[m, :, pl.ds(hp * 128 + 1536, 128)] = grad_v

        mixed_back(0)
        for g in range(3):
            if g < 2:
                mixed_back(g + 1)
            attend_back(2 * g)
            attend_back(2 * g + 1)
            c = g * 256
            term = dot_nt(qkv_s[m, :, c:c + 256], wq[:, c:c + 256])
            for c in (g * 256 + 768, g * 256 + 1536):
                term = term + dot_nt(qkv_s[m, :, c:c + 256], wq[:, c:c + 256])
            if g == 0:
                acc_s[...] = term
            else:
                acc_s[...] += term

        @pl.when(early)
        def _():
            step(2, 0)

        @pl.when(first & (m == 1))
        def _():
            out_copy(0).wait()

        grad_a = acc_s[...] + f_s[...]

        @pl.when(second)
        def _():
            send_s[m] = bf16(grad_a)
            hand_back(m).start()

        @pl.when(first)
        def _():
            out_s[...] = grad_a
            out_copy(m).start()

        return carry

    lax.fori_loop(0, 2, backward, 0)
    for k in range(8):
        v_acc[0, k:k + 1] = jnp.sum(vec_s[k], 0, keepdims=True)
    v_start(0)

    def tail_step(i, carry):
        step(i, carry)
        for stage in range(4):
            @pl.when(i == 2 * stage + 5)
            def _():
                v_finish(stage)
                if stage < 3:
                    v_start(stage + 1)

        return carry

    lax.fori_loop(3 * (1 - sec), N_CHUNKS + 4, tail_step, 0)
    o_vec[...] = v_acc[4]

    @pl.when(second)
    def _():
        hand_back(0).wait_send()
        hand_back(1).wait_send()

    out_copy(1).wait()


def run_layers(short_lens, long_lens, tokens, cotangent, w_qkv, w_out, w_gate_up, w_down, gains, biases):
    low, wide = jnp.bfloat16, jnp.float32
    hbm = pl.BlockSpec(memory_space=pl.ANY)
    vmem = pl.BlockSpec(memory_space=pltpu.VMEM)
    smem = pl.BlockSpec(memory_space=pltpu.SMEM)
    dma = pltpu.SemaphoreType.DMA
    of = pltpu.VMEM
    s = SLOTS
    return pl.pallas_call(
        layers_kernel,
        out_shape=[
            jax.ShapeDtypeStruct((2, 256, 768), wide),
            jax.ShapeDtypeStruct((12, 1, 2304), wide),
            jax.ShapeDtypeStruct((12, 1, 768), wide),
            jax.ShapeDtypeStruct((12, 1, 6144), wide),
            jax.ShapeDtypeStruct((48, 768), wide),
            jax.ShapeDtypeStruct((8, 768), wide),
        ],
        in_specs=[smem] * 2 + [hbm] * 6 + [vmem] * 2,
        out_specs=[hbm] + [vmem] * 5,
        scratch_shapes=[
            of((768, 2304), low), of((768, 768), low), of((768, 6144), low), of((3072, 768), low),
            of((2, 256, 768), low), of((2, 256, 768), low), of((2, 256, 2304), low), of((2, 12, 256, 256), low),
            of((2, 256, 768), low), of((2, 256, 768), low),
            of((2, 256, 768), low), of((2, 256, 768), low),
            of((2, 256, 2), wide), of((2, 256, 6144), low), of((2, 32, 2, 48, 256), low),
            of((2, 256, 768), low), of((2, 256, 768), low), of((2, 256, 768), low), of((256, 768), wide),
            of((256, 768), wide), of((256, 768), wide), of((256, BLOCK), wide),
            of((2, 256, 256), wide), of((8, 8, 768), wide),
            of((2, 256, 768), low), of((2, 32, 48, 256), low), of((2, 256, 768), low), of((2, 256, 3072), low),
            of((OWN_SLOTS, 2, 4, 4, 48, 256), low),
            of((s, 2, 4, 48, 256), low), of((s, 2, 2, 4, 48, 256), low), of((2, 2, 4, 48, 256), low),
            of((OWN_SLOTS, 2, 4, 48, 256), low),
            of((s, 2, 48, 256), low), of((s, 2, 2, 48, 256), low), of((2, 2, 48, 256), low),
            of((2, 48, 256), wide), of((2, 48, 256), wide), of((s, 48, 256), wide),
            of((48, 256), wide), of((2, 2, 16, 256), wide), of((2, 2, 16, 256), wide), of((s, 2, 16, 256), wide),
            of((3, 8, 48, 256), low), of((3, 2, 16, 256), wide), of((3, 2, 16, 256), wide), of((3, 2, 16, 256), wide),
            of((5, 8, 768), wide), of((8, 8, 768), wide),
            dma((4,)), dma((2,)), dma((2,)), dma((2,)), dma((2,)), dma((2,)), dma((2,)), dma((2,)),
            dma((8, 2)), dma((8, 2)),
            dma((s, 4)), dma((s, 2)), dma((s, 2, 2)), dma((2, 2)),
            dma((s, 4)), dma((s, 2)), dma((s, 2, 2)), dma((2, 2)),
            dma((2,)), dma((s,)), dma((2,)), dma((s,)), dma((8,)), dma((8,)),
            dma((3, 8)), dma((3, 8)), dma((3,)), dma((3,)),
        ],
        compiler_params=pltpu.CompilerParams(
            collective_id=0, has_side_effects=True, vmem_limit_bytes=VMEM_LIMIT
        ),
        cost_estimate=pl.CostEstimate(flops=3 * 10 ** 10, bytes_accessed=4 * 10 ** 7, transcendentals=10 ** 7),
        name="run_layers",
    )(short_lens, long_lens, tokens, cotangent, w_qkv, w_out, w_gate_up, w_down, gains, biases)


def place_kernel(start, boundary, qkv, out, gate_up, down, vec, o_b, o_q, o_o, o_g, o_d, o_gains, o_biases, sems):
    copies = [
        pltpu.make_async_copy(source, target, sems.at[k])
        for k, (source, target) in enumerate(
            ((boundary, o_b.at[0]), (gate_up, o_g), (qkv, o_q), (out, o_o), (down, o_d.at[0]))
        )
    ]
    for copy in copies:
        copy.start()
    mine = pltpu.roll(vec[...], lax.rem(D - start[0], D), axis=1)
    o_gains[0] = mine[:2, :12]
    o_biases[:, 0] = mine[2:, :12]
    for copy in copies:
        copy.wait()


def place(start, boundary, qkv, out, gate_up, down, vec):
    wide = jnp.float32
    vmem = pl.BlockSpec(memory_space=pltpu.VMEM)
    return pl.pallas_call(
        place_kernel,
        out_shape=[
            jax.ShapeDtypeStruct((1, 2, 256, 768), wide),
            jax.ShapeDtypeStruct((12, 1, 2304), wide),
            jax.ShapeDtypeStruct((12, 1, 768), wide),
            jax.ShapeDtypeStruct((12, 1, 6144), wide),
            jax.ShapeDtypeStruct((1, 48, 768), wide),
            jax.ShapeDtypeStruct((1, 2, 12), wide),
            jax.ShapeDtypeStruct((6, 1, 12), wide),
        ],
        in_specs=[pl.BlockSpec(memory_space=pltpu.SMEM)] + [pl.BlockSpec(memory_space=pltpu.HBM)] * 5 + [vmem],
        out_specs=[vmem] * 7,
        scratch_shapes=[pltpu.SemaphoreType.DMA((5,))],
        compiler_params=pltpu.CompilerParams(vmem_limit_bytes=VMEM_LIMIT),
        name="place",
    )(start, boundary, qkv, out, gate_up, down, vec)


def on_device(
    tokens, cotangent, short_lens, long_lens, w_qkv, w_out, w_gate_up, w_down, gains, biases
):
    boundary, q, o, g, d, vec = run_layers(
        short_lens, long_lens, tokens, cotangent, w_qkv[0], w_out[0], w_gate_up[0], w_down[0], gains[0],
        jnp.transpose(biases, (1, 0, 2)),
    )
    start = jnp.full((1,), lax.axis_index("dp") * 12, jnp.int32)
    b, q, o, g, d, gains_out, biases_out = place(start, boundary, q, o, g, d, vec)
    q, o, g, biases_out = (jnp.transpose(rows, (1, 0, 2)) for rows in (q, o, g, biases_out))
    return (b, q, o, g, d, gains_out, biases_out)


def solution(mesh):
    placed = (
        P(None, "dp", None),
        P(None, "dp", None),
        P("dp"),
        P("dp"),
        P("section", None, None),
        P("section", None, None),
        P("section", None, None),
        P("section", None, None),
        P("section", None, None),
        P("section", None, None),
    )
    return jax.shard_map(
        on_device,
        mesh=mesh,
        in_specs=placed,
        out_specs=(
            P("section", None, "dp", None),
            P("section", "dp", None),
            P("section", "dp", None),
            P("section", "dp", None),
            P("section", "dp", None),
            P("section", None, "dp"),
            P("section", None, "dp"),
        ),
        check_vma=False,
    )
```
